32 devices in a mesh: src: 4 (over y, x), tgt: 8 (over z, core).
Axes of the slice: x: 2, y: 2, z: 4, core: 2. Of those that a mesh axis runs over, the one named last changes fastest.
Arguments:
- box_weights: bfloat16 [128, 1024, 128], P('src', 'tgt'), may hold values from -6 to 6
- slowness: float32 [1024], P('tgt'), may hold values from 0 to 3
- dip_field: float32 [128], P('src'), may hold values from 0 to 3
Outputs:
- interpolants: bfloat16 [128, 1024, 128], P('src', 'tgt')
The draws below stay inside these ranges and needn't reach their ends.
All inputs are finite; a program needn't handle non-finite values.
Results may differ from the reference program's by a relative error of at most 0.038.
Values may be sent and summed in bfloat16 or wider, within the bound.
No kernel may reach another device: no remote copies, remote signals or barrier semaphores. Data moves between devices by JAX's collectives and lax.ppermute only.
A program may use at most 64 MiB of HBM per device.

```python
import math
import jax
import jax.numpy as jnp

W = 128
NS = 128
NT = 1024


def steps_of(own_key, dims, split, low, largest):
    def one(axis_at, shards_of):
        heights = jax.random.uniform(jax.random.fold_in(jax.random.fold_in(own_key, 6), axis_at), (shards_of,), jnp.float32, low / len(split), largest / len(split))
        return jnp.repeat(jnp.exp(heights), dims[axis_at] // shards_of).reshape((-1,) + (1,) * (len(dims) - axis_at - 1))

    gain = one(*split[0])
    for cut in split[1:]:
        gain = gain * one(*cut)
    return gain


def normal_values(own_key, extent, spread, bound, split=(), held_as=jnp.bfloat16):
    values = jax.random.normal(own_key, extent, jnp.float32) * spread
    if len(split) > 0:
        values = steps_of(own_key, extent, split, -0.22, 0.18) * values
    return jnp.clip(values, min=-bound, max=bound).astype(held_as)


def setup_inputs(seed: int = 0) -> dict:
    splits = jax.random.split(jax.random.key(seed), 4)
    box_weights = normal_values(splits[0], (NS, NT, W), 1.0, 6.0, ((0, 4), (1, 8)))
    slowness = jnp.clip(3.0 * jax.random.uniform(splits[1], (NT,), jnp.float32) ** steps_of(splits[1], (NT,), ((0, 8),), -0.2, 0.2), 0.0, 3.0)
    dip_field = jnp.clip(3.0 * jax.random.uniform(splits[2], (NS,), jnp.float32) ** steps_of(splits[2], (NS,), ((0, 4),), -0.2, 0.2), 0.0, 3.0)
    return dict(box_weights=box_weights, slowness=slowness, dip_field=dip_field)


def chebyshev_nodes():
    angles = (2.0 * jnp.arange(8, dtype=jnp.float32) + 1.0) * (math.pi / 16.0)
    points = jnp.cos(angles)
    first_coord = jnp.repeat(points, 8)
    second_coord = jnp.tile(points, 8)
    return (first_coord, second_coord)

def node_weights():
    first_coord, second_coord = chebyshev_nodes()
    return first_coord * first_coord + second_coord * second_coord

def level_blocks(number):
    first_coord, second_coord = chebyshev_nodes()
    frequency = 9.0 + 3.0 * (number % 5)
    shifts = jnp.array([-0.5, 0.5], dtype=jnp.float32)
    out_first = first_coord[None, :] + shifts[:, None]
    in_second = second_coord[None, :] + shifts[:, None]
    inner_prod = out_first[:, None, :, None] * first_coord[None, None, None, :] + second_coord[None, None, :, None] * in_second[None, :, None, :]
    out_norm = jnp.sqrt(out_first * out_first + second_coord[None, :] * second_coord[None, :])
    in_norm = jnp.sqrt(first_coord[None, :] * first_coord[None, :] + in_second * in_second)
    phases = frequency * (inner_prod + 0.5 * out_norm[:, None, :, None] * in_norm[None, :, None, :])
    factor = 1.0 / math.sqrt(128.0)
    real_part = (factor * jnp.cos(phases)).astype(jnp.bfloat16)
    imag_part = (factor * jnp.sin(phases)).astype(jnp.bfloat16)
    real_swap = jnp.swapaxes(real_part, 2, 3)
    imag_swap = jnp.swapaxes(imag_part, 2, 3)
    upper_rows = jnp.concatenate([real_swap, imag_swap], axis=3)
    lower_rows = jnp.concatenate([-imag_swap, real_swap], axis=3)
    blocks = jnp.concatenate([upper_rows, lower_rows], axis=2)
    return jnp.swapaxes(blocks, 0, 1)

def rotate_phase(values, angles):
    cosine = jnp.cos(angles)
    sine_val = jnp.sin(angles)
    real_part = values[..., :64]
    imag_part = values[..., 64:]
    return jnp.concatenate([real_part * cosine - imag_part * sine_val, real_part * sine_val + imag_part * cosine], axis=-1)

def source_level(current, bit_index, blocks, angles):
    source_count, target_count, feature = current.shape
    shaped = current.reshape(source_count >> bit_index + 1, 2, 1 << bit_index, target_count, feature).astype(jnp.float32)
    combined = jnp.einsum('htlrw,tswv->hslrv', shaped, blocks.astype(jnp.float32))
    combined = rotate_phase(combined, angles[None, None, None, :, :])
    return combined.astype(jnp.bfloat16).reshape(source_count, target_count, feature)

def target_level(current, bit_index, blocks, angles):
    source_count, target_count, feature = current.shape
    shaped = current.reshape(source_count, target_count >> bit_index + 1, 2, 1 << bit_index, feature).astype(jnp.float32)
    combined = jnp.einsum('ahtlw,tswv->ahslv', shaped, blocks.astype(jnp.float32))
    combined = rotate_phase(combined, angles[:, None, None, None, :])
    return combined.astype(jnp.bfloat16).reshape(source_count, target_count, feature)

def reference(box_weights, slowness, dip_field):
    node_sq = node_weights()
    source_angles = slowness[:, None] * node_sq[None, :]
    target_angles = dip_field[:, None] * node_sq[None, :]
    source_bits = int(NS).bit_length() - 1
    target_bits = int(NT).bit_length() - 1
    current = box_weights
    for number in range(source_bits):
        current = source_level(current, number, level_blocks(number), source_angles)
    for offset in range(target_bits):
        current = target_level(current, target_bits - 1 - offset, level_blocks(source_bits + offset), target_angles)
    return current
```

```python
import functools
import math

import jax
import jax.numpy as jnp
import ml_dtypes
import numpy as np
from jax import lax
from jax.experimental import pallas as pl
from jax.experimental.pallas import tpu as pltpu
from jax.sharding import PartitionSpec as P

HALF = 64
WIDE = 128


def nodes():
    points = np.cos((2.0 * np.arange(8) + 1.0) * (math.pi / 16.0))
    return np.repeat(points, 8), np.tile(points, 8)


def node_weights():
    first, second = nodes()
    return (first * first + second * second).astype(np.float32)


def level_matrix(number):
    first, second = nodes()
    frequency = 9.0 + 3.0 * (number % 5)
    shifts = np.array([-0.5, 0.5])
    out_first = first[None, :] + shifts[:, None]
    in_second = second[None, :] + shifts[:, None]
    inner = (
        out_first[:, None, :, None] * first[None, None, None, :]
        + second[None, None, :, None] * in_second[None, :, None, :]
    )
    out_norm = np.sqrt(out_first**2 + second[None, :] ** 2)
    in_norm = np.sqrt(first[None, :] ** 2 + in_second**2)
    phases = frequency * (inner + 0.5 * out_norm[:, None, :, None] * in_norm[None, :, None, :])
    factor = 1.0 / math.sqrt(128.0)
    real = np.transpose(factor * np.cos(phases), (1, 3, 0, 2))
    imag = np.transpose(factor * np.sin(phases), (1, 3, 0, 2))
    upper = np.concatenate([real, imag], axis=3)
    lower = np.concatenate([-imag, real], axis=3)
    full = np.concatenate([upper, lower], axis=1)
    return full.reshape(2 * WIDE, 2 * WIDE).astype(ml_dtypes.bfloat16)


def tables(scales):
    weights = np.tile(node_weights(), 2)
    angles = scales[..., None] * weights
    signs = np.repeat(np.array([-1.0, 1.0], np.float32), HALF)
    return jnp.cos(angles), jnp.sin(angles) * signs


def butterfly(source, target, apart, matrix, phase_of, group):
    count = source.shape[0]
    lows = [i for i in range(count) if not i & apart]
    for start in range(0, len(lows), group):
        picked = lows[start : start + group]
        left = jnp.concatenate([source[i] for i in picked], axis=0)
        right = jnp.concatenate([source[i + apart] for i in picked], axis=0)
        both = jnp.dot(
            jnp.concatenate([left, right], axis=1), matrix, preferred_element_type=jnp.float32
        )
        rows = source.shape[1]
        for place, low in enumerate(picked):
            for child in range(2):
                value = both[
                    place * rows : (place + 1) * rows, child * WIDE : (child + 1) * WIDE
                ]
                index = low + child * apart
                cosine, sine = phase_of(index)
                value = value * cosine + pltpu.roll(value, HALF, 1) * sine
                target[index] = value.astype(target.dtype)


def local_kernel(aparts, group, x_ref, m_ref, c_ref, s_ref, o_ref):
    source = x_ref
    for step, apart in enumerate(aparts):
        butterfly(
            source, o_ref, apart, m_ref[step], lambda index: (c_ref[...], s_ref[...]), group
        )
        source = o_ref


def local_levels(x, matrices, cosine, sine, aparts):
    rows = x.shape[1]
    return pl.pallas_call(
        functools.partial(local_kernel, aparts, max(1, 512 // rows)),
        out_shape=jax.ShapeDtypeStruct(x.shape, x.dtype),
        in_specs=[pl.BlockSpec(memory_space=pltpu.VMEM)] * 4,
        out_specs=pl.BlockSpec(memory_space=pltpu.VMEM),
        compiler_params=pltpu.CompilerParams(vmem_limit_bytes=32 << 20),
    )(x, matrices, cosine, sine)


def swapped_kernel(levels, group, tgt_count, x_ref, m_ref, cs_ref, ss_ref, ct_ref, st_ref, o_ref):
    source = x_ref
    for step, (apart, by_source) in enumerate(levels):

        def phase_of(index):
            if by_source:
                at = index % tgt_count
                return cs_ref[at], ss_ref[at]
            at = index // tgt_count
            return ct_ref[at], st_ref[at]

        butterfly(source, o_ref, apart, m_ref[step], phase_of, group)
        source = o_ref


def swapped_levels(x, matrices, src_tables, tgt_tables, levels, tgt_count):
    rows = x.shape[1]
    return pl.pallas_call(
        functools.partial(swapped_kernel, levels, max(1, 512 // rows), tgt_count),
        out_shape=jax.ShapeDtypeStruct(x.shape, x.dtype),
        in_specs=[pl.BlockSpec(memory_space=pltpu.VMEM)] * 6,
        out_specs=pl.BlockSpec(memory_space=pltpu.VMEM),
        compiler_params=pltpu.CompilerParams(vmem_limit_bytes=32 << 20),
    )(x, matrices, *src_tables, *tgt_tables)


def local(box_weights, slowness, dip_field):
    rows, cols, _ = box_weights.shape
    src_count = lax.axis_size("src")
    tgt_count = lax.axis_size("tgt")
    devices = src_count * tgt_count
    row_bits, col_bits = rows.bit_length() - 1, cols.bit_length() - 1
    src_bits, tgt_bits = src_count.bit_length() - 1, tgt_count.bit_length() - 1
    first_target = row_bits + src_bits
    total = first_target + tgt_bits + col_bits
    matrices = [level_matrix(number) for number in range(total)]

    def matrices_of(low, high):
        return jnp.asarray(np.stack(matrices[low:high]))

    row_parts = min(rows, devices)
    col_parts = devices // row_parts
    row_each, col_each = rows // row_parts, cols // col_parts
    place = lax.axis_index("src") * tgt_count + lax.axis_index("tgt")
    row_at, col_at = place // col_parts, place % col_parts

    all_slowness = lax.all_gather(slowness, "tgt")
    all_dip = lax.all_gather(dip_field, "src")

    cosine, sine = tables(slowness)
    state = local_levels(
        box_weights,
        matrices_of(0, row_bits),
        cosine,
        sine,
        [1 << bit for bit in range(row_bits)],
    )

    state = state.reshape(row_parts, row_each, col_parts, col_each, WIDE)
    state = jnp.swapaxes(state, 1, 2).reshape(devices, row_each * col_each, WIDE)
    state = lax.all_to_all(state, ("src", "tgt"), 0, 0, tiled=True)

    part_slowness = lax.dynamic_slice_in_dim(all_slowness, col_at * col_each, col_each, 1)
    part_slowness = jnp.broadcast_to(
        part_slowness[:, None, :], (tgt_count, row_each, col_each)
    ).reshape(tgt_count, row_each * col_each)
    part_dip = lax.dynamic_slice_in_dim(all_dip, row_at * row_each, row_each, 1)
    part_dip = jnp.broadcast_to(
        part_dip[:, :, None], (src_count, row_each, col_each)
    ).reshape(src_count, row_each * col_each)
    levels = [(tgt_count << bit, True) for bit in range(src_bits)]
    levels += [(1 << bit, False) for bit in reversed(range(tgt_bits))]
    state = swapped_levels(
        state,
        matrices_of(row_bits, first_target + tgt_bits),
        tables(part_slowness),
        tables(part_dip),
        levels,
        tgt_count,
    )

    state = lax.all_to_all(state, ("src", "tgt"), 0, 0, tiled=True)
    state = state.reshape(row_parts, col_parts, row_each, col_each, WIDE)
    state = jnp.transpose(state, (1, 3, 0, 2, 4)).reshape(cols, rows, WIDE)

    cosine, sine = tables(dip_field)
    state = local_levels(
        state,
        matrices_of(first_target + tgt_bits, total),
        cosine,
        sine,
        [1 << bit for bit in reversed(range(col_bits))],
    )
    return jnp.swapaxes(state, 0, 1)


def solution(mesh):
    in_specs = (P("src", "tgt", None), P("tgt"), P("src"))
    out_specs = P("src", "tgt", None)
    return jax.shard_map(local, mesh=mesh, in_specs=in_specs, out_specs=out_specs, check_vma=False)
```

```python
import functools
import math

import jax
import jax.numpy as jnp
import ml_dtypes
import numpy as np
from jax import lax
from jax.experimental import pallas as pl
from jax.experimental.pallas import tpu as pltpu
from jax.sharding import PartitionSpec as P

HALF = 64
WIDE = 128


def nodes():
    points = np.cos((2.0 * np.arange(8) + 1.0) * (math.pi / 16.0))
    return np.repeat(points, 8), np.tile(points, 8)


def node_weights():
    first, second = nodes()
    return (first * first + second * second).astype(np.float32)


def level_matrix(number):
    first, second = nodes()
    frequency = 9.0 + 3.0 * (number % 5)
    shifts = np.array([-0.5, 0.5])
    out_first = first[None, :] + shifts[:, None]
    in_second = second[None, :] + shifts[:, None]
    inner = (
        out_first[:, None, :, None] * first[None, None, None, :]
        + second[None, None, :, None] * in_second[None, :, None, :]
    )
    out_norm = np.sqrt(out_first**2 + second[None, :] ** 2)
    in_norm = np.sqrt(first[None, :] ** 2 + in_second**2)
    phases = frequency * (inner + 0.5 * out_norm[:, None, :, None] * in_norm[None, :, None, :])
    factor = 1.0 / math.sqrt(128.0)
    real = np.transpose(factor * np.cos(phases), (1, 3, 0, 2))
    imag = np.transpose(factor * np.sin(phases), (1, 3, 0, 2))
    upper = np.concatenate([real, imag], axis=3)
    lower = np.concatenate([-imag, real], axis=3)
    full = np.concatenate([upper, lower], axis=1)
    return full.reshape(2 * WIDE, 2 * WIDE).astype(ml_dtypes.bfloat16)


def tables(scales):
    weights = np.tile(node_weights(), 2)
    angles = scales[..., None] * weights
    signs = np.repeat(np.array([-1.0, 1.0], np.float32), HALF)
    return jnp.cos(angles), jnp.sin(angles) * signs


def rotated(value, cosine, sine):
    return value * cosine + pltpu.roll(value, HALF, 1) * sine


def butterfly(load, store, count, apart, matrix, phase_of, group):
    lows = [i for i in range(count) if not i & apart]
    for start in range(0, len(lows), group):
        picked = lows[start : start + group]
        left = jnp.concatenate([load(i) for i in picked], axis=0)
        right = jnp.concatenate([load(i + apart) for i in picked], axis=0)
        rows = left.shape[0] // len(picked)
        both = jnp.dot(
            jnp.concatenate([left, right], axis=1), matrix, preferred_element_type=jnp.float32
        )
        for place, low in enumerate(picked):
            for child in range(2):
                index = low + child * apart
                value = both[
                    place * rows : (place + 1) * rows, child * WIDE : (child + 1) * WIDE
                ]
                store(index, rotated(value, *phase_of(index)))


def source_kernel(parts, x_ref, m_ref, c_ref, s_ref, *rest):
    out_refs, state_ref, wide_ref = rest[:parts], rest[parts], rest[parts + 1]
    rows, cols, _ = x_ref.shape
    levels = m_ref.shape[0]
    cosine, sine = c_ref[...], s_ref[...]
    for level in range(levels):
        source = x_ref if level == 0 else state_ref

        def store(index, value):
            if level < levels - 1:
                state_ref[index] = value.astype(jnp.bfloat16)
            else:
                wide_ref[pl.ds(index * cols, cols), :] = value

        butterfly(
            lambda index: source[index],
            store,
            rows,
            1 << level,
            m_ref[level],
            lambda index: (cosine, sine),
            max(1, 512 // cols),
        )
    each = rows // parts
    for part in range(parts):
        for col in range(cols):
            picked = wide_ref[pl.ds(part * each * cols + col, each, stride=cols), :]
            out_refs[part][col] = picked.astype(jnp.bfloat16)


def source_levels(x, matrices, cosine, sine, parts):
    rows, cols, _ = x.shape
    block = min(cols, 32)
    each = rows // parts
    table = pl.BlockSpec((block, WIDE), lambda i: (i, 0))
    return pl.pallas_call(
        functools.partial(source_kernel, parts),
        out_shape=[jax.ShapeDtypeStruct((cols, each, WIDE), x.dtype)] * parts,
        grid=(cols // block,),
        in_specs=[
            pl.BlockSpec((rows, block, WIDE), lambda i: (0, i, 0)),
            pl.BlockSpec(matrices.shape, lambda i: (0, 0, 0)),
            table,
            table,
        ],
        out_specs=[pl.BlockSpec((block, each, WIDE), lambda i: (i, 0, 0))] * parts,
        scratch_shapes=[
            pltpu.VMEM((rows, block, WIDE), x.dtype),
            pltpu.VMEM((rows * block, WIDE), jnp.float32),
        ],
        compiler_params=pltpu.CompilerParams(vmem_limit_bytes=32 << 20),
    )(x, matrices, cosine, sine)


def swapped_kernel(levels, tgt_count, x_ref, m_ref, cs_ref, ss_ref, ct_ref, st_ref, o_ref):
    count, rows, _ = x_ref.shape
    cols, each = cs_ref.shape[1], ct_ref.shape[1]

    def spread(ref, at):
        return jnp.concatenate(
            [jnp.broadcast_to(ref[at, col : col + 1, :], (each, WIDE)) for col in range(cols)],
            axis=0,
        )

    def tiled(ref, at):
        return jnp.concatenate([ref[at]] * cols, axis=0)

    for step, (apart, by_source) in enumerate(levels):
        source = x_ref if step == 0 else o_ref

        def phase_of(index):
            if by_source:
                at = index % tgt_count
                return spread(cs_ref, at), spread(ss_ref, at)
            at = index // tgt_count
            return tiled(ct_ref, at), tiled(st_ref, at)

        def store(index, value):
            o_ref[index] = value.astype(jnp.bfloat16)

        butterfly(
            lambda index: source[index],
            store,
            count,
            apart,
            m_ref[step],
            phase_of,
            max(1, 512 // rows),
        )


def swapped_levels(x, matrices, src_tables, tgt_tables, levels, tgt_count):
    return pl.pallas_call(
        functools.partial(swapped_kernel, levels, tgt_count),
        out_shape=jax.ShapeDtypeStruct(x.shape, x.dtype),
        in_specs=[pl.BlockSpec(memory_space=pltpu.VMEM)] * 6,
        out_specs=pl.BlockSpec(memory_space=pltpu.VMEM),
        compiler_params=pltpu.CompilerParams(vmem_limit_bytes=32 << 20),
    )(x, matrices, *src_tables, *tgt_tables)


def target_kernel(x_ref, m_ref, c_ref, s_ref, *rest):
    o_ref, state_ref, wide_ref = rest[-3:]
    cols, each, _ = x_ref.shape
    levels = m_ref.shape[0]
    cosine, sine = c_ref[...], s_ref[...]
    for level in range(levels):
        source = x_ref if level == 0 else state_ref

        def store(index, value):
            if level < levels - 1:
                state_ref[index] = value.astype(jnp.bfloat16)
            else:
                wide_ref[pl.ds(index * each, each), :] = value

        butterfly(
            lambda index: source[index],
            store,
            cols,
            1 << (levels - 1 - level),
            m_ref[level],
            lambda index: (cosine, sine),
            max(1, 512 // each),
        )
    for row in range(each):
        for col in range(0, cols, 16):
            picked = wide_ref[pl.ds(col * each + row, 16, stride=each), :]
            o_ref[row, pl.ds(col, 16), :] = picked.astype(jnp.bfloat16)


def target_levels(x, matrices, cosine, sine, part, parts, earlier):
    cols, each, _ = x.shape
    whole = pl.BlockSpec(memory_space=pltpu.VMEM)
    operands = [x, matrices, cosine, sine]
    in_specs = [
        pl.BlockSpec(x.shape, lambda i: (0, 0, 0)),
        pl.BlockSpec(matrices.shape, lambda i: (0, 0, 0)),
        pl.BlockSpec(cosine.shape, lambda i: (0, 0)),
        pl.BlockSpec(sine.shape, lambda i: (0, 0)),
    ]
    if earlier is not None:
        operands.append(earlier)
        in_specs.append(pl.BlockSpec(memory_space=pl.ANY))
    return pl.pallas_call(
        target_kernel,
        out_shape=jax.ShapeDtypeStruct((each * parts, cols, WIDE), x.dtype),
        grid=(1,),
        in_specs=in_specs,
        out_specs=pl.BlockSpec((each, cols, WIDE), lambda i: (part, 0, 0)),
        scratch_shapes=[
            pltpu.VMEM((cols, each, WIDE), x.dtype),
            pltpu.VMEM((cols * each, WIDE), jnp.float32),
        ],
        input_output_aliases={} if earlier is None else {4: 0},
        compiler_params=pltpu.CompilerParams(vmem_limit_bytes=32 << 20),
    )(*operands)


def local(box_weights, slowness, dip_field):
    rows, cols, _ = box_weights.shape
    src_count = lax.axis_size("src")
    tgt_count = lax.axis_size("tgt")
    devices = src_count * tgt_count
    row_bits, col_bits = rows.bit_length() - 1, cols.bit_length() - 1
    src_bits, tgt_bits = src_count.bit_length() - 1, tgt_count.bit_length() - 1
    first_target = row_bits + src_bits
    total = first_target + tgt_bits + col_bits
    matrices = [level_matrix(number) for number in range(total)]

    def matrices_of(low, high):
        return jnp.asarray(np.stack(matrices[low:high]))

    parts = max(1, rows // 16)
    each = rows // parts
    run = cols // devices
    place = lax.axis_index("src") * tgt_count + lax.axis_index("tgt")

    both = lax.all_gather(jnp.concatenate([slowness, dip_field]), ("src", "tgt"))
    both = both.reshape(src_count, tgt_count, cols + rows)
    all_slowness = lax.dynamic_slice_in_dim(both[0, :, :cols], place * run, run, 1)
    all_dip = both[:, 0, cols:]

    states = source_levels(
        box_weights, matrices_of(0, row_bits), *tables(slowness), parts
    )

    states = [
        lax.all_to_all(
            state.reshape(devices, run * each, WIDE), ("src", "tgt"), 0, 0, tiled=True
        )
        for state in states
    ]
    levels = [(tgt_count << bit, True) for bit in range(src_bits)]
    levels += [(1 << bit, False) for bit in reversed(range(tgt_bits))]
    src_tables = tables(all_slowness)
    tgt_tables = tables(all_dip)
    middle = matrices_of(row_bits, first_target + tgt_bits)
    backs = []
    for part, state in enumerate(states):
        picked = [table[:, part * each : (part + 1) * each] for table in tgt_tables]
        state = swapped_levels(state, middle, src_tables, picked, levels, tgt_count)
        backs.append(lax.all_to_all(state, ("src", "tgt"), 0, 0, tiled=True))

    last = matrices_of(first_target + tgt_bits, total)
    cosine, sine = tables(dip_field)
    result = None
    for part, state in enumerate(backs):
        own = slice(part * each, (part + 1) * each)
        result = target_levels(
            state.reshape(cols, each, WIDE), last, cosine[own], sine[own], part, parts, result
        )
    return result


def solution(mesh):
    in_specs = (P("src", "tgt", None), P("tgt"), P("src"))
    out_specs = P("src", "tgt", None)
    return jax.shard_map(local, mesh=mesh, in_specs=in_specs, out_specs=out_specs, check_vma=False)
```

```python
import functools
import math

import jax
import jax.numpy as jnp
import ml_dtypes
import numpy as np
from jax import lax
from jax.experimental import pallas as pl
from jax.experimental.pallas import tpu as pltpu
from jax.sharding import PartitionSpec as P

HALF = 64
WIDE = 128


def nodes():
    points = np.cos((2.0 * np.arange(8) + 1.0) * (math.pi / 16.0))
    return np.repeat(points, 8), np.tile(points, 8)


def node_weights():
    first, second = nodes()
    return (first * first + second * second).astype(np.float32)


def level_matrix(number):
    first, second = nodes()
    frequency = 9.0 + 3.0 * (number % 5)
    shifts = np.array([-0.5, 0.5])
    out_first = first[None, :] + shifts[:, None]
    in_second = second[None, :] + shifts[:, None]
    inner = (
        out_first[:, None, :, None] * first[None, None, None, :]
        + second[None, None, :, None] * in_second[None, :, None, :]
    )
    out_norm = np.sqrt(out_first**2 + second[None, :] ** 2)
    in_norm = np.sqrt(first[None, :] ** 2 + in_second**2)
    phases = frequency * (inner + 0.5 * out_norm[:, None, :, None] * in_norm[None, :, None, :])
    factor = 1.0 / math.sqrt(128.0)
    real = np.transpose(factor * np.cos(phases), (1, 3, 0, 2))
    imag = np.transpose(factor * np.sin(phases), (1, 3, 0, 2))
    upper = np.concatenate([real, imag], axis=3)
    lower = np.concatenate([-imag, real], axis=3)
    full = np.concatenate([upper, lower], axis=1)
    return full.reshape(2 * WIDE, 2 * WIDE).astype(ml_dtypes.bfloat16)


def tables(scales):
    weights = np.tile(node_weights(), 2)
    angles = scales[..., None] * weights
    signs = np.repeat(np.array([-1.0, 1.0], np.float32), HALF)
    return jnp.cos(angles), jnp.sin(angles) * signs


def flipped(matrix):
    return np.roll(matrix, (WIDE, WIDE), (0, 1))


def shuffles(run, each):
    groups = 16 // run
    found = np.zeros((groups, 16 * each, 16 * each), np.float32)
    for own in range(groups):
        for chip in range(groups):
            for col in range(run):
                for row in range(each):
                    at = (chip * run + col) * each + row
                    found[own, at, row * 16 + (chip ^ own) * run + col] = 1.0
    return found.astype(ml_dtypes.bfloat16)


def rotated(value, cosine, sine):
    return value * cosine + pltpu.roll(value, HALF, 1) * sine


def butterfly(load, store, count, apart, matrix, phase_of, group):
    lows = [i for i in range(count) if not i & apart]
    for start in range(0, len(lows), group):
        picked = lows[start : start + group]
        left = jnp.concatenate([load(i) for i in picked], axis=0)
        right = jnp.concatenate([load(i + apart) for i in picked], axis=0)
        rows = left.shape[0] // len(picked)
        both = jnp.dot(
            jnp.concatenate([left, right], axis=1), matrix, preferred_element_type=jnp.float32
        )
        for place, low in enumerate(picked):
            for child in range(2):
                index = low + child * apart
                value = both[
                    place * rows : (place + 1) * rows, child * WIDE : (child + 1) * WIDE
                ]
                store(index, rotated(value, *phase_of(index)).astype(jnp.bfloat16))


def source_kernel(parts, own_ref, x_ref, m_ref, c_ref, s_ref, p_ref, *rest):
    out_refs, state_ref = rest[:-1], rest[-1]
    rows, cols, _ = x_ref.shape
    chips = len(out_refs) // parts
    run, each = cols // chips, rows // parts
    for level in range(m_ref.shape[0]):
        source = x_ref if level == 0 else state_ref

        def store(index, value):
            state_ref[index] = value

        butterfly(
            lambda index: source[index],
            store,
            rows,
            1 << level,
            m_ref[level],
            lambda index: (c_ref[...], s_ref[...]),
            max(1, 512 // cols),
        )
    groups = 16 // run
    own = own_ref[0]
    shuffle = p_ref[lax.rem(own, groups)]
    own_high = lax.div(own, groups)
    for part in range(parts):
        for high in range(0, cols // 16, 2):
            sides = []
            for at in (high, high + 1):
                begin = pl.multiple_of(lax.bitwise_xor(own_high, at) * 16, 16)
                side = state_ref[part * each : (part + 1) * each, pl.ds(begin, 16), :]
                sides.append(side.reshape(each * 16, WIDE))
            moved = jnp.dot(
                shuffle, jnp.concatenate(sides, axis=1), preferred_element_type=jnp.float32
            ).astype(jnp.bfloat16)
            for side in range(2):
                for chip in range(groups):
                    block = moved[
                        chip * run * each : (chip + 1) * run * each,
                        side * WIDE : (side + 1) * WIDE,
                    ]
                    mask = (high + side) * groups + chip
                    out_refs[part * chips + mask][...] = block


def call(kernel, out_shape, operands, scratch, own=None, out_specs=None, aliases=None, whole=()):
    in_specs = []
    if own is not None:
        operands = (own, *operands)
        in_specs.append(pl.BlockSpec(memory_space=pltpu.SMEM))
    while len(in_specs) < len(operands):
        in_specs.append(pl.BlockSpec(memory_space=pltpu.VMEM))
    for at in whole:
        in_specs[at] = pl.BlockSpec(memory_space=pl.ANY)
    if out_specs is None:
        out_specs = jax.tree.map(lambda _: pl.BlockSpec(memory_space=pltpu.VMEM), out_shape)
    return pl.pallas_call(
        kernel,
        out_shape=out_shape,
        in_specs=in_specs,
        out_specs=out_specs,
        scratch_shapes=scratch,
        input_output_aliases=aliases or {},
        compiler_params=pltpu.CompilerParams(vmem_limit_bytes=32 << 20),
    )(*operands)


def middle_kernel(levels, part, each, own_ref, m_ref, cs_ref, ss_ref, ct_ref, st_ref, *rest):
    x_refs, o_ref = rest[:-1], rest[-1]
    count, rows, _ = o_ref.shape
    run = rows // each
    own = own_ref[0]
    rows_of = pl.ds(part * each, each)

    def spread(ref, at):
        return jnp.concatenate(
            [jnp.broadcast_to(ref[at, col : col + 1, :], (each, WIDE)) for col in range(run)],
            axis=0,
        )

    def tiled(ref, at):
        return jnp.concatenate([ref[at, rows_of, :]] * run, axis=0)

    tgt_chips = cs_ref.shape[0]
    for step, (bit, by_source) in enumerate(levels):

        def phase_of(index):
            if by_source:
                at = index % tgt_chips
                return spread(cs_ref, at), spread(ss_ref, at)
            at = index // tgt_chips
            return tiled(ct_ref, at), tiled(st_ref, at)

        def load(index):
            return x_refs[index][...] if step == 0 else o_ref[index]

        def store(index, value):
            o_ref[index] = value

        side = lax.rem(lax.div(own, 1 << bit), 2)
        butterfly(
            load, store, count, 1 << bit, m_ref[2 * step + side], phase_of, max(1, 512 // rows)
        )


def core_kernel(part, each, own_ref, m_ref, ct_ref, st_ref, x_ref, y_ref, *out_refs):
    count, rows, _ = x_ref.shape
    run = rows // each
    matrix = m_ref[own_ref[1]]
    tgt_chips = count // ct_ref.shape[0]
    group = max(1, 512 // rows)
    for start in range(0, count, group):
        picked = range(start, start + group)
        left = jnp.concatenate([x_ref[i] for i in picked], axis=0)
        right = jnp.concatenate([y_ref[i] for i in picked], axis=0)
        both = jnp.dot(
            jnp.concatenate([left, right], axis=1), matrix, preferred_element_type=jnp.float32
        )
        for place, index in enumerate(picked):
            at = index // tgt_chips
            cosine = jnp.concatenate([ct_ref[at, pl.ds(part * each, each), :]] * run, axis=0)
            sine = jnp.concatenate([st_ref[at, pl.ds(part * each, each), :]] * run, axis=0)
            value = both[place * rows : (place + 1) * rows]
            out_refs[index][...] = rotated(value, cosine, sine).astype(jnp.bfloat16)


def target_kernel(chips, part, own_ref, m_ref, c_ref, s_ref, p_ref, *rest):
    x_refs = rest[:chips]
    o_ref, state_ref = rest[-2:]
    cols, each, _ = state_ref.shape
    run = cols // chips
    chip_bits, run_bits = chips.bit_length() - 1, run.bit_length() - 1
    own = own_ref[0]
    rows_of = pl.ds(part * each, each)
    cosine, sine = c_ref[rows_of, :], s_ref[rows_of, :]

    def load_first(index):
        return x_refs[index // run][pl.ds(index % run * each, each), :]

    def store(index, value):
        state_ref[index] = value

    for step in range(chip_bits + run_bits):
        bit = chip_bits + run_bits - 1 - step
        if step < chip_bits:
            side = lax.rem(lax.div(own, 1 << (bit - run_bits)), 2)
            matrix = m_ref[2 * step + side]
        else:
            matrix = m_ref[chip_bits + step]
        butterfly(
            load_first if step == 0 else lambda index: state_ref[index],
            store,
            cols,
            1 << bit,
            matrix,
            lambda index: (cosine, sine),
            max(1, 512 // each),
        )
    groups = 16 // run
    shuffle = p_ref[lax.rem(own, groups)]
    own_high = lax.div(own, groups)
    for high in range(0, cols // 16, 2):
        sides = [state_ref[at * 16 : at * 16 + 16].reshape(16 * each, WIDE) for at in (high, high + 1)]
        moved = jnp.dot(
            shuffle, jnp.concatenate(sides, axis=1), preferred_element_type=jnp.float32
        ).astype(jnp.bfloat16)
        for side in range(2):
            begin = pl.multiple_of(lax.bitwise_xor(own_high, high + side) * 16, 16)
            block = moved[:, side * WIDE : (side + 1) * WIDE].reshape(each, 16, WIDE)
            o_ref[:, pl.ds(begin, 16), :] = block


def target_levels(own, matrices, cosine, sine, shuffle, blocks, part, parts, earlier):
    chips = len(blocks)
    run = blocks[0].shape[0] * parts // cosine.shape[0]
    each, cols = cosine.shape[0] // parts, run * chips
    operands = [matrices, cosine, sine, shuffle, *blocks]
    whole, aliases = (), None
    if earlier is not None:
        operands.append(earlier)
        whole, aliases = (len(operands),), {len(operands): 0}
    in_specs = [pl.BlockSpec(memory_space=pltpu.SMEM)]
    for operand in operands:
        zeros = (0,) * operand.ndim
        in_specs.append(pl.BlockSpec(operand.shape, lambda i, zeros=zeros: zeros))
    for at in whole:
        in_specs[at] = pl.BlockSpec(memory_space=pl.ANY)
    return pl.pallas_call(
        functools.partial(target_kernel, chips, part),
        out_shape=jax.ShapeDtypeStruct((each * parts, cols, WIDE), jnp.bfloat16),
        grid=(1,),
        in_specs=in_specs,
        out_specs=pl.BlockSpec((each, cols, WIDE), lambda i: (part, 0, 0)),
        scratch_shapes=[pltpu.VMEM((cols, each, WIDE), jnp.bfloat16)],
        input_output_aliases=aliases or {},
        compiler_params=pltpu.CompilerParams(vmem_limit_bytes=32 << 20),
    )(own, *operands)


def local(box_weights, slowness, dip_field):
    rows, cols, _ = box_weights.shape
    src_count = lax.axis_size("src")
    tgt_count = lax.axis_size("tgt")
    tgt_chips = tgt_count // 2
    chips = src_count * tgt_chips
    row_bits, col_bits = rows.bit_length() - 1, cols.bit_length() - 1
    src_bits, chip_bits = src_count.bit_length() - 1, tgt_chips.bit_length() - 1
    first_target = row_bits + src_bits
    core_level = first_target + chip_bits
    total = core_level + 1 + col_bits
    matrices = [level_matrix(number) for number in range(total)]
    parts = max(1, rows // 16)
    each = rows // parts
    run = cols // chips
    src_at, tgt_at = lax.axis_index("src"), lax.axis_index("tgt")
    chip = src_at * tgt_chips + tgt_at // 2
    own = jnp.stack([chip, tgt_at % 2]).astype(jnp.int32)

    def traded(block, mask):
        devices = src_count * tgt_count
        return lax.ppermute(block, ("src", "tgt"), [(i, i ^ mask) for i in range(devices)])

    def chip_mask(mask):
        return mask // tgt_chips * tgt_count + mask % tgt_chips * 2

    all_slowness = jnp.stack([slowness] + [traded(slowness, 2 * m) for m in range(1, tgt_chips)])
    all_dip = jnp.stack(
        [dip_field] + [traded(dip_field, tgt_count * m) for m in range(1, src_count)]
    )
    run_slowness = lax.dynamic_slice_in_dim(all_slowness, chip * run, run, 1)

    shuffle = shuffles(run, each)
    block = jax.ShapeDtypeStruct((run * each, WIDE), jnp.bfloat16)
    blocks = call(
        functools.partial(source_kernel, parts),
        [block] * (parts * chips),
        (
            box_weights,
            jnp.asarray(np.stack(matrices[:row_bits])),
            *tables(slowness),
            jnp.asarray(shuffle),
        ),
        [pltpu.VMEM(box_weights.shape, jnp.bfloat16)],
        own,
    )

    levels = [(chip_bits + bit, True) for bit in range(src_bits)]
    levels += [(bit, False) for bit in reversed(range(chip_bits))]
    middle = [
        kind(matrix)
        for matrix in matrices[row_bits:core_level]
        for kind in (lambda m: m, flipped)
    ]
    middle = jnp.asarray(np.stack(middle))
    core = matrices[core_level]
    core = jnp.asarray(np.stack([core[:, :WIDE], flipped(core)[:, :WIDE]]))
    last = [
        kind(matrix)
        for matrix in matrices[core_level + 1 : core_level + 1 + src_bits + chip_bits]
        for kind in (lambda m: m, flipped)
    ]
    last = jnp.asarray(np.stack(last + matrices[core_level + 1 + src_bits + chip_bits :]))
    back_shuffle = jnp.asarray(np.swapaxes(shuffle, 1, 2))
    src_tables, tgt_tables = tables(run_slowness), tables(all_dip)
    own_tables = tables(dip_field)

    result = None
    for part in range(parts):
        mine = blocks[part * chips : (part + 1) * chips]
        here = [mine[0]] + [traded(mine[m], chip_mask(m)) for m in range(1, chips)]
        state = call(
            functools.partial(middle_kernel, levels, part, each),
            jax.ShapeDtypeStruct((chips, run * each, WIDE), jnp.bfloat16),
            (middle, *src_tables, *tgt_tables, *here),
            [],
            own,
        )
        outs = call(
            functools.partial(core_kernel, part, each),
            [block] * chips,
            (core, *tgt_tables, state, traded(state, 1)),
            [],
            own,
        )
        home = [outs[0]] + [traded(outs[m], chip_mask(m)) for m in range(1, chips)]
        result = target_levels(
            own, last, *own_tables, back_shuffle, home, part, parts, result
        )
    return result


def solution(mesh):
    in_specs = (P("src", "tgt", None), P("tgt"), P("src"))
    out_specs = P("src", "tgt", None)
    return jax.shard_map(local, mesh=mesh, in_specs=in_specs, out_specs=out_specs, check_vma=False)
```

```python
import functools
import math

import jax
import jax.numpy as jnp
import ml_dtypes
import numpy as np
from jax import lax
from jax.experimental import pallas as pl
from jax.experimental.pallas import tpu as pltpu
from jax.sharding import PartitionSpec as P

HALF = 64
WIDE = 128


def nodes():
    points = np.cos((2.0 * np.arange(8) + 1.0) * (math.pi / 16.0))
    return np.repeat(points, 8), np.tile(points, 8)


def node_weights():
    first, second = nodes()
    return (first * first + second * second).astype(np.float32)


def level_matrix(number):
    first, second = nodes()
    frequency = 9.0 + 3.0 * (number % 5)
    shifts = np.array([-0.5, 0.5])
    out_first = first[None, :] + shifts[:, None]
    in_second = second[None, :] + shifts[:, None]
    inner = (
        out_first[:, None, :, None] * first[None, None, None, :]
        + second[None, None, :, None] * in_second[None, :, None, :]
    )
    out_norm = np.sqrt(out_first**2 + second[None, :] ** 2)
    in_norm = np.sqrt(first[None, :] ** 2 + in_second**2)
    phases = frequency * (inner + 0.5 * out_norm[:, None, :, None] * in_norm[None, :, None, :])
    factor = 1.0 / math.sqrt(128.0)
    real = np.transpose(factor * np.cos(phases), (1, 3, 0, 2))
    imag = np.transpose(factor * np.sin(phases), (1, 3, 0, 2))
    upper = np.concatenate([real, imag], axis=3)
    lower = np.concatenate([-imag, real], axis=3)
    full = np.concatenate([upper, lower], axis=1)
    return full.reshape(2 * WIDE, 2 * WIDE).astype(ml_dtypes.bfloat16)


def tables(scales):
    weights = np.tile(node_weights(), 2)
    angles = scales[..., None] * weights
    signs = np.repeat(np.array([-1.0, 1.0], np.float32), HALF)
    return jnp.cos(angles), jnp.sin(angles) * signs


def shuffle_matrix():
    rows = np.arange(256)
    found = np.zeros((256, 256), np.float32)
    found[rows, rows % 16 * 16 + rows // 16] = 1.0
    return found.astype(ml_dtypes.bfloat16)


def rotated(value, cosine, sine):
    return (value * cosine + pltpu.roll(value, HALF, 1) * sine).astype(jnp.bfloat16)


def butterfly(load, store, count, apart, matrix, phase_of, group):
    lows = [i for i in range(count) if not i & apart]
    for start in range(0, len(lows), group):
        picked = lows[start : start + group]
        left = jnp.concatenate([load(i) for i in picked], axis=0)
        right = jnp.concatenate([load(i + apart) for i in picked], axis=0)
        rows = left.shape[0] // len(picked)
        both = jnp.dot(
            jnp.concatenate([left, right], axis=1), matrix, preferred_element_type=jnp.float32
        )
        for place, low in enumerate(picked):
            for child in range(2):
                index = low + child * apart
                value = both[
                    place * rows : (place + 1) * rows, child * WIDE : (child + 1) * WIDE
                ]
                store(index, rotated(value, *phase_of(index)))


def swap_axes(load, store, outer, inner, shuffle):
    for low in range(0, outer, 2):
        for at in range(inner):
            sides = [load(low + side, at).reshape(256, WIDE) for side in range(2)]
            moved = jnp.dot(
                shuffle, jnp.concatenate(sides, axis=1), preferred_element_type=jnp.float32
            ).astype(jnp.bfloat16)
            for side in range(2):
                block = moved[:, side * WIDE : (side + 1) * WIDE]
                store(at, low + side, block.reshape(16, 16, WIDE))


def block_at(first, second):
    return (slice(first * 16, first * 16 + 16), slice(second * 16, second * 16 + 16))


def source_kernel(pieces, a_ref, x_hbm, m_hbm, p_ref, o_ref, x_ref, m_ref, x_sems, m_sems):
    rows, cols, _ = x_ref.shape
    levels = m_ref.shape[0]
    each = rows // pieces
    x_copies = [
        pltpu.make_async_copy(
            x_hbm.at[pl.ds(i * each, each)], x_ref.at[pl.ds(i * each, each)], x_sems.at[i]
        )
        for i in range(pieces)
    ]
    m_copies = [
        pltpu.make_async_copy(m_hbm.at[i], m_ref.at[i], m_sems.at[i]) for i in range(levels)
    ]
    m_copies[0].start()
    for copy in x_copies:
        copy.start()
    for copy in m_copies[1:]:
        copy.start()
    angles = a_ref[...]
    cosines = jnp.cos(angles)
    lanes = lax.broadcasted_iota(jnp.int32, angles.shape, 1)
    sines = jnp.where(lanes < HALF, -jnp.sin(angles), jnp.sin(angles))
    block = 32
    for level in range(levels):
        m_copies[level].wait()
        if level == 0:
            for copy in x_copies:
                copy.wait()
        for start in range(0, cols, block):
            cosine, sine = cosines[start : start + block], sines[start : start + block]

            def store(index, value):
                x_ref[index, start : start + block, :] = value

            butterfly(
                lambda index: x_ref[index, start : start + block, :],
                store,
                rows,
                1 << level,
                m_ref[level],
                lambda index: (cosine, sine),
                16,
            )

    def store_block(first, second, block):
        o_ref[block_at(first, second)] = block

    swap_axes(
        lambda first, second: x_ref[block_at(first, second)],
        store_block,
        rows // 16,
        cols // 16,
        p_ref[...],
    )


VMEM = pl.BlockSpec(memory_space=pltpu.VMEM)
PARAMS = pltpu.CompilerParams(vmem_limit_bytes=32 << 20)


def source_levels(x, matrices, angles, shuffle):
    rows, cols, _ = x.shape
    pieces = 4
    far = pl.BlockSpec(memory_space=pltpu.HBM)
    return pl.pallas_call(
        functools.partial(source_kernel, pieces),
        out_shape=jax.ShapeDtypeStruct((cols, rows, WIDE), x.dtype),
        in_specs=[VMEM, far, far, VMEM],
        out_specs=VMEM,
        scratch_shapes=[
            pltpu.VMEM(x.shape, x.dtype),
            pltpu.VMEM(matrices.shape, x.dtype),
            pltpu.SemaphoreType.DMA((pieces,)),
            pltpu.SemaphoreType.DMA((matrices.shape[0],)),
        ],
        compiler_params=PARAMS,
    )(angles, x, matrices, shuffle)


def middle_kernel(levels, rows, x_ref, m_ref, cs_ref, ss_ref, ct_ref, st_ref, o_ref):
    count, total, _ = x_ref.shape
    run = total // rows
    tgt_count = cs_ref.shape[0] // run
    for step, (apart, by_source) in enumerate(levels):
        source = x_ref if step == 0 else o_ref
        for col in range(run):
            own = slice(col * rows, (col + 1) * rows)

            def phase_of(index):
                if by_source:
                    at = index % tgt_count * run + col
                    return cs_ref[at : at + 1, :], ss_ref[at : at + 1, :]
                at = index // tgt_count
                return ct_ref[at], st_ref[at]

            def store(index, value):
                o_ref[index, own, :] = value

            butterfly(
                lambda index: source[index, own, :],
                store,
                count,
                apart,
                m_ref[step],
                phase_of,
                16,
            )


def middle_levels(x, matrices, src_tables, tgt_tables, levels):
    rows = tgt_tables[0].shape[1]
    return pl.pallas_call(
        functools.partial(middle_kernel, levels, rows),
        out_shape=jax.ShapeDtypeStruct(x.shape, x.dtype),
        in_specs=[VMEM] * 6,
        out_specs=VMEM,
        compiler_params=PARAMS,
    )(x, matrices, *src_tables, *tgt_tables)


def target_kernel(x_ref, m_ref, c_ref, s_ref, p_ref, o_ref, state_ref):
    cols, rows, _ = x_ref.shape
    levels = m_ref.shape[0]
    for level in range(levels):
        source = x_ref if level == 0 else state_ref
        for start in range(0, rows, 16):
            own = slice(start, start + 16)
            cosine, sine = c_ref[own, :], s_ref[own, :]

            def store(index, value):
                state_ref[index, own, :] = value

            butterfly(
                lambda index: source[index, own, :],
                store,
                cols,
                1 << (levels - 1 - level),
                m_ref[level],
                lambda index: (cosine, sine),
                32,
            )

    def store_block(first, second, block):
        o_ref[block_at(first, second)] = block

    swap_axes(
        lambda first, second: state_ref[block_at(first, second)],
        store_block,
        cols // 16,
        rows // 16,
        p_ref[...],
    )


def target_levels(x, matrices, cosine, sine, shuffle):
    cols, rows, _ = x.shape
    return pl.pallas_call(
        target_kernel,
        out_shape=jax.ShapeDtypeStruct((rows, cols, WIDE), x.dtype),
        in_specs=[VMEM] * 5,
        out_specs=VMEM,
        scratch_shapes=[pltpu.VMEM(x.shape, x.dtype)],
        compiler_params=PARAMS,
    )(x, matrices, cosine, sine, shuffle)


def gathered(values, axis):
    count = lax.axis_size(axis)
    place = lax.axis_index(axis)
    values = values[None]
    apart = 1
    while apart < count:
        other = lax.ppermute(values, axis, [(i, i ^ apart) for i in range(count)])
        mine_first = (place & apart) == 0
        values = jnp.concatenate(
            [jnp.where(mine_first, values, other), jnp.where(mine_first, other, values)]
        )
        apart *= 2
    return values


def local(box_weights, slowness, dip_field):
    rows, cols, _ = box_weights.shape
    src_count = lax.axis_size("src")
    tgt_count = lax.axis_size("tgt")
    devices = src_count * tgt_count
    row_bits, col_bits = rows.bit_length() - 1, cols.bit_length() - 1
    src_bits, tgt_bits = src_count.bit_length() - 1, tgt_count.bit_length() - 1
    first_target = row_bits + src_bits
    total = first_target + tgt_bits + col_bits
    matrices = [level_matrix(number) for number in range(total)]

    def matrices_of(low, high):
        return jnp.asarray(np.stack(matrices[low:high]))

    run = cols // devices
    place = lax.axis_index("src") * tgt_count + lax.axis_index("tgt")
    shuffle = jnp.asarray(shuffle_matrix())

    angles = slowness[:, None] * np.tile(node_weights(), 2)
    state = source_levels(box_weights, matrices_of(0, row_bits), angles, shuffle)

    state, slowness, dip_field = lax.optimization_barrier((state, slowness, dip_field))
    all_dip = gathered(dip_field, "src")
    all_slowness = gathered(slowness, "tgt")
    run_slowness = lax.dynamic_slice_in_dim(all_slowness, place * run, run, 1)

    state = state.reshape(devices, run * rows, WIDE)
    state = lax.all_to_all(state, ("src", "tgt"), 0, 0, tiled=True)
    levels = [(tgt_count << bit, True) for bit in range(src_bits)]
    levels += [(1 << bit, False) for bit in reversed(range(tgt_bits))]
    state = middle_levels(
        state,
        matrices_of(row_bits, first_target + tgt_bits),
        tables(run_slowness.reshape(-1)),
        tables(all_dip),
        levels,
    )
    state = lax.all_to_all(state, ("src", "tgt"), 0, 0, tiled=True)

    return target_levels(
        state.reshape(cols, rows, WIDE),
        matrices_of(first_target + tgt_bits, total),
        *tables(dip_field),
        shuffle,
    )


def solution(mesh):
    in_specs = (P("src", "tgt", None), P("tgt"), P("src"))
    out_specs = P("src", "tgt", None)
    return jax.shard_map(local, mesh=mesh, in_specs=in_specs, out_specs=out_specs, check_vma=False)
```

```python
import functools
import math

import jax
import jax.numpy as jnp
import ml_dtypes
import numpy as np
from jax import lax
from jax.experimental import pallas as pl
from jax.experimental.pallas import tpu as pltpu
from jax.sharding import PartitionSpec as P

HALF = 64
WIDE = 128


def nodes():
    points = np.cos((2.0 * np.arange(8) + 1.0) * (math.pi / 16.0))
    return np.repeat(points, 8), np.tile(points, 8)


def node_weights():
    first, second = nodes()
    return (first * first + second * second).astype(np.float32)


def level_matrix(number):
    first, second = nodes()
    frequency = 9.0 + 3.0 * (number % 5)
    shifts = np.array([-0.5, 0.5])
    out_first = first[None, :] + shifts[:, None]
    in_second = second[None, :] + shifts[:, None]
    inner = (
        out_first[:, None, :, None] * first[None, None, None, :]
        + second[None, None, :, None] * in_second[None, :, None, :]
    )
    out_norm = np.sqrt(out_first**2 + second[None, :] ** 2)
    in_norm = np.sqrt(first[None, :] ** 2 + in_second**2)
    phases = frequency * (inner + 0.5 * out_norm[:, None, :, None] * in_norm[None, :, None, :])
    factor = 1.0 / math.sqrt(128.0)
    real = np.transpose(factor * np.cos(phases), (1, 3, 0, 2))
    imag = np.transpose(factor * np.sin(phases), (1, 3, 0, 2))
    upper = np.concatenate([real, imag], axis=3)
    lower = np.concatenate([-imag, real], axis=3)
    full = np.concatenate([upper, lower], axis=1)
    return full.reshape(2 * WIDE, 2 * WIDE).astype(ml_dtypes.bfloat16)


def tables(scales):
    weights = np.tile(node_weights(), 2)
    angles = scales[..., None] * weights
    signs = np.repeat(np.array([-1.0, 1.0], np.float32), HALF)
    return jnp.cos(angles), jnp.sin(angles) * signs


def shuffle_matrix():
    rows = np.arange(256)
    found = np.zeros((256, 256), np.float32)
    found[rows, rows % 16 * 16 + rows // 16] = 1.0
    return found.astype(ml_dtypes.bfloat16)


def cos_sin(angles):
    turns = jnp.floor(angles * (2.0 / math.pi) + 0.5)
    rest = angles - turns * 1.5703125
    rest = rest - turns * 4.837512969970703125e-4
    rest = rest - turns * 7.54978995489188e-8
    square = rest * rest
    sine = 1.0 / 362880.0
    for factor in (-1.0 / 5040.0, 1.0 / 120.0, -1.0 / 6.0, 1.0):
        sine = sine * square + factor
    sine = sine * rest
    cosine = -1.0 / 3628800.0
    for factor in (1.0 / 40320.0, -1.0 / 720.0, 1.0 / 24.0, -0.5, 1.0):
        cosine = cosine * square + factor
    quarter = turns.astype(jnp.int32)
    odd = (quarter & 1) == 1
    first = jnp.where(odd, sine, cosine)
    second = jnp.where(odd, cosine, sine)
    first = jnp.where(((quarter + 1) & 2) == 2, -first, first)
    second = jnp.where((quarter & 2) == 2, -second, second)
    return first, second


def node_row():
    lanes = lax.broadcasted_iota(jnp.int32, (1, WIDE), 1) % HALF
    points = [math.cos((2 * a + 1) * math.pi / 16) ** 2 for a in range(4)]

    def square(at):
        near = jnp.minimum(at, 7 - at)
        value = jnp.full(near.shape, points[3], jnp.float32)
        for a in range(3):
            value = jnp.where(near == a, jnp.float32(points[a]), value)
        return value

    return square(lanes // 8) + square(lanes % 8)


def rotation(column):
    cosine, sine = cos_sin(column * node_row())
    lanes = lax.broadcasted_iota(jnp.int32, cosine.shape, 1)
    return cosine, jnp.where(lanes < HALF, -sine, sine)


def column_of(row, count):
    shape = (count, WIDE)
    here = lax.broadcasted_iota(jnp.int32, shape, 0) == lax.broadcasted_iota(jnp.int32, shape, 1)
    return jnp.sum(jnp.where(here, jnp.broadcast_to(row, shape), 0.0), axis=1, keepdims=True)


def rotated(value, cosine, sine):
    return (value * cosine + pltpu.roll(value, HALF, 1) * sine).astype(jnp.bfloat16)


def butterfly(load, store, count, apart, matrix, phase_of, group):
    lows = [i for i in range(count) if not i & apart]
    for start in range(0, len(lows), group):
        picked = lows[start : start + group]
        left = jnp.concatenate([load(i) for i in picked], axis=0)
        right = jnp.concatenate([load(i + apart) for i in picked], axis=0)
        rows = left.shape[0] // len(picked)
        both = jnp.dot(
            jnp.concatenate([left, right], axis=1), matrix, preferred_element_type=jnp.float32
        )
        for place, low in enumerate(picked):
            for child in range(2):
                index = low + child * apart
                value = both[
                    place * rows : (place + 1) * rows, child * WIDE : (child + 1) * WIDE
                ]
                store(index, rotated(value, *phase_of(index)))


def swap_axes(load, store, outer, inner, shuffle):
    for low in range(0, outer, 2):
        for at in range(inner):
            sides = [load(low + side, at).reshape(256, WIDE) for side in range(2)]
            moved = jnp.dot(
                shuffle, jnp.concatenate(sides, axis=1), preferred_element_type=jnp.float32
            ).astype(jnp.bfloat16)
            for side in range(2):
                block = moved[:, side * WIDE : (side + 1) * WIDE]
                store(at, low + side, block.reshape(16, 16, WIDE))


def block_at(first, second):
    return (slice(first * 16, first * 16 + 16), slice(second * 16, second * 16 + 16))


BLOCK = 32
NOTE = 8
VMEM = pl.BlockSpec(memory_space=pltpu.VMEM)
FAR = pl.BlockSpec(memory_space=pltpu.HBM)


def params(mib):
    return pltpu.CompilerParams(vmem_limit_bytes=mib << 20)


def source_kernel(run, side, a_ref, d_ref, x_hbm, m_hbm, p_hbm, *rest):
    outs, (x_ref, m_ref, p_ref, note_ref, x_sems, m_sems, p_sem) = rest[:-7], rest[-7:]
    rows, cols, _ = x_ref.shape
    levels = m_ref.shape[0]
    starts = range(0, cols, BLOCK)
    x_copies = []
    for piece, start in enumerate(starts):
        own = (slice(None), pl.ds(start, BLOCK))
        x_copies.append(
            pltpu.make_async_copy(x_hbm.at[own], x_ref.at[own], x_sems.at[piece])
        )
    m_copies = [
        pltpu.make_async_copy(m_hbm.at[i], m_ref.at[i], m_sems.at[i]) for i in range(levels)
    ]
    p_copy = pltpu.make_async_copy(p_hbm, p_ref, p_sem)
    m_copies[0].start()
    for copy in x_copies:
        copy.start()
    for copy in m_copies[1:]:
        copy.start()
    p_copy.start()

    slowness = a_ref[...]
    note_ref[...] = jnp.zeros_like(note_ref)
    note_ref[0:1, :rows] = d_ref[...]
    note_ref[3:4, :] = slowness
    for at in (0, 3):
        left = note_ref[at : at + 1, :]
        for part in range(3):
            piece = left.astype(jnp.bfloat16).astype(jnp.float32)
            note_ref[at + part : at + part + 1, :] = piece
            left = left - piece
    note = note_ref[...].astype(jnp.bfloat16)
    kept = (run - side) * rows
    for device in range(outs[0].shape[0]):
        outs[0][device, kept : kept + NOTE, :] = note

    cosines, sines = rotation(column_of(slowness, cols))
    for level in range(levels):
        m_copies[level].wait()
        for piece, start in enumerate(starts):
            if level == 0:
                x_copies[piece].wait()
            cosine, sine = cosines[start : start + BLOCK], sines[start : start + BLOCK]

            def store(index, value):
                x_ref[index, start : start + BLOCK, :] = value

            butterfly(
                lambda index: x_ref[index, start : start + BLOCK, :],
                store,
                rows,
                1 << level,
                m_ref[level],
                lambda index: (cosine, sine),
                16,
            )

    def store_block(first, second, block):
        for inner in range(16):
            device, col = divmod(first * 16 + inner, run)
            begin = second * 16
            if col < run - side:
                begin += col * rows
                outs[0][device, begin : begin + 16, :] = block[inner]
            else:
                outs[1][device * side + col - (run - side), begin : begin + 16, :] = block[inner]

    p_copy.wait()
    swap_axes(
        lambda first, second: x_ref[block_at(first, second)],
        store_block,
        rows // 16,
        cols // 16,
        p_ref[...],
    )


def source_levels(x, matrices, slowness, dip_field, shuffle, devices, run, side):
    rows, cols, _ = x.shape
    out_shape = [jax.ShapeDtypeStruct((devices, (run - side) * rows + NOTE, WIDE), x.dtype)]
    if side:
        out_shape.append(jax.ShapeDtypeStruct((devices * side, rows, WIDE), x.dtype))
    return pl.pallas_call(
        functools.partial(source_kernel, run, side),
        out_shape=out_shape,
        in_specs=[VMEM, VMEM, FAR, FAR, FAR],
        out_specs=[VMEM] * len(out_shape),
        scratch_shapes=[
            pltpu.VMEM(x.shape, x.dtype),
            pltpu.VMEM(matrices.shape, x.dtype),
            pltpu.VMEM(shuffle.shape, x.dtype),
            pltpu.VMEM((NOTE, WIDE), jnp.float32),
            pltpu.SemaphoreType.DMA((cols // BLOCK,)),
            pltpu.SemaphoreType.DMA((matrices.shape[0],)),
            pltpu.SemaphoreType.DMA,
        ],
        compiler_params=params(60),
    )(slowness[None, :], dip_field[None, :], x, matrices, shuffle)


def middle_kernel(levels, rows, run, tgt_count, x_ref, m_ref, o_ref):
    count, total, _ = x_ref.shape
    kept = (total - NOTE) // rows
    place = lax.axis_index("src") * tgt_count + lax.axis_index("tgt")

    def noted(device, at):
        note = x_ref[device, kept * rows :, :].astype(jnp.float32)
        return note[at : at + 1] + note[at + 1 : at + 2] + note[at + 2 : at + 3]

    slowness = jnp.concatenate([noted(at, 3) for at in range(tgt_count)], axis=0)
    lanes = lax.broadcasted_iota(jnp.int32, slowness.shape, 1)
    by_col = []
    for col in range(kept):
        picked = jnp.where(lanes == place * run + col, slowness, 0.0)
        by_col.append(rotation(jnp.sum(picked, axis=1, keepdims=True)))
    by_src = [
        rotation(column_of(noted(at * tgt_count, 0), rows)) for at in range(count // tgt_count)
    ]

    for step, (apart, by_source) in enumerate(levels):
        source = x_ref if step == 0 else o_ref
        for col in range(kept):
            own = slice(col * rows, (col + 1) * rows)

            def phase_of(index):
                if by_source:
                    at = index % tgt_count
                    return tuple(table[at : at + 1, :] for table in by_col[col])
                return by_src[index // tgt_count]

            def store(index, value):
                o_ref[index, own, :] = value

            butterfly(
                lambda index: source[index, own, :],
                store,
                count,
                apart,
                m_ref[step],
                phase_of,
                16,
            )


def middle_levels(x, matrices, levels, rows, run, tgt_count):
    count, total, _ = x.shape
    return pl.pallas_call(
        functools.partial(middle_kernel, levels, rows, run, tgt_count),
        out_shape=jax.ShapeDtypeStruct((count, total - NOTE, WIDE), x.dtype),
        in_specs=[VMEM] * 2,
        out_specs=VMEM,
        compiler_params=params(32),
    )(x, matrices)


def pair_kernel(axis, bit, by_row, x_ref, y_ref, m_ref, c_ref, s_ref, o_ref):
    count, rows, _ = x_ref.shape
    matrix = m_ref[lax.rem(lax.div(lax.axis_index(axis), 1 << bit), 2)]
    group = 16
    for start in range(0, count, group):
        picked = slice(start, start + group)
        left = x_ref[picked].reshape(-1, WIDE)
        right = y_ref[picked].reshape(-1, WIDE)
        both = jnp.dot(
            jnp.concatenate([left, right], axis=1), matrix, preferred_element_type=jnp.float32
        )
        for place in range(left.shape[0] // rows):
            index = start + place
            if by_row:
                cosine, sine = c_ref[...], s_ref[...]
            else:
                cosine, sine = c_ref[index : index + 1, :], s_ref[index : index + 1, :]
            o_ref[index] = rotated(both[place * rows : (place + 1) * rows], cosine, sine)


def pair_level(x, axis, bit, matrix, angles, by_row):
    count = lax.axis_size(axis)
    other = lax.ppermute(x, axis, [(i, i ^ 1 << bit) for i in range(count)])
    flipped = np.roll(matrix, (WIDE, WIDE), (0, 1))
    halves = jnp.asarray(np.stack([matrix[:, :WIDE], flipped[:, :WIDE]]))
    return pl.pallas_call(
        functools.partial(pair_kernel, axis, bit, by_row),
        out_shape=jax.ShapeDtypeStruct(x.shape, x.dtype),
        in_specs=[VMEM] * 5,
        out_specs=VMEM,
        compiler_params=params(32),
    )(x, other, halves, *angles)


def target_kernel(run, m_ref, c_ref, s_ref, p_ref, *rest):
    xs, (o_ref, state_ref) = rest[:-2], rest[-2:]
    cols, rows, _ = state_ref.shape
    kept = xs[0].shape[1] // rows
    side = run - kept
    levels = m_ref.shape[0]

    def first(index, start):
        device, col = divmod(index, run)
        if col < kept:
            start += col * rows
            return xs[0][device, start : start + 16, :]
        return xs[1][device * side + col - kept, start : start + 16, :]

    for level in range(levels):
        for start in range(0, rows, 16):
            own = slice(start, start + 16)
            cosine, sine = c_ref[own, :], s_ref[own, :]

            def load(index):
                return first(index, start) if level == 0 else state_ref[index, own, :]

            def store(index, value):
                state_ref[index, own, :] = value

            butterfly(
                load,
                store,
                cols,
                1 << (levels - 1 - level),
                m_ref[level],
                lambda index: (cosine, sine),
                32,
            )

    def store_block(first, second, block):
        o_ref[block_at(first, second)] = block

    swap_axes(
        lambda first, second: state_ref[block_at(first, second)],
        store_block,
        cols // 16,
        rows // 16,
        p_ref[...],
    )


def target_levels(states, matrices, angles, shuffle, cols, rows, run):
    return pl.pallas_call(
        functools.partial(target_kernel, run),
        out_shape=jax.ShapeDtypeStruct((rows, cols, WIDE), jnp.bfloat16),
        in_specs=[VMEM] * (4 + len(states)),
        out_specs=VMEM,
        scratch_shapes=[pltpu.VMEM((cols, rows, WIDE), jnp.bfloat16)],
        compiler_params=params(32),
    )(matrices, *angles, shuffle, *states)


def local(box_weights, slowness, dip_field):
    rows, cols, _ = box_weights.shape
    src_count = lax.axis_size("src")
    tgt_count = lax.axis_size("tgt")
    devices = src_count * tgt_count
    row_bits, col_bits = rows.bit_length() - 1, cols.bit_length() - 1
    src_bits, tgt_bits = src_count.bit_length() - 1, tgt_count.bit_length() - 1
    first_target = row_bits + src_bits
    total = first_target + tgt_bits + col_bits
    matrices = [level_matrix(number) for number in range(total)]

    def matrices_of(low, high):
        return jnp.asarray(np.stack(matrices[low:high]))

    run = cols // devices
    side = run // 4
    shuffle = jnp.asarray(shuffle_matrix())

    states = source_levels(
        box_weights, matrices_of(0, row_bits), slowness, dip_field, shuffle, devices, run, side
    )
    *states, slowness, dip_field = lax.optimization_barrier((*states, slowness, dip_field))
    by_row = tables(dip_field)

    if side:
        kept = slowness.reshape(devices, run)[:, run - side :].reshape(-1)
        by_col = tables(kept)
        stay = states[1]
        for bit in range(src_bits):
            stay = pair_level(stay, "src", bit, matrices[row_bits + bit], by_col, False)
        for at, bit in enumerate(reversed(range(tgt_bits))):
            stay = pair_level(stay, "tgt", bit, matrices[first_target + at], by_row, True)

    levels = [(tgt_count << bit, True) for bit in range(src_bits)]
    levels += [(1 << bit, False) for bit in reversed(range(tgt_bits))]
    state = lax.all_to_all(states[0], ("src", "tgt"), 0, 0, tiled=True)
    state = middle_levels(
        state, matrices_of(row_bits, first_target + tgt_bits), levels, rows, run, tgt_count
    )
    state = lax.all_to_all(state, ("src", "tgt"), 0, 0, tiled=True)

    return target_levels(
        [state, stay] if side else [state],
        matrices_of(first_target + tgt_bits, total),
        by_row,
        shuffle,
        cols,
        rows,
        run,
    )


def solution(mesh):
    in_specs = (P("src", "tgt", None), P("tgt"), P("src"))
    out_specs = P("src", "tgt", None)
    return jax.shard_map(local, mesh=mesh, in_specs=in_specs, out_specs=out_specs, check_vma=False)
```

```python
import functools
import math

import jax
import jax.numpy as jnp
import ml_dtypes
import numpy as np
from jax import lax
from jax.experimental import pallas as pl
from jax.experimental.pallas import tpu as pltpu
from jax.sharding import PartitionSpec as P

HALF = 64
WIDE = 128


def nodes():
    points = np.cos((2.0 * np.arange(8) + 1.0) * (math.pi / 16.0))
    return np.repeat(points, 8), np.tile(points, 8)


def node_weights():
    first, second = nodes()
    return (first * first + second * second).astype(np.float32)


def level_matrix(number):
    first, second = nodes()
    frequency = 9.0 + 3.0 * (number % 5)
    shifts = np.array([-0.5, 0.5])
    out_first = first[None, :] + shifts[:, None]
    in_second = second[None, :] + shifts[:, None]
    inner = (
        out_first[:, None, :, None] * first[None, None, None, :]
        + second[None, None, :, None] * in_second[None, :, None, :]
    )
    out_norm = np.sqrt(out_first**2 + second[None, :] ** 2)
    in_norm = np.sqrt(first[None, :] ** 2 + in_second**2)
    phases = frequency * (inner + 0.5 * out_norm[:, None, :, None] * in_norm[None, :, None, :])
    factor = 1.0 / math.sqrt(128.0)
    real = np.transpose(factor * np.cos(phases), (1, 3, 0, 2))
    imag = np.transpose(factor * np.sin(phases), (1, 3, 0, 2))
    upper = np.concatenate([real, imag], axis=3)
    lower = np.concatenate([-imag, real], axis=3)
    full = np.concatenate([upper, lower], axis=1)
    return full.reshape(2 * WIDE, 2 * WIDE).astype(ml_dtypes.bfloat16)


def tables(scales):
    weights = np.tile(node_weights(), 2)
    angles = scales[..., None] * weights
    signs = np.repeat(np.array([-1.0, 1.0], np.float32), HALF)
    return jnp.cos(angles), jnp.sin(angles) * signs


def shuffle_matrix():
    rows = np.arange(256)
    found = np.zeros((256, 256), np.float32)
    found[rows, rows % 16 * 16 + rows // 16] = 1.0
    return found.astype(ml_dtypes.bfloat16)


def cos_sin(angles):
    turns = jnp.floor(angles * (2.0 / math.pi) + 0.5)
    rest = angles - turns * 1.5703125
    rest = rest - turns * 4.837512969970703125e-4
    rest = rest - turns * 7.54978995489188e-8
    square = rest * rest
    sine = 1.0 / 362880.0
    for factor in (-1.0 / 5040.0, 1.0 / 120.0, -1.0 / 6.0, 1.0):
        sine = sine * square + factor
    sine = sine * rest
    cosine = -1.0 / 3628800.0
    for factor in (1.0 / 40320.0, -1.0 / 720.0, 1.0 / 24.0, -0.5, 1.0):
        cosine = cosine * square + factor
    quarter = turns.astype(jnp.int32)
    odd = (quarter & 1) == 1
    first = jnp.where(odd, sine, cosine)
    second = jnp.where(odd, cosine, sine)
    first = jnp.where(((quarter + 1) & 2) == 2, -first, first)
    second = jnp.where((quarter & 2) == 2, -second, second)
    return first, second


def node_row():
    lanes = lax.broadcasted_iota(jnp.int32, (1, WIDE), 1) % HALF
    points = [math.cos((2 * a + 1) * math.pi / 16) ** 2 for a in range(4)]

    def square(at):
        near = jnp.minimum(at, 7 - at)
        value = jnp.full(near.shape, points[3], jnp.float32)
        for a in range(3):
            value = jnp.where(near == a, jnp.float32(points[a]), value)
        return value

    return square(lanes // 8) + square(lanes % 8)


def rotation(column):
    cosine, sine = cos_sin(column * node_row())
    lanes = lax.broadcasted_iota(jnp.int32, cosine.shape, 1)
    return cosine, jnp.where(lanes < HALF, -sine, sine)


def column_of(row, count):
    shape = (count, WIDE)
    here = lax.broadcasted_iota(jnp.int32, shape, 0) == lax.broadcasted_iota(jnp.int32, shape, 1)
    return jnp.sum(jnp.where(here, jnp.broadcast_to(row, shape), 0.0), axis=1, keepdims=True)


def rotated(value, cosine, sine):
    return (value * cosine + pltpu.roll(value, HALF, 1) * sine).astype(jnp.bfloat16)


def butterfly(load, store, count, apart, matrix, phase_of, group):
    lows = [i for i in range(count) if not i & apart]
    for start in range(0, len(lows), group):
        picked = lows[start : start + group]
        left = jnp.concatenate([load(i) for i in picked], axis=0)
        right = jnp.concatenate([load(i + apart) for i in picked], axis=0)
        rows = left.shape[0] // len(picked)
        both = jnp.dot(
            jnp.concatenate([left, right], axis=1), matrix, preferred_element_type=jnp.float32
        )
        for place, low in enumerate(picked):
            for child in range(2):
                index = low + child * apart
                value = both[
                    place * rows : (place + 1) * rows, child * WIDE : (child + 1) * WIDE
                ]
                store(index, rotated(value, *phase_of(index)))


def swap_axes(load, store, outer, inner, shuffle):
    for low in range(0, outer, 2):
        for at in range(inner):
            sides = [load(low + side, at).reshape(256, WIDE) for side in range(2)]
            moved = jnp.dot(
                shuffle, jnp.concatenate(sides, axis=1), preferred_element_type=jnp.float32
            ).astype(jnp.bfloat16)
            for side in range(2):
                block = moved[:, side * WIDE : (side + 1) * WIDE]
                store(at, low + side, block.reshape(16, 16, WIDE))


def block_at(first, second):
    return (slice(first * 16, first * 16 + 16), slice(second * 16, second * 16 + 16))


BLOCK = 32
NOTE = 8
VMEM = pl.BlockSpec(memory_space=pltpu.VMEM)
FAR = pl.BlockSpec(memory_space=pltpu.HBM)


def params(mib):
    return pltpu.CompilerParams(vmem_limit_bytes=mib << 20)


def source_kernel(run, side, a_ref, d_ref, x_hbm, m_hbm, p_hbm, *rest):
    outs, (x_ref, m_ref, p_ref, note_ref, x_sems, m_sems, p_sem) = rest[:-7], rest[-7:]
    rows, cols, _ = x_ref.shape
    levels = m_ref.shape[0]
    starts = range(0, cols, BLOCK)
    x_copies = []
    for piece, start in enumerate(starts):
        own = (slice(None), pl.ds(start, BLOCK))
        x_copies.append(
            pltpu.make_async_copy(x_hbm.at[own], x_ref.at[own], x_sems.at[piece])
        )
    m_copies = [
        pltpu.make_async_copy(m_hbm.at[i], m_ref.at[i], m_sems.at[i]) for i in range(levels)
    ]
    p_copy = pltpu.make_async_copy(p_hbm, p_ref, p_sem)
    m_copies[0].start()
    for copy in x_copies:
        copy.start()
    for copy in m_copies[1:]:
        copy.start()
    p_copy.start()

    slowness = a_ref[...]
    note_ref[...] = jnp.zeros_like(note_ref)
    note_ref[0:1, :rows] = d_ref[...]
    note_ref[3:4, :] = slowness
    for at in (0, 3):
        left = note_ref[at : at + 1, :]
        for part in range(3):
            piece = left.astype(jnp.bfloat16).astype(jnp.float32)
            note_ref[at + part : at + part + 1, :] = piece
            left = left - piece
    note = note_ref[...].astype(jnp.bfloat16)
    kept = (run - side) * rows
    for device in range(outs[0].shape[0]):
        outs[0][device, kept : kept + NOTE, :] = note

    cosines, sines = rotation(column_of(slowness, cols))
    for level in range(levels):
        m_copies[level].wait()
        for piece, start in enumerate(starts):
            if level == 0:
                x_copies[piece].wait()
            cosine, sine = cosines[start : start + BLOCK], sines[start : start + BLOCK]

            def store(index, value):
                x_ref[index, start : start + BLOCK, :] = value

            butterfly(
                lambda index: x_ref[index, start : start + BLOCK, :],
                store,
                rows,
                1 << level,
                m_ref[level],
                lambda index: (cosine, sine),
                16,
            )

    def store_block(first, second, block):
        for inner in range(16):
            device, col = divmod(first * 16 + inner, run)
            begin = second * 16
            if col < run - side:
                begin += col * rows
                outs[0][device, begin : begin + 16, :] = block[inner]
            else:
                outs[1][device * side + col - (run - side), begin : begin + 16, :] = block[inner]

    p_copy.wait()
    swap_axes(
        lambda first, second: x_ref[block_at(first, second)],
        store_block,
        rows // 16,
        cols // 16,
        p_ref[...],
    )


def source_levels(x, matrices, slowness, dip_field, shuffle, devices, run, side):
    rows, cols, _ = x.shape
    out_shape = [jax.ShapeDtypeStruct((devices, (run - side) * rows + NOTE, WIDE), x.dtype)]
    if side:
        out_shape.append(jax.ShapeDtypeStruct((devices * side, rows, WIDE), x.dtype))
    return pl.pallas_call(
        functools.partial(source_kernel, run, side),
        out_shape=out_shape,
        in_specs=[VMEM, VMEM, FAR, FAR, FAR],
        out_specs=[VMEM] * len(out_shape),
        scratch_shapes=[
            pltpu.VMEM(x.shape, x.dtype),
            pltpu.VMEM(matrices.shape, x.dtype),
            pltpu.VMEM(shuffle.shape, x.dtype),
            pltpu.VMEM((NOTE, WIDE), jnp.float32),
            pltpu.SemaphoreType.DMA((cols // BLOCK,)),
            pltpu.SemaphoreType.DMA((matrices.shape[0],)),
            pltpu.SemaphoreType.DMA,
        ],
        compiler_params=params(60),
    )(slowness[None, :], dip_field[None, :], x, matrices, shuffle)


def middle_kernel(levels, rows, run, tgt_count, x_ref, m_ref, o_ref):
    count, total, _ = x_ref.shape
    kept = (total - NOTE) // rows
    place = lax.axis_index("src") * tgt_count + lax.axis_index("tgt")

    def noted(device, at):
        note = x_ref[device, kept * rows :, :].astype(jnp.float32)
        return note[at : at + 1] + note[at + 1 : at + 2] + note[at + 2 : at + 3]

    slowness = jnp.concatenate([noted(at, 3) for at in range(tgt_count)], axis=0)
    lanes = lax.broadcasted_iota(jnp.int32, slowness.shape, 1)
    by_col = []
    for col in range(kept):
        picked = jnp.where(lanes == place * run + col, slowness, 0.0)
        by_col.append(rotation(jnp.sum(picked, axis=1, keepdims=True)))
    by_src = [
        rotation(column_of(noted(at * tgt_count, 0), rows)) for at in range(count // tgt_count)
    ]

    for step, (apart, by_source) in enumerate(levels):
        source = x_ref if step == 0 else o_ref
        for col in range(kept):
            own = slice(col * rows, (col + 1) * rows)

            def phase_of(index):
                if by_source:
                    at = index % tgt_count
                    return tuple(table[at : at + 1, :] for table in by_col[col])
                return by_src[index // tgt_count]

            def store(index, value):
                o_ref[index, own, :] = value

            butterfly(
                lambda index: source[index, own, :],
                store,
                count,
                apart,
                m_ref[step],
                phase_of,
                16,
            )


def middle_levels(x, matrices, levels, rows, run, tgt_count):
    count, total, _ = x.shape
    return pl.pallas_call(
        functools.partial(middle_kernel, levels, rows, run, tgt_count),
        out_shape=jax.ShapeDtypeStruct((count, total - NOTE, WIDE), x.dtype),
        in_specs=[VMEM] * 2,
        out_specs=VMEM,
        compiler_params=params(32),
    )(x, matrices)


def pair_kernel(axis, bit, by_row, x_ref, y_ref, m_ref, c_ref, s_ref, o_ref):
    count, rows, _ = x_ref.shape
    matrix = m_ref[lax.rem(lax.div(lax.axis_index(axis), 1 << bit), 2)]
    group = 16
    for start in range(0, count, group):
        picked = slice(start, start + group)
        left = x_ref[picked].reshape(-1, WIDE)
        right = y_ref[picked].reshape(-1, WIDE)
        both = jnp.dot(
            jnp.concatenate([left, right], axis=1), matrix, preferred_element_type=jnp.float32
        )
        for place in range(left.shape[0] // rows):
            index = start + place
            if by_row:
                cosine, sine = c_ref[...], s_ref[...]
            else:
                cosine, sine = c_ref[index : index + 1, :], s_ref[index : index + 1, :]
            o_ref[index] = rotated(both[place * rows : (place + 1) * rows], cosine, sine)


def pair_level(x, axis, bit, matrix, angles, by_row):
    count = lax.axis_size(axis)
    other = lax.ppermute(x, axis, [(i, i ^ 1 << bit) for i in range(count)])
    flipped = np.roll(matrix, (WIDE, WIDE), (0, 1))
    halves = jnp.asarray(np.stack([matrix[:, :WIDE], flipped[:, :WIDE]]))
    return pl.pallas_call(
        functools.partial(pair_kernel, axis, bit, by_row),
        out_shape=jax.ShapeDtypeStruct(x.shape, x.dtype),
        in_specs=[VMEM] * 5,
        out_specs=VMEM,
        compiler_params=params(32),
    )(x, other, halves, *angles)


def target_kernel(run, m_ref, c_ref, s_ref, p_ref, *rest):
    xs, (o_ref, state_ref) = rest[:-2], rest[-2:]
    cols, rows, _ = state_ref.shape
    kept = xs[0].shape[1] // rows
    side = run - kept
    levels = m_ref.shape[0]

    def first(index, start):
        device, col = divmod(index, run)
        if col < kept:
            start += col * rows
            return xs[0][device, start : start + 16, :]
        return xs[1][device * side + col - kept, start : start + 16, :]

    for level in range(levels):
        for start in range(0, rows, 16):
            own = slice(start, start + 16)
            cosine, sine = c_ref[own, :], s_ref[own, :]

            def load(index):
                return first(index, start) if level == 0 else state_ref[index, own, :]

            def store(index, value):
                state_ref[index, own, :] = value

            butterfly(
                load,
                store,
                cols,
                1 << (levels - 1 - level),
                m_ref[level],
                lambda index: (cosine, sine),
                32,
            )

    def store_block(first, second, block):
        o_ref[block_at(first, second)] = block

    swap_axes(
        lambda first, second: state_ref[block_at(first, second)],
        store_block,
        cols // 16,
        rows // 16,
        p_ref[...],
    )


def target_levels(states, matrices, angles, shuffle, cols, rows, run):
    return pl.pallas_call(
        functools.partial(target_kernel, run),
        out_shape=jax.ShapeDtypeStruct((rows, cols, WIDE), jnp.bfloat16),
        in_specs=[VMEM] * (4 + len(states)),
        out_specs=VMEM,
        scratch_shapes=[pltpu.VMEM((cols, rows, WIDE), jnp.bfloat16)],
        compiler_params=params(32),
    )(matrices, *angles, shuffle, *states)


def local(box_weights, slowness, dip_field):
    rows, cols, _ = box_weights.shape
    src_count = lax.axis_size("src")
    tgt_count = lax.axis_size("tgt")
    devices = src_count * tgt_count
    row_bits, col_bits = rows.bit_length() - 1, cols.bit_length() - 1
    src_bits, tgt_bits = src_count.bit_length() - 1, tgt_count.bit_length() - 1
    first_target = row_bits + src_bits
    total = first_target + tgt_bits + col_bits
    matrices = [level_matrix(number) for number in range(total)]

    def matrices_of(low, high):
        return jnp.asarray(np.stack(matrices[low:high]))

    run = cols // devices
    side = run // 4
    shuffle = jnp.asarray(shuffle_matrix())

    states = source_levels(
        box_weights, matrices_of(0, row_bits), slowness, dip_field, shuffle, devices, run, side
    )
    *states, slowness, dip_field = lax.optimization_barrier((*states, slowness, dip_field))
    by_row = tables(dip_field)

    state = lax.all_to_all(states[0], ("src", "tgt"), 0, 0, tiled=True)
    if side:
        kept = slowness.reshape(devices, run)[:, run - side :].reshape(-1)
        by_col = tables(kept)
        stay = states[1]
        for bit in range(src_bits):
            stay = pair_level(stay, "src", bit, matrices[row_bits + bit], by_col, False)
        state, stay = lax.optimization_barrier((state, stay))
        for at, bit in enumerate(reversed(range(tgt_bits))):
            stay = pair_level(stay, "tgt", bit, matrices[first_target + at], by_row, True)

    levels = [(tgt_count << bit, True) for bit in range(src_bits)]
    levels += [(1 << bit, False) for bit in reversed(range(tgt_bits))]
    state = middle_levels(
        state, matrices_of(row_bits, first_target + tgt_bits), levels, rows, run, tgt_count
    )
    state = lax.all_to_all(state, ("src", "tgt"), 0, 0, tiled=True)

    return target_levels(
        [state, stay] if side else [state],
        matrices_of(first_target + tgt_bits, total),
        by_row,
        shuffle,
        cols,
        rows,
        run,
    )


def solution(mesh):
    in_specs = (P("src", "tgt", None), P("tgt"), P("src"))
    out_specs = P("src", "tgt", None)
    return jax.shard_map(local, mesh=mesh, in_specs=in_specs, out_specs=out_specs, check_vma=False)
```

```python
import functools
import math

import jax
import jax.numpy as jnp
import ml_dtypes
import numpy as np
from jax import lax
from jax.experimental import pallas as pl
from jax.experimental.pallas import tpu as pltpu
from jax.sharding import PartitionSpec as P

HALF = 64
WIDE = 128


def nodes():
    points = np.cos((2.0 * np.arange(8) + 1.0) * (math.pi / 16.0))
    return np.repeat(points, 8), np.tile(points, 8)


def node_weights():
    first, second = nodes()
    return (first * first + second * second).astype(np.float32)


def level_matrix(number):
    first, second = nodes()
    frequency = 9.0 + 3.0 * (number % 5)
    shifts = np.array([-0.5, 0.5])
    out_first = first[None, :] + shifts[:, None]
    in_second = second[None, :] + shifts[:, None]
    inner = (
        out_first[:, None, :, None] * first[None, None, None, :]
        + second[None, None, :, None] * in_second[None, :, None, :]
    )
    out_norm = np.sqrt(out_first**2 + second[None, :] ** 2)
    in_norm = np.sqrt(first[None, :] ** 2 + in_second**2)
    phases = frequency * (inner + 0.5 * out_norm[:, None, :, None] * in_norm[None, :, None, :])
    factor = 1.0 / math.sqrt(128.0)
    real = np.transpose(factor * np.cos(phases), (1, 3, 0, 2))
    imag = np.transpose(factor * np.sin(phases), (1, 3, 0, 2))
    upper = np.concatenate([real, imag], axis=3)
    lower = np.concatenate([-imag, real], axis=3)
    full = np.concatenate([upper, lower], axis=1)
    return full.reshape(2 * WIDE, 2 * WIDE).astype(ml_dtypes.bfloat16)


def tables(scales):
    weights = np.tile(node_weights(), 2)
    angles = scales[..., None] * weights
    signs = np.repeat(np.array([-1.0, 1.0], np.float32), HALF)
    return jnp.cos(angles), jnp.sin(angles) * signs


def shuffle_matrix():
    rows = np.arange(256)
    found = np.zeros((256, 256), np.float32)
    found[rows, rows % 16 * 16 + rows // 16] = 1.0
    return found.astype(ml_dtypes.bfloat16)


def cos_sin(angles):
    turns = jnp.floor(angles * (2.0 / math.pi) + 0.5)
    rest = angles - turns * 1.5703125
    rest = rest - turns * 4.837512969970703125e-4
    rest = rest - turns * 7.54978995489188e-8
    square = rest * rest
    sine = 1.0 / 362880.0
    for factor in (-1.0 / 5040.0, 1.0 / 120.0, -1.0 / 6.0, 1.0):
        sine = sine * square + factor
    sine = sine * rest
    cosine = -1.0 / 3628800.0
    for factor in (1.0 / 40320.0, -1.0 / 720.0, 1.0 / 24.0, -0.5, 1.0):
        cosine = cosine * square + factor
    quarter = turns.astype(jnp.int32)
    odd = (quarter & 1) == 1
    first = jnp.where(odd, sine, cosine)
    second = jnp.where(odd, cosine, sine)
    first = jnp.where(((quarter + 1) & 2) == 2, -first, first)
    second = jnp.where((quarter & 2) == 2, -second, second)
    return first, second


def node_row():
    lanes = lax.broadcasted_iota(jnp.int32, (1, WIDE), 1) % HALF
    points = [math.cos((2 * a + 1) * math.pi / 16) ** 2 for a in range(4)]

    def square(at):
        near = jnp.minimum(at, 7 - at)
        value = jnp.full(near.shape, points[3], jnp.float32)
        for a in range(3):
            value = jnp.where(near == a, jnp.float32(points[a]), value)
        return value

    return square(lanes // 8) + square(lanes % 8)


def rotation(column):
    cosine, sine = cos_sin(column * node_row())
    lanes = lax.broadcasted_iota(jnp.int32, cosine.shape, 1)
    return cosine, jnp.where(lanes < HALF, -sine, sine)


def column_of(row, count):
    shape = (count, WIDE)
    here = lax.broadcasted_iota(jnp.int32, shape, 0) == lax.broadcasted_iota(jnp.int32, shape, 1)
    return jnp.sum(jnp.where(here, jnp.broadcast_to(row, shape), 0.0), axis=1, keepdims=True)


def rotated(value, cosine, sine):
    return (value * cosine + pltpu.roll(value, HALF, 1) * sine).astype(jnp.bfloat16)


def butterfly(load, store, count, apart, matrix, phase_of, group):
    lows = [i for i in range(count) if not i & apart]
    for start in range(0, len(lows), group):
        picked = lows[start : start + group]
        left = jnp.concatenate([load(i) for i in picked], axis=0)
        right = jnp.concatenate([load(i + apart) for i in picked], axis=0)
        rows = left.shape[0] // len(picked)
        both = jnp.dot(
            jnp.concatenate([left, right], axis=1), matrix, preferred_element_type=jnp.float32
        )
        for place, low in enumerate(picked):
            for child in range(2):
                index = low + child * apart
                value = both[
                    place * rows : (place + 1) * rows, child * WIDE : (child + 1) * WIDE
                ]
                store(index, rotated(value, *phase_of(index)))


def swap_axes(load, store, outer, inner, shuffle):
    for low in range(0, outer, 2):
        for at in range(inner):
            sides = [load(low + side, at).reshape(256, WIDE) for side in range(2)]
            moved = jnp.dot(
                shuffle, jnp.concatenate(sides, axis=1), preferred_element_type=jnp.float32
            ).astype(jnp.bfloat16)
            for side in range(2):
                block = moved[:, side * WIDE : (side + 1) * WIDE]
                store(at, low + side, block.reshape(16, 16, WIDE))


def block_at(first, second):
    return (slice(first * 16, first * 16 + 16), slice(second * 16, second * 16 + 16))


BLOCK = 32
NOTE = 8
VMEM = pl.BlockSpec(memory_space=pltpu.VMEM)
FAR = pl.BlockSpec(memory_space=pltpu.HBM)


def params(mib):
    return pltpu.CompilerParams(vmem_limit_bytes=mib << 20)


def weighed(flops):
    return pl.CostEstimate(flops=flops, bytes_accessed=1 << 20, transcendentals=0)


def source_kernel(first_col, keep, a_ref, d_ref, x_hbm, m_hbm, p_hbm, *rest):
    o_ref, x_ref, m_ref, p_ref, note_ref, x_sems, m_sems, p_sem = rest
    rows, cols, _ = x_ref.shape
    levels = m_ref.shape[0]
    starts = range(0, cols, BLOCK)
    x_copies = [
        pltpu.make_async_copy(
            x_hbm.at[:, pl.ds(first_col + start, BLOCK)],
            x_ref.at[:, pl.ds(start, BLOCK)],
            x_sems.at[piece],
        )
        for piece, start in enumerate(starts)
    ]
    m_copies = [
        pltpu.make_async_copy(m_hbm.at[i], m_ref.at[i], m_sems.at[i]) for i in range(levels)
    ]
    p_copy = pltpu.make_async_copy(p_hbm, p_ref, p_sem)
    m_copies[0].start()
    for copy in x_copies:
        copy.start()
    for copy in m_copies[1:]:
        copy.start()
    p_copy.start()

    slowness = a_ref[...]
    if keep:
        note_ref[...] = jnp.zeros_like(note_ref)
        note_ref[0:1, :rows] = d_ref[...]
        note_ref[3:4, :] = slowness
        for at in (0, 3):
            left = note_ref[at : at + 1, :]
            for part in range(3):
                piece = left.astype(jnp.bfloat16).astype(jnp.float32)
                note_ref[at + part : at + part + 1, :] = piece
                left = left - piece
        note = note_ref[...].astype(jnp.bfloat16)
        for device in range(o_ref.shape[0]):
            o_ref[device, keep * rows : keep * rows + NOTE, :] = note

    cosines, sines = rotation(column_of(slowness, first_col + cols)[first_col:])
    for level in range(levels):
        m_copies[level].wait()
        for piece, start in enumerate(starts):
            if level == 0:
                x_copies[piece].wait()
            cosine, sine = cosines[start : start + BLOCK], sines[start : start + BLOCK]

            def store(index, value):
                x_ref[index, start : start + BLOCK, :] = value

            butterfly(
                lambda index: x_ref[index, start : start + BLOCK, :],
                store,
                rows,
                1 << level,
                m_ref[level],
                lambda index: (cosine, sine),
                16,
            )

    def store_block(first, second, block):
        begin = second * 16
        if not keep:
            o_ref[first * 16 : first * 16 + 16, begin : begin + 16, :] = block
            return
        for inner in range(16):
            device, col = divmod(first * 16 + inner, keep)
            at = col * rows + begin
            o_ref[device, at : at + 16, :] = block[inner]

    p_copy.wait()
    swap_axes(
        lambda first, second: x_ref[block_at(first, second)],
        store_block,
        rows // 16,
        cols // 16,
        p_ref[...],
    )


def source_levels(x, matrices, slowness, dip_field, shuffle, first_col, count, keep):
    rows = x.shape[0]
    shape = (count // keep, keep * rows + NOTE, WIDE) if keep else (count, rows, WIDE)
    return pl.pallas_call(
        functools.partial(source_kernel, first_col, keep),
        out_shape=jax.ShapeDtypeStruct(shape, x.dtype),
        in_specs=[VMEM, VMEM, FAR, FAR, FAR],
        out_specs=VMEM,
        scratch_shapes=[
            pltpu.VMEM((rows, count, WIDE), x.dtype),
            pltpu.VMEM(matrices.shape, x.dtype),
            pltpu.VMEM(shuffle.shape, x.dtype),
            pltpu.VMEM((NOTE, WIDE), jnp.float32),
            pltpu.SemaphoreType.DMA((count // BLOCK,)),
            pltpu.SemaphoreType.DMA((matrices.shape[0],)),
            pltpu.SemaphoreType.DMA,
        ],
        cost_estimate=weighed(10**10),
        compiler_params=params(60),
    )(slowness[None, :], dip_field[None, :], x, matrices, shuffle)


def middle_kernel(levels, rows, tgt_count, x_ref, m_ref, o_ref):
    count, total, _ = x_ref.shape
    kept = (total - NOTE) // rows
    place = lax.axis_index("src") * tgt_count + lax.axis_index("tgt")

    def noted(device, at):
        note = x_ref[device, kept * rows :, :].astype(jnp.float32)
        return note[at : at + 1] + note[at + 1 : at + 2] + note[at + 2 : at + 3]

    slowness = jnp.concatenate([noted(at, 3) for at in range(tgt_count)], axis=0)
    lanes = lax.broadcasted_iota(jnp.int32, slowness.shape, 1)
    by_col = []
    for col in range(kept):
        picked = jnp.where(lanes == place * kept + col, slowness, 0.0)
        by_col.append(rotation(jnp.sum(picked, axis=1, keepdims=True)))
    by_src = [
        rotation(column_of(noted(at * tgt_count, 0), rows)) for at in range(count // tgt_count)
    ]

    for step, (apart, by_source) in enumerate(levels):
        source = x_ref if step == 0 else o_ref
        for col in range(kept):
            own = slice(col * rows, (col + 1) * rows)

            def phase_of(index):
                if by_source:
                    at = index % tgt_count
                    return tuple(table[at : at + 1, :] for table in by_col[col])
                return by_src[index // tgt_count]

            def store(index, value):
                o_ref[index, own, :] = value

            butterfly(
                lambda index: source[index, own, :],
                store,
                count,
                apart,
                m_ref[step],
                phase_of,
                16,
            )


def middle_levels(x, matrices, levels, rows, tgt_count):
    count, total, _ = x.shape
    return pl.pallas_call(
        functools.partial(middle_kernel, levels, rows, tgt_count),
        out_shape=jax.ShapeDtypeStruct((count, total - NOTE, WIDE), x.dtype),
        in_specs=[VMEM] * 2,
        out_specs=VMEM,
        cost_estimate=weighed(2 * 10**10),
        compiler_params=params(32),
    )(x, matrices)


def pair_kernel(axis, bit, by_row, x_ref, y_ref, m_ref, c_ref, s_ref, o_ref):
    count, rows, _ = x_ref.shape
    matrix = m_ref[lax.rem(lax.div(lax.axis_index(axis), 1 << bit), 2)]
    group = 16
    for start in range(0, count, group):
        picked = slice(start, start + group)
        left = x_ref[picked].reshape(-1, WIDE)
        right = y_ref[picked].reshape(-1, WIDE)
        both = jnp.dot(
            jnp.concatenate([left, right], axis=1), matrix, preferred_element_type=jnp.float32
        )
        for place in range(left.shape[0] // rows):
            index = start + place
            if by_row:
                cosine, sine = c_ref[...], s_ref[...]
            else:
                cosine, sine = c_ref[index : index + 1, :], s_ref[index : index + 1, :]
            o_ref[index] = rotated(both[place * rows : (place + 1) * rows], cosine, sine)


def pair_level(x, axis, bit, matrix, angles, by_row):
    count = lax.axis_size(axis)
    other = lax.ppermute(x, axis, [(i, i ^ 1 << bit) for i in range(count)])
    flipped = np.roll(matrix, (WIDE, WIDE), (0, 1))
    halves = jnp.asarray(np.stack([matrix[:, :WIDE], flipped[:, :WIDE]]))
    return pl.pallas_call(
        functools.partial(pair_kernel, axis, bit, by_row),
        out_shape=jax.ShapeDtypeStruct(x.shape, x.dtype),
        in_specs=[VMEM] * 5,
        out_specs=VMEM,
        compiler_params=params(32),
    )(x, other, halves, *angles)


def target_kernel(m_ref, c_ref, s_ref, p_ref, *rest):
    xs, (o_ref, state_ref) = rest[:-2], rest[-2:]
    cols, rows, _ = state_ref.shape
    devices, kept = xs[0].shape[0], xs[0].shape[1] // rows
    levels = m_ref.shape[0]

    def first(index, start):
        if index >= devices * kept:
            return xs[1][index - devices * kept, start : start + 16, :]
        device, col = divmod(index, kept)
        start += col * rows
        return xs[0][device, start : start + 16, :]

    for level in range(levels):
        for start in range(0, rows, 16):
            own = slice(start, start + 16)
            cosine, sine = c_ref[own, :], s_ref[own, :]

            def load(index):
                return first(index, start) if level == 0 else state_ref[index, own, :]

            def store(index, value):
                state_ref[index, own, :] = value

            butterfly(
                load,
                store,
                cols,
                1 << (levels - 1 - level),
                m_ref[level],
                lambda index: (cosine, sine),
                32,
            )

    def store_block(first, second, block):
        o_ref[block_at(first, second)] = block

    swap_axes(
        lambda first, second: state_ref[block_at(first, second)],
        store_block,
        cols // 16,
        rows // 16,
        p_ref[...],
    )


def target_levels(states, matrices, angles, shuffle, cols, rows):
    return pl.pallas_call(
        target_kernel,
        out_shape=jax.ShapeDtypeStruct((rows, cols, WIDE), jnp.bfloat16),
        in_specs=[VMEM] * (4 + len(states)),
        out_specs=VMEM,
        scratch_shapes=[pltpu.VMEM((cols, rows, WIDE), jnp.bfloat16)],
        compiler_params=params(32),
    )(matrices, *angles, shuffle, *states)


def local(box_weights, slowness, dip_field):
    rows, cols, _ = box_weights.shape
    src_count = lax.axis_size("src")
    tgt_count = lax.axis_size("tgt")
    devices = src_count * tgt_count
    row_bits, col_bits = rows.bit_length() - 1, cols.bit_length() - 1
    src_bits, tgt_bits = src_count.bit_length() - 1, tgt_count.bit_length() - 1
    first_target = row_bits + src_bits
    total = first_target + tgt_bits + col_bits
    matrices = [level_matrix(number) for number in range(total)]

    def matrices_of(low, high):
        return jnp.asarray(np.stack(matrices[low:high]))

    run = cols // devices
    side = run // 4
    keep = run - side
    sent = devices * keep
    shuffle = jnp.asarray(shuffle_matrix())

    first = matrices_of(0, row_bits)
    sources = (box_weights, first, slowness, dip_field, shuffle)
    if side:
        stay = source_levels(*sources, sent, cols - sent, 0)
    state = source_levels(*sources, 0, sent, keep)
    state, slowness, dip_field = lax.optimization_barrier((state, slowness, dip_field))
    by_row = tables(dip_field)

    state = lax.all_to_all(state, ("src", "tgt"), 0, 0, tiled=True)
    if side:
        by_col = tables(slowness[sent:])
        for bit in range(src_bits):
            stay = pair_level(stay, "src", bit, matrices[row_bits + bit], by_col, False)
        state, stay = lax.optimization_barrier((state, stay))
        for at, bit in enumerate(reversed(range(tgt_bits))):
            stay = pair_level(stay, "tgt", bit, matrices[first_target + at], by_row, True)

    levels = [(tgt_count << bit, True) for bit in range(src_bits)]
    levels += [(1 << bit, False) for bit in reversed(range(tgt_bits))]
    state = middle_levels(
        state, matrices_of(row_bits, first_target + tgt_bits), levels, rows, tgt_count
    )
    state = lax.all_to_all(state, ("src", "tgt"), 0, 0, tiled=True)

    return target_levels(
        [state, stay] if side else [state],
        matrices_of(first_target + tgt_bits, total),
        by_row,
        shuffle,
        cols,
        rows,
    )


def solution(mesh):
    in_specs = (P("src", "tgt", None), P("tgt"), P("src"))
    out_specs = P("src", "tgt", None)
    return jax.shard_map(local, mesh=mesh, in_specs=in_specs, out_specs=out_specs, check_vma=False)
```

```python
import functools
import math

import jax
import jax.numpy as jnp
import ml_dtypes
import numpy as np
from jax import lax
from jax.experimental import pallas as pl
from jax.experimental.pallas import tpu as pltpu
from jax.sharding import PartitionSpec as P

HALF = 64
WIDE = 128


def nodes():
    points = np.cos((2.0 * np.arange(8) + 1.0) * (math.pi / 16.0))
    return np.repeat(points, 8), np.tile(points, 8)


def node_weights():
    first, second = nodes()
    return (first * first + second * second).astype(np.float32)


def level_matrix(number):
    first, second = nodes()
    frequency = 9.0 + 3.0 * (number % 5)
    shifts = np.array([-0.5, 0.5])
    out_first = first[None, :] + shifts[:, None]
    in_second = second[None, :] + shifts[:, None]
    inner = (
        out_first[:, None, :, None] * first[None, None, None, :]
        + second[None, None, :, None] * in_second[None, :, None, :]
    )
    out_norm = np.sqrt(out_first**2 + second[None, :] ** 2)
    in_norm = np.sqrt(first[None, :] ** 2 + in_second**2)
    phases = frequency * (inner + 0.5 * out_norm[:, None, :, None] * in_norm[None, :, None, :])
    factor = 1.0 / math.sqrt(128.0)
    real = np.transpose(factor * np.cos(phases), (1, 3, 0, 2))
    imag = np.transpose(factor * np.sin(phases), (1, 3, 0, 2))
    upper = np.concatenate([real, imag], axis=3)
    lower = np.concatenate([-imag, real], axis=3)
    full = np.concatenate([upper, lower], axis=1)
    swapped = np.concatenate([full[..., HALF:], full[..., :HALF]], axis=3)
    whole = [part.reshape(2 * WIDE, 2 * WIDE) for part in (full, swapped)]
    return np.concatenate(whole, axis=1).astype(ml_dtypes.bfloat16)


def tables(scales):
    weights = np.tile(node_weights(), 2)
    angles = scales[..., None] * weights
    signs = np.repeat(np.array([-1.0, 1.0], np.float32), HALF)
    return jnp.cos(angles), jnp.sin(angles) * signs


def shuffle_matrix():
    rows = np.arange(256)
    found = np.zeros((256, 256), np.float32)
    found[rows, rows % 16 * 16 + rows // 16] = 1.0
    return found.astype(ml_dtypes.bfloat16)


def cos_sin(angles):
    turns = jnp.floor(angles * (2.0 / math.pi) + 0.5)
    rest = angles - turns * 1.5703125
    rest = rest - turns * 4.837512969970703125e-4
    rest = rest - turns * 7.54978995489188e-8
    square = rest * rest
    sine = 1.0 / 362880.0
    for factor in (-1.0 / 5040.0, 1.0 / 120.0, -1.0 / 6.0, 1.0):
        sine = sine * square + factor
    sine = sine * rest
    cosine = -1.0 / 3628800.0
    for factor in (1.0 / 40320.0, -1.0 / 720.0, 1.0 / 24.0, -0.5, 1.0):
        cosine = cosine * square + factor
    quarter = turns.astype(jnp.int32)
    odd = (quarter & 1) == 1
    first = jnp.where(odd, sine, cosine)
    second = jnp.where(odd, cosine, sine)
    first = jnp.where(((quarter + 1) & 2) == 2, -first, first)
    second = jnp.where((quarter & 2) == 2, -second, second)
    return first, second


def node_row():
    lanes = lax.broadcasted_iota(jnp.int32, (1, WIDE), 1) % HALF
    points = [math.cos((2 * a + 1) * math.pi / 16) ** 2 for a in range(4)]

    def square(at):
        near = jnp.minimum(at, 7 - at)
        value = jnp.full(near.shape, points[3], jnp.float32)
        for a in range(3):
            value = jnp.where(near == a, jnp.float32(points[a]), value)
        return value

    return square(lanes // 8) + square(lanes % 8)


def rotation(column):
    cosine, sine = cos_sin(column * node_row())
    lanes = lax.broadcasted_iota(jnp.int32, cosine.shape, 1)
    return cosine, jnp.where(lanes < HALF, -sine, sine)


def column_of(row, count):
    shape = (count, WIDE)
    here = lax.broadcasted_iota(jnp.int32, shape, 0) == lax.broadcasted_iota(jnp.int32, shape, 1)
    return jnp.sum(jnp.where(here, jnp.broadcast_to(row, shape), 0.0), axis=1, keepdims=True)


def butterfly(load, store, count, apart, matrix, phase_of, group):
    lows = [i for i in range(count) if not i & apart]
    for start in range(0, len(lows), group):
        picked = lows[start : start + group]
        left = jnp.concatenate([load(i) for i in picked], axis=0)
        right = jnp.concatenate([load(i + apart) for i in picked], axis=0)
        rows = left.shape[0] // len(picked)
        both = jnp.dot(
            jnp.concatenate([left, right], axis=1), matrix, preferred_element_type=jnp.float32
        )
        for place, low in enumerate(picked):
            for child in range(2):
                index = low + child * apart
                cosine, sine = phase_of(index)
                mine = slice(place * rows, (place + 1) * rows)
                at = child * WIDE
                value = both[mine, at : at + WIDE] * cosine
                value += both[mine, at + 2 * WIDE : at + 3 * WIDE] * sine
                store(index, value.astype(jnp.bfloat16))


def swap_axes(load, store, outer, inner, shuffle):
    for low in range(0, outer, 2):
        for at in range(inner):
            sides = [load(low + side, at).reshape(256, WIDE) for side in range(2)]
            moved = jnp.dot(
                shuffle, jnp.concatenate(sides, axis=1), preferred_element_type=jnp.float32
            ).astype(jnp.bfloat16)
            for side in range(2):
                block = moved[:, side * WIDE : (side + 1) * WIDE]
                store(at, low + side, block.reshape(16, 16, WIDE))


def block_at(first, second):
    return (slice(first * 16, first * 16 + 16), slice(second * 16, second * 16 + 16))


BLOCK = 32
NOTE = 8
VMEM = pl.BlockSpec(memory_space=pltpu.VMEM)
FAR = pl.BlockSpec(memory_space=pltpu.HBM)


def params(mib):
    return pltpu.CompilerParams(vmem_limit_bytes=mib << 20)


def weighed(flops):
    return pl.CostEstimate(flops=flops, bytes_accessed=1 << 20, transcendentals=0)


def source_kernel(first_col, keep, a_ref, d_ref, x_hbm, m_hbm, p_hbm, *rest):
    o_ref, x_ref, m_ref, p_ref, note_ref, x_sems, m_sems, p_sem = rest
    rows, cols, _ = x_ref.shape
    levels = m_ref.shape[0]
    starts = range(0, cols, BLOCK)
    x_copies = [
        pltpu.make_async_copy(
            x_hbm.at[:, pl.ds(first_col + start, BLOCK)],
            x_ref.at[:, pl.ds(start, BLOCK)],
            x_sems.at[piece],
        )
        for piece, start in enumerate(starts)
    ]
    m_copies = [
        pltpu.make_async_copy(m_hbm.at[i], m_ref.at[i], m_sems.at[i]) for i in range(levels)
    ]
    p_copy = pltpu.make_async_copy(p_hbm, p_ref, p_sem)
    m_copies[0].start()
    for copy in x_copies:
        copy.start()
    for copy in m_copies[1:]:
        copy.start()
    p_copy.start()

    slowness = a_ref[...]
    if keep:
        note_ref[...] = jnp.zeros_like(note_ref)
        note_ref[0:1, :rows] = d_ref[...]
        note_ref[3:4, :] = slowness
        for at in (0, 3):
            left = note_ref[at : at + 1, :]
            for part in range(3):
                piece = left.astype(jnp.bfloat16).astype(jnp.float32)
                note_ref[at + part : at + part + 1, :] = piece
                left = left - piece
        note = note_ref[...].astype(jnp.bfloat16)
        for device in range(o_ref.shape[0]):
            o_ref[device, keep * rows : keep * rows + NOTE, :] = note

    cosines, sines = rotation(column_of(slowness, first_col + cols)[first_col:])
    for level in range(levels):
        m_copies[level].wait()
        for piece, start in enumerate(starts):
            if level == 0:
                x_copies[piece].wait()
            cosine, sine = cosines[start : start + BLOCK], sines[start : start + BLOCK]

            def store(index, value):
                x_ref[index, start : start + BLOCK, :] = value

            butterfly(
                lambda index: x_ref[index, start : start + BLOCK, :],
                store,
                rows,
                1 << level,
                m_ref[level],
                lambda index: (cosine, sine),
                8,
            )

    def store_block(first, second, block):
        begin = second * 16
        if not keep:
            o_ref[first * 16 : first * 16 + 16, begin : begin + 16, :] = block
            return
        for inner in range(16):
            device, col = divmod(first * 16 + inner, keep)
            at = col * rows + begin
            o_ref[device, at : at + 16, :] = block[inner]

    p_copy.wait()
    swap_axes(
        lambda first, second: x_ref[block_at(first, second)],
        store_block,
        rows // 16,
        cols // 16,
        p_ref[...],
    )


def source_levels(x, matrices, slowness, dip_field, shuffle, first_col, count, keep):
    rows = x.shape[0]
    shape = (count // keep, keep * rows + NOTE, WIDE) if keep else (count, rows, WIDE)
    return pl.pallas_call(
        functools.partial(source_kernel, first_col, keep),
        out_shape=jax.ShapeDtypeStruct(shape, x.dtype),
        in_specs=[VMEM, VMEM, FAR, FAR, FAR],
        out_specs=VMEM,
        scratch_shapes=[
            pltpu.VMEM((rows, count, WIDE), x.dtype),
            pltpu.VMEM(matrices.shape, x.dtype),
            pltpu.VMEM(shuffle.shape, x.dtype),
            pltpu.VMEM((NOTE, WIDE), jnp.float32),
            pltpu.SemaphoreType.DMA((count // BLOCK,)),
            pltpu.SemaphoreType.DMA((matrices.shape[0],)),
            pltpu.SemaphoreType.DMA,
        ],
        cost_estimate=weighed(10**10),
        compiler_params=params(60),
    )(slowness[None, :], dip_field[None, :], x, matrices, shuffle)


def middle_kernel(levels, rows, tgt_count, x_ref, m_ref, o_ref):
    count, total, _ = x_ref.shape
    kept = (total - NOTE) // rows
    place = lax.axis_index("src") * tgt_count + lax.axis_index("tgt")

    def noted(device, at):
        note = x_ref[device, kept * rows :, :].astype(jnp.float32)
        return note[at : at + 1] + note[at + 1 : at + 2] + note[at + 2 : at + 3]

    slowness = jnp.concatenate([noted(at, 3) for at in range(tgt_count)], axis=0)
    lanes = lax.broadcasted_iota(jnp.int32, slowness.shape, 1)
    by_col = []
    for col in range(kept):
        picked = jnp.where(lanes == place * kept + col, slowness, 0.0)
        by_col.append(rotation(jnp.sum(picked, axis=1, keepdims=True)))
    by_src = [
        rotation(column_of(noted(at * tgt_count, 0), rows)) for at in range(count // tgt_count)
    ]

    for step, (apart, by_source) in enumerate(levels):
        source = x_ref if step == 0 else o_ref
        for col in range(kept):
            own = slice(col * rows, (col + 1) * rows)

            def phase_of(index):
                if by_source:
                    at = index % tgt_count
                    return tuple(table[at : at + 1, :] for table in by_col[col])
                return by_src[index // tgt_count]

            def store(index, value):
                o_ref[index, own, :] = value

            butterfly(
                lambda index: source[index, own, :],
                store,
                count,
                apart,
                m_ref[step],
                phase_of,
                8,
            )


def middle_levels(x, matrices, levels, rows, tgt_count):
    count, total, _ = x.shape
    return pl.pallas_call(
        functools.partial(middle_kernel, levels, rows, tgt_count),
        out_shape=jax.ShapeDtypeStruct((count, total - NOTE, WIDE), x.dtype),
        in_specs=[VMEM] * 2,
        out_specs=VMEM,
        cost_estimate=weighed(2 * 10**10),
        compiler_params=params(32),
    )(x, matrices)


def target_kernel(m_ref, c_ref, s_ref, p_ref, x_ref, o_ref, state_ref):
    cols, rows, _ = state_ref.shape
    kept = x_ref.shape[1] // rows
    levels = m_ref.shape[0]

    def first(index, start):
        device, col = divmod(index, kept)
        start += col * rows
        return x_ref[device, start : start + 16, :]

    for level in range(levels):
        for start in range(0, rows, 16):
            own = slice(start, start + 16)
            cosine, sine = c_ref[own, :], s_ref[own, :]

            def load(index):
                return first(index, start) if level == 0 else state_ref[index, own, :]

            def store(index, value):
                state_ref[index, own, :] = value

            butterfly(
                load,
                store,
                cols,
                1 << (levels - 1 - level),
                m_ref[level],
                lambda index: (cosine, sine),
                16,
            )

    def store_block(first, second, block):
        o_ref[block_at(first, second)] = block

    swap_axes(
        lambda first, second: state_ref[block_at(first, second)],
        store_block,
        cols // 16,
        rows // 16,
        p_ref[...],
    )


def target_levels(x, matrices, angles, shuffle, cols, rows):
    return pl.pallas_call(
        target_kernel,
        out_shape=jax.ShapeDtypeStruct((rows, cols, WIDE), jnp.bfloat16),
        in_specs=[VMEM] * 5,
        out_specs=VMEM,
        scratch_shapes=[pltpu.VMEM((cols, rows, WIDE), jnp.bfloat16)],
        compiler_params=params(32),
    )(matrices, *angles, shuffle, x)


def local(box_weights, slowness, dip_field):
    rows, cols, _ = box_weights.shape
    src_count = lax.axis_size("src")
    tgt_count = lax.axis_size("tgt")
    devices = src_count * tgt_count
    row_bits, col_bits = rows.bit_length() - 1, cols.bit_length() - 1
    src_bits, tgt_bits = src_count.bit_length() - 1, tgt_count.bit_length() - 1
    first_target = row_bits + src_bits
    total = first_target + tgt_bits + col_bits
    matrices = [level_matrix(number) for number in range(total)]

    def matrices_of(low, high):
        return jnp.asarray(np.stack(matrices[low:high]))

    keep = cols // devices
    shuffle = jnp.asarray(shuffle_matrix())

    state = source_levels(
        box_weights, matrices_of(0, row_bits), slowness, dip_field, shuffle, 0, cols, keep
    )
    state, dip_field = lax.optimization_barrier((state, dip_field))
    by_row = tables(dip_field)

    state = lax.all_to_all(state, ("src", "tgt"), 0, 0, tiled=True)
    levels = [(tgt_count << bit, True) for bit in range(src_bits)]
    levels += [(1 << bit, False) for bit in reversed(range(tgt_bits))]
    state = middle_levels(
        state, matrices_of(row_bits, first_target + tgt_bits), levels, rows, tgt_count
    )
    state = lax.all_to_all(state, ("src", "tgt"), 0, 0, tiled=True)

    return target_levels(
        state,
        matrices_of(first_target + tgt_bits, total),
        by_row,
        shuffle,
        cols,
        rows,
    )


def solution(mesh):
    in_specs = (P("src", "tgt", None), P("tgt"), P("src"))
    out_specs = P("src", "tgt", None)
    return jax.shard_map(local, mesh=mesh, in_specs=in_specs, out_specs=out_specs, check_vma=False)
```

```python
import functools
import math

import jax
import jax.numpy as jnp
import ml_dtypes
import numpy as np
from jax import lax
from jax.experimental import pallas as pl
from jax.experimental.pallas import tpu as pltpu
from jax.sharding import PartitionSpec as P

HALF = 64
WIDE = 128


def nodes():
    points = np.cos((2.0 * np.arange(8) + 1.0) * (math.pi / 16.0))
    return np.repeat(points, 8), np.tile(points, 8)


def node_weights():
    first, second = nodes()
    return (first * first + second * second).astype(np.float32)


def level_matrix(number):
    first, second = nodes()
    frequency = 9.0 + 3.0 * (number % 5)
    shifts = np.array([-0.5, 0.5])
    out_first = first[None, :] + shifts[:, None]
    in_second = second[None, :] + shifts[:, None]
    inner = (
        out_first[:, None, :, None] * first[None, None, None, :]
        + second[None, None, :, None] * in_second[None, :, None, :]
    )
    out_norm = np.sqrt(out_first**2 + second[None, :] ** 2)
    in_norm = np.sqrt(first[None, :] ** 2 + in_second**2)
    phases = frequency * (inner + 0.5 * out_norm[:, None, :, None] * in_norm[None, :, None, :])
    factor = 1.0 / math.sqrt(128.0)
    real = np.transpose(factor * np.cos(phases), (1, 3, 0, 2))
    imag = np.transpose(factor * np.sin(phases), (1, 3, 0, 2))
    upper = np.concatenate([real, imag], axis=3)
    lower = np.concatenate([-imag, real], axis=3)
    full = np.concatenate([upper, lower], axis=1)
    return full.reshape(2 * WIDE, 2 * WIDE).astype(ml_dtypes.bfloat16)


def tables(scales):
    weights = np.tile(node_weights(), 2)
    angles = scales[..., None] * weights
    signs = np.repeat(np.array([-1.0, 1.0], np.float32), HALF)
    return jnp.cos(angles), jnp.sin(angles) * signs


def shuffle_matrix():
    rows = np.arange(256)
    found = np.zeros((256, 256), np.float32)
    found[rows, rows % 16 * 16 + rows // 16] = 1.0
    return found.astype(ml_dtypes.bfloat16)


def cos_sin(angles):
    turns = jnp.floor(angles * (2.0 / math.pi) + 0.5)
    rest = angles - turns * 1.5703125
    rest = rest - turns * 4.837512969970703125e-4
    rest = rest - turns * 7.54978995489188e-8
    square = rest * rest
    sine = 1.0 / 362880.0
    for factor in (-1.0 / 5040.0, 1.0 / 120.0, -1.0 / 6.0, 1.0):
        sine = sine * square + factor
    sine = sine * rest
    cosine = -1.0 / 3628800.0
    for factor in (1.0 / 40320.0, -1.0 / 720.0, 1.0 / 24.0, -0.5, 1.0):
        cosine = cosine * square + factor
    quarter = turns.astype(jnp.int32)
    odd = (quarter & 1) == 1
    first = jnp.where(odd, sine, cosine)
    second = jnp.where(odd, cosine, sine)
    first = jnp.where(((quarter + 1) & 2) == 2, -first, first)
    second = jnp.where((quarter & 2) == 2, -second, second)
    return first, second


def node_row():
    lanes = lax.broadcasted_iota(jnp.int32, (1, WIDE), 1) % HALF
    points = [math.cos((2 * a + 1) * math.pi / 16) ** 2 for a in range(4)]

    def square(at):
        near = jnp.minimum(at, 7 - at)
        value = jnp.full(near.shape, points[3], jnp.float32)
        for a in range(3):
            value = jnp.where(near == a, jnp.float32(points[a]), value)
        return value

    return square(lanes // 8) + square(lanes % 8)


def rotation(column):
    cosine, sine = cos_sin(column * node_row())
    lanes = lax.broadcasted_iota(jnp.int32, cosine.shape, 1)
    return cosine, jnp.where(lanes < HALF, -sine, sine)


def column_of(row, count):
    shape = (count, WIDE)
    here = lax.broadcasted_iota(jnp.int32, shape, 0) == lax.broadcasted_iota(jnp.int32, shape, 1)
    return jnp.sum(jnp.where(here, jnp.broadcast_to(row, shape), 0.0), axis=1, keepdims=True)


def swapped_columns(matrix):
    parts = [matrix[:, at : at + HALF] for at in (HALF, 0, 3 * HALF, 2 * HALF)]
    return jnp.concatenate(parts, axis=1)


def butterfly(load, store, count, apart, matrix, swapped, phase_of, group):
    lows = [i for i in range(count) if not i & apart]
    for turn, start in enumerate(range(0, len(lows), group)):
        picked = lows[start : start + group]
        left = jnp.concatenate([load(i) for i in picked], axis=0)
        right = jnp.concatenate([load(i + apart) for i in picked], axis=0)
        rows = left.shape[0] // len(picked)
        pair = jnp.concatenate([left, right], axis=1)
        both = jnp.dot(pair, matrix, preferred_element_type=jnp.float32)
        if turn % 2 == 0:
            other = jnp.dot(pair, swapped, preferred_element_type=jnp.float32)
        for place, low in enumerate(picked):
            for child in range(2):
                index = low + child * apart
                cosine, sine = phase_of(index)
                mine = slice(place * rows, (place + 1) * rows)
                own = slice(child * WIDE, (child + 1) * WIDE)
                value = both[mine, own]
                turned = other[mine, own] if turn % 2 == 0 else pltpu.roll(value, HALF, 1)
                store(index, (value * cosine + turned * sine).astype(jnp.bfloat16))


def swap_axes(load, store, outer, inner, shuffle):
    for low in range(0, outer, 2):
        for at in range(inner):
            sides = [load(low + side, at).reshape(256, WIDE) for side in range(2)]
            moved = jnp.dot(
                shuffle, jnp.concatenate(sides, axis=1), preferred_element_type=jnp.float32
            ).astype(jnp.bfloat16)
            for side in range(2):
                block = moved[:, side * WIDE : (side + 1) * WIDE]
                store(at, low + side, block.reshape(16, 16, WIDE))


def block_at(first, second):
    return (slice(first * 16, first * 16 + 16), slice(second * 16, second * 16 + 16))


BLOCK = 32
VMEM = pl.BlockSpec(memory_space=pltpu.VMEM)
FAR = pl.BlockSpec(memory_space=pltpu.HBM)
PARAMS = pltpu.CompilerParams(vmem_limit_bytes=32 << 20)


def source_kernel(a_ref, x_hbm, m_hbm, p_hbm, o_ref, x_ref, m_ref, p_ref, x_sems, m_sems, p_sem):
    rows, cols, _ = x_ref.shape
    levels = m_ref.shape[0]
    starts = range(0, cols, BLOCK)
    x_copies = [
        pltpu.make_async_copy(
            x_hbm.at[:, pl.ds(start, BLOCK)], x_ref.at[:, pl.ds(start, BLOCK)], x_sems.at[piece]
        )
        for piece, start in enumerate(starts)
    ]
    m_copies = [
        pltpu.make_async_copy(m_hbm.at[i], m_ref.at[i], m_sems.at[i]) for i in range(levels)
    ]
    p_copy = pltpu.make_async_copy(p_hbm, p_ref, p_sem)
    m_copies[0].start()
    for copy in x_copies:
        copy.start()
    for copy in m_copies[1:]:
        copy.start()
    p_copy.start()

    cosines, sines = rotation(column_of(a_ref[...], cols))
    for level in range(levels):
        m_copies[level].wait()
        matrix = m_ref[level]
        swapped = swapped_columns(matrix)
        for piece, start in enumerate(starts):
            if level == 0:
                x_copies[piece].wait()
            cosine, sine = cosines[start : start + BLOCK], sines[start : start + BLOCK]

            def store(index, value):
                x_ref[index, start : start + BLOCK, :] = value

            butterfly(
                lambda index: x_ref[index, start : start + BLOCK, :],
                store,
                rows,
                1 << level,
                matrix,
                swapped,
                lambda index: (cosine, sine),
                8,
            )

    def store_block(first, second, block):
        o_ref[block_at(first, second)] = block

    p_copy.wait()
    swap_axes(
        lambda first, second: x_ref[block_at(first, second)],
        store_block,
        rows // 16,
        cols // 16,
        p_ref[...],
    )


def source_levels(x, matrices, slowness, shuffle):
    rows, cols, _ = x.shape
    far = [pltpu.with_memory_space_constraint(v, pltpu.HBM) for v in (x, matrices, shuffle)]
    return pl.pallas_call(
        source_kernel,
        out_shape=jax.ShapeDtypeStruct((cols, rows, WIDE), x.dtype),
        in_specs=[VMEM, FAR, FAR, FAR],
        out_specs=VMEM,
        scratch_shapes=[
            pltpu.VMEM(x.shape, x.dtype),
            pltpu.VMEM(matrices.shape, x.dtype),
            pltpu.VMEM(shuffle.shape, x.dtype),
            pltpu.SemaphoreType.DMA((cols // BLOCK,)),
            pltpu.SemaphoreType.DMA((matrices.shape[0],)),
            pltpu.SemaphoreType.DMA,
        ],
        compiler_params=PARAMS,
    )(slowness[None, :], *far)


def middle_kernel(levels, rows, x_ref, m_ref, cs_ref, ss_ref, ct_ref, st_ref, o_ref):
    count, total, _ = x_ref.shape
    run = total // rows
    tgt_count = cs_ref.shape[0] // run
    for step, (apart, by_source) in enumerate(levels):
        source = x_ref if step == 0 else o_ref
        matrix = m_ref[step]
        swapped = swapped_columns(matrix)
        for col in range(run):
            own = slice(col * rows, (col + 1) * rows)

            def phase_of(index):
                if by_source:
                    at = index % tgt_count * run + col
                    return cs_ref[at : at + 1, :], ss_ref[at : at + 1, :]
                at = index // tgt_count
                return ct_ref[at], st_ref[at]

            def store(index, value):
                o_ref[index, own, :] = value

            butterfly(
                lambda index: source[index, own, :],
                store,
                count,
                apart,
                matrix,
                swapped,
                phase_of,
                8,
            )


def middle_levels(x, matrices, src_tables, tgt_tables, levels):
    rows = tgt_tables[0].shape[1]
    return pl.pallas_call(
        functools.partial(middle_kernel, levels, rows),
        out_shape=jax.ShapeDtypeStruct(x.shape, x.dtype),
        in_specs=[VMEM] * 6,
        out_specs=VMEM,
        compiler_params=PARAMS,
    )(x, matrices, *src_tables, *tgt_tables)


def target_kernel(m_ref, c_ref, s_ref, p_ref, x_ref, o_hbm, state_ref, o_ref, o_sems):
    cols, rows, _ = x_ref.shape
    levels = m_ref.shape[0]
    for level in range(levels):
        source = x_ref if level == 0 else state_ref
        matrix = m_ref[level]
        swapped = swapped_columns(matrix)
        for start in range(0, rows, 16):
            own = slice(start, start + 16)
            cosine, sine = c_ref[own, :], s_ref[own, :]

            def store(index, value):
                state_ref[index, own, :] = value

            butterfly(
                lambda index: source[index, own, :],
                store,
                cols,
                1 << (levels - 1 - level),
                matrix,
                swapped,
                lambda index: (cosine, sine),
                16,
            )

    copies = []
    for piece in range(rows // 16):
        own = pl.ds(piece * 16, 16)
        copies.append(pltpu.make_async_copy(o_ref.at[own], o_hbm.at[own], o_sems.at[piece]))

        def store_block(first, second, block):
            o_ref[block_at(piece, second)] = block

        swap_axes(
            lambda first, second: state_ref[block_at(first, piece)],
            store_block,
            cols // 16,
            1,
            p_ref[...],
        )
        copies[-1].start()
    for copy in copies:
        copy.wait()


def target_levels(x, matrices, angles, shuffle):
    cols, rows, _ = x.shape
    shape = (rows, cols, WIDE)
    return pl.pallas_call(
        target_kernel,
        out_shape=jax.ShapeDtypeStruct(shape, x.dtype),
        in_specs=[VMEM] * 5,
        out_specs=FAR,
        scratch_shapes=[
            pltpu.VMEM(x.shape, x.dtype),
            pltpu.VMEM(shape, x.dtype),
            pltpu.SemaphoreType.DMA((rows // 16,)),
        ],
        compiler_params=PARAMS,
    )(matrices, *angles, shuffle, x)


def gathered(values, axis):
    count = lax.axis_size(axis)
    place = lax.axis_index(axis)
    values = values[None]
    apart = 1
    while apart < count:
        other = lax.ppermute(values, axis, [(i, i ^ apart) for i in range(count)])
        mine_first = (place & apart) == 0
        values = jnp.concatenate(
            [jnp.where(mine_first, values, other), jnp.where(mine_first, other, values)]
        )
        apart *= 2
    return values


def local(box_weights, slowness, dip_field):
    rows, cols, _ = box_weights.shape
    src_count = lax.axis_size("src")
    tgt_count = lax.axis_size("tgt")
    devices = src_count * tgt_count
    row_bits, col_bits = rows.bit_length() - 1, cols.bit_length() - 1
    src_bits, tgt_bits = src_count.bit_length() - 1, tgt_count.bit_length() - 1
    first_target = row_bits + src_bits
    total = first_target + tgt_bits + col_bits
    matrices = [level_matrix(number) for number in range(total)]

    def matrices_of(low, high):
        return jnp.asarray(np.stack(matrices[low:high]))

    run = cols // devices
    place = lax.axis_index("src") * tgt_count + lax.axis_index("tgt")
    shuffle = jnp.asarray(shuffle_matrix())

    state = source_levels(box_weights, matrices_of(0, row_bits), slowness, shuffle)

    state, slowness, dip_field = lax.optimization_barrier((state, slowness, dip_field))
    all_dip = gathered(dip_field, "src")
    all_slowness = gathered(slowness, "tgt")
    run_slowness = lax.dynamic_slice_in_dim(all_slowness, place * run, run, 1)

    state = state.reshape(devices, run * rows, WIDE)
    state = lax.all_to_all(state, ("src", "tgt"), 0, 0, tiled=True)
    levels = [(tgt_count << bit, True) for bit in range(src_bits)]
    levels += [(1 << bit, False) for bit in reversed(range(tgt_bits))]
    state = middle_levels(
        state,
        matrices_of(row_bits, first_target + tgt_bits),
        tables(run_slowness.reshape(-1)),
        tables(all_dip),
        levels,
    )
    state = lax.all_to_all(state, ("src", "tgt"), 0, 0, tiled=True)

    return target_levels(
        state.reshape(cols, rows, WIDE),
        matrices_of(first_target + tgt_bits, total),
        tables(dip_field),
        shuffle,
    )


def solution(mesh):
    in_specs = (P("src", "tgt", None), P("tgt"), P("src"))
    out_specs = P("src", "tgt", None)
    return jax.shard_map(local, mesh=mesh, in_specs=in_specs, out_specs=out_specs, check_vma=False)
```

```python
import functools
import math

import jax
import jax.numpy as jnp
import ml_dtypes
import numpy as np
from jax import lax
from jax.experimental import pallas as pl
from jax.experimental.pallas import tpu as pltpu
from jax.sharding import PartitionSpec as P

HALF = 64
WIDE = 128


def nodes():
    points = np.cos((2.0 * np.arange(8) + 1.0) * (math.pi / 16.0))
    return np.repeat(points, 8), np.tile(points, 8)


def node_weights():
    first, second = nodes()
    return (first * first + second * second).astype(np.float32)


def level_matrix(number):
    first, second = nodes()
    frequency = 9.0 + 3.0 * (number % 5)
    shifts = np.array([-0.5, 0.5])
    out_first = first[None, :] + shifts[:, None]
    in_second = second[None, :] + shifts[:, None]
    inner = (
        out_first[:, None, :, None] * first[None, None, None, :]
        + second[None, None, :, None] * in_second[None, :, None, :]
    )
    out_norm = np.sqrt(out_first**2 + second[None, :] ** 2)
    in_norm = np.sqrt(first[None, :] ** 2 + in_second**2)
    phases = frequency * (inner + 0.5 * out_norm[:, None, :, None] * in_norm[None, :, None, :])
    factor = 1.0 / math.sqrt(128.0)
    real = np.transpose(factor * np.cos(phases), (1, 3, 0, 2))
    imag = np.transpose(factor * np.sin(phases), (1, 3, 0, 2))
    upper = np.concatenate([real, imag], axis=3)
    return upper.reshape(WIDE, 2 * WIDE).astype(ml_dtypes.bfloat16)


def tables(scales):
    weights = np.tile(node_weights(), 2)
    angles = scales[..., None] * weights
    signs = np.repeat(np.array([-1.0, 1.0], np.float32), HALF)
    return jnp.cos(angles), jnp.sin(angles) * signs


def shuffle_matrix():
    to = lax.broadcasted_iota(jnp.int32, (256, 256), 0)
    source = lax.broadcasted_iota(jnp.int32, (256, 256), 1)
    here = source == (to & 15) * 16 + (to >> 4)
    return jnp.where(here, 1.0, 0.0).astype(jnp.bfloat16)


def cos_sin(angles):
    turns = jnp.floor(angles * (2.0 / math.pi) + 0.5)
    rest = angles - turns * 1.5703125
    rest = rest - turns * 4.837512969970703125e-4
    rest = rest - turns * 7.54978995489188e-8
    square = rest * rest
    sine = 1.0 / 362880.0
    for factor in (-1.0 / 5040.0, 1.0 / 120.0, -1.0 / 6.0, 1.0):
        sine = sine * square + factor
    sine = sine * rest
    cosine = -1.0 / 3628800.0
    for factor in (1.0 / 40320.0, -1.0 / 720.0, 1.0 / 24.0, -0.5, 1.0):
        cosine = cosine * square + factor
    quarter = turns.astype(jnp.int32)
    odd = (quarter & 1) == 1
    first = jnp.where(odd, sine, cosine)
    second = jnp.where(odd, cosine, sine)
    first = jnp.where(((quarter + 1) & 2) == 2, -first, first)
    second = jnp.where((quarter & 2) == 2, -second, second)
    return first, second


def node_row():
    lanes = lax.broadcasted_iota(jnp.int32, (1, WIDE), 1) % HALF
    points = [math.cos((2 * a + 1) * math.pi / 16) ** 2 for a in range(4)]

    def square(at):
        near = jnp.minimum(at, 7 - at)
        value = jnp.full(near.shape, points[3], jnp.float32)
        for a in range(3):
            value = jnp.where(near == a, jnp.float32(points[a]), value)
        return value

    return square(lanes // 8) + square(lanes % 8)


def rotation(column):
    cosine, sine = cos_sin(column * node_row())
    lanes = lax.broadcasted_iota(jnp.int32, cosine.shape, 1)
    return cosine, jnp.where(lanes < HALF, -sine, sine)


def column_of(row, count):
    shape = (count, WIDE)
    here = lax.broadcasted_iota(jnp.int32, shape, 0) == lax.broadcasted_iota(jnp.int32, shape, 1)
    return jnp.sum(jnp.where(here, jnp.broadcast_to(row, shape), 0.0), axis=1, keepdims=True)


def whole_matrix(upper):
    parts = [upper[:, at : at + HALF] for at in (HALF, 0, 3 * HALF, 2 * HALF)]
    traded = jnp.concatenate(parts, axis=1)
    im_lane = (lax.broadcasted_iota(jnp.int32, upper.shape, 1) & HALF) != 0
    below = jnp.where(im_lane, traded, -traded)
    traded_below = jnp.where(im_lane, -upper, upper)

    def stacked(first, second):
        children = (slice(0, HALF), slice(HALF, WIDE))
        return jnp.concatenate([half[rows] for rows in children for half in (first, second)], axis=0)

    return stacked(upper, below), stacked(traded, traded_below)


def butterfly(load, store, count, apart, matrix, swapped, phase_of, group, turn=0):
    lows = [i for i in range(count) if not i & apart]
    for start in range(0, len(lows), group):
        picked = lows[start : start + group]
        left = jnp.concatenate([load(i) for i in picked], axis=0)
        right = jnp.concatenate([load(i + apart) for i in picked], axis=0)
        rows = left.shape[0] // len(picked)
        pair = jnp.concatenate([left, right], axis=1)
        both = jnp.dot(pair, matrix, preferred_element_type=jnp.float32)
        if turn % 2 == 0:
            other = jnp.dot(pair, swapped, preferred_element_type=jnp.float32)
        for place, low in enumerate(picked):
            for child in range(2):
                index = low + child * apart
                cosine, sine = phase_of(index)
                mine = slice(place * rows, (place + 1) * rows)
                own = slice(child * WIDE, (child + 1) * WIDE)
                value = both[mine, own]
                turned = other[mine, own] if turn % 2 == 0 else pltpu.roll(value, HALF, 1)
                store(index, (value * cosine + turned * sine).astype(jnp.bfloat16))
        turn += 1


def swap_axes(load, store, outer, inner, shuffle):
    for low in range(0, outer, 2):
        for at in range(inner):
            sides = [load(low + side, at).reshape(256, WIDE) for side in range(2)]
            moved = jnp.dot(
                shuffle, jnp.concatenate(sides, axis=1), preferred_element_type=jnp.float32
            ).astype(jnp.bfloat16)
            for side in range(2):
                block = moved[:, side * WIDE : (side + 1) * WIDE]
                store(at, low + side, block.reshape(16, 16, WIDE))


def block_at(first, second):
    return (slice(first * 16, first * 16 + 16), slice(second * 16, second * 16 + 16))


PIECE = 8
VMEM = pl.BlockSpec(memory_space=pltpu.VMEM)
FAR = pl.BlockSpec(memory_space=pltpu.HBM)
PARAMS = pltpu.CompilerParams(vmem_limit_bytes=32 << 20)


def source_kernel(a_hbm, x_hbm, m_hbm, o_ref, a_ref, x_ref, m_ref, w_ref, a_sem, x_sems, m_sems):
    rows, cols, _ = x_ref.shape
    levels = m_ref.shape[0]
    low_levels = PIECE.bit_length() - 1
    a_copy = pltpu.make_async_copy(a_hbm, a_ref, a_sem)
    x_copies = []
    for piece in range(rows // PIECE):
        own = pl.ds(piece * PIECE, PIECE)
        x_copies.append(pltpu.make_async_copy(x_hbm.at[own], x_ref.at[own], x_sems.at[piece]))
    m_copies = [
        pltpu.make_async_copy(m_hbm.at[i], m_ref.at[i], m_sems.at[i]) for i in range(levels)
    ]
    first = [a_copy, m_copies[0], x_copies[0], *m_copies[1:low_levels], *x_copies[1:]]
    for copy in first + m_copies[low_levels:]:
        copy.start()

    def ready(level):
        m_copies[level].wait()
        w_ref[2 * level], w_ref[2 * level + 1] = whole_matrix(m_ref[level])

    def level_on(level, base, count, begin, block, group, turn):
        own = slice(begin, begin + block)

        def store(index, value):
            x_ref[base + index, own, :] = value

        butterfly(
            lambda index: x_ref[base + index, own, :],
            store,
            count,
            1 << level,
            w_ref[2 * level],
            w_ref[2 * level + 1],
            lambda index: (cosines[own], sines[own]),
            group,
            turn,
        )

    a_copy.wait()
    cosines, sines = rotation(column_of(a_ref[...], cols))
    for piece in range(rows // PIECE):
        x_copies[piece].wait()
        for level in range(low_levels):
            if piece == 0:
                ready(level)
            for turn, begin in enumerate(range(0, cols, 64)):
                level_on(level, piece * PIECE, PIECE, begin, 64, PIECE // 2, turn)
    for level in range(low_levels, levels):
        ready(level)
        for begin in range(0, cols, 32):
            level_on(level, 0, rows, begin, 32, 8, 0)

    def store_block(first, second, block):
        o_ref[block_at(first, second)] = block

    swap_axes(
        lambda first, second: x_ref[block_at(first, second)],
        store_block,
        rows // 16,
        cols // 16,
        shuffle_matrix(),
    )


def source_levels(x, matrices, slowness):
    rows, cols, _ = x.shape
    levels = matrices.shape[0]
    far = [pltpu.with_memory_space_constraint(v, pltpu.HBM) for v in (slowness[None, :], x, matrices)]
    return pl.pallas_call(
        source_kernel,
        out_shape=jax.ShapeDtypeStruct((cols, rows, WIDE), x.dtype),
        in_specs=[FAR, FAR, FAR],
        out_specs=VMEM,
        scratch_shapes=[
            pltpu.VMEM((1, cols), jnp.float32),
            pltpu.VMEM(x.shape, x.dtype),
            pltpu.VMEM(matrices.shape, x.dtype),
            pltpu.VMEM((2 * levels, 2 * WIDE, 2 * WIDE), x.dtype),
            pltpu.SemaphoreType.DMA,
            pltpu.SemaphoreType.DMA((rows // PIECE,)),
            pltpu.SemaphoreType.DMA((levels,)),
        ],
        compiler_params=PARAMS,
    )(*far)


def middle_kernel(levels, spots, rows, x_ref, m_ref, cs_ref, ss_ref, ct_ref, st_ref, o_ref):
    count, total, _ = x_ref.shape
    run = total // rows
    tgt_count = cs_ref.shape[0] // run
    for step, (apart, by_source) in enumerate(levels):
        source = x_ref if step == 0 else o_ref
        matrix, swapped = whole_matrix(m_ref[step])
        for col in range(run):
            own = slice(col * rows, (col + 1) * rows)

            def phase_of(index):
                if by_source:
                    at = index % tgt_count * run + col
                    return cs_ref[at : at + 1, :], ss_ref[at : at + 1, :]
                at = index // tgt_count
                return ct_ref[at], st_ref[at]

            def store(index, value):
                o_ref[spots[index], own, :] = value

            butterfly(
                lambda index: source[spots[index], own, :],
                store,
                count,
                apart,
                matrix,
                swapped,
                phase_of,
                8,
            )


def middle_levels(x, matrices, src_tables, tgt_tables, levels, spots):
    rows = tgt_tables[0].shape[1]
    return pl.pallas_call(
        functools.partial(middle_kernel, levels, spots, rows),
        out_shape=jax.ShapeDtypeStruct(x.shape, x.dtype),
        in_specs=[VMEM] * 6,
        out_specs=VMEM,
        compiler_params=PARAMS,
    )(x, matrices, *src_tables, *tgt_tables)


def target_kernel(m_ref, c_ref, s_ref, x_ref, o_hbm, state_ref, o_ref, o_sems):
    cols, rows, _ = x_ref.shape
    levels = m_ref.shape[0]
    for level in range(levels):
        source = x_ref if level == 0 else state_ref
        matrix, swapped = whole_matrix(m_ref[level])
        for start in range(0, rows, 16):
            own = slice(start, start + 16)
            cosine, sine = c_ref[own, :], s_ref[own, :]

            def store(index, value):
                state_ref[index, own, :] = value

            butterfly(
                lambda index: source[index, own, :],
                store,
                cols,
                1 << (levels - 1 - level),
                matrix,
                swapped,
                lambda index: (cosine, sine),
                16,
            )

    shuffle = shuffle_matrix()
    copies = []
    for piece in range(rows // 16):
        own = pl.ds(piece * 16, 16)
        copies.append(pltpu.make_async_copy(o_ref.at[own], o_hbm.at[own], o_sems.at[piece]))

        def store_block(first, second, block):
            o_ref[block_at(piece, second)] = block

        swap_axes(
            lambda first, second: state_ref[block_at(first, piece)],
            store_block,
            cols // 16,
            1,
            shuffle,
        )
        copies[-1].start()
    for copy in copies:
        copy.wait()


def target_levels(x, matrices, angles):
    cols, rows, _ = x.shape
    shape = (rows, cols, WIDE)
    return pl.pallas_call(
        target_kernel,
        out_shape=jax.ShapeDtypeStruct(shape, x.dtype),
        in_specs=[VMEM] * 4,
        out_specs=FAR,
        scratch_shapes=[
            pltpu.VMEM(x.shape, x.dtype),
            pltpu.VMEM(shape, x.dtype),
            pltpu.SemaphoreType.DMA((rows // 16,)),
        ],
        compiler_params=PARAMS,
    )(matrices, *angles, x)


def gathered(values, axis):
    count = lax.axis_size(axis)
    place = lax.axis_index(axis)
    values = values[None]
    apart = 1
    while apart < count:
        other = lax.ppermute(values, axis, [(i, i ^ apart) for i in range(count)])
        mine_first = (place & apart) == 0
        values = jnp.concatenate(
            [jnp.where(mine_first, values, other), jnp.where(mine_first, other, values)]
        )
        apart *= 2
    return values


def local(box_weights, slowness, dip_field):
    rows, cols, _ = box_weights.shape
    src_count = lax.axis_size("src")
    tgt_count = lax.axis_size("tgt")
    devices = src_count * tgt_count
    row_bits, col_bits = rows.bit_length() - 1, cols.bit_length() - 1
    src_bits, tgt_bits = src_count.bit_length() - 1, tgt_count.bit_length() - 1
    first_target = row_bits + src_bits
    total = first_target + tgt_bits + col_bits
    matrices = [level_matrix(number) for number in range(total)]

    def matrices_of(low, high):
        return jnp.asarray(np.stack(matrices[low:high]))

    run = cols // devices
    pairs = sorted(range(tgt_count // 2), key=lambda at: abs(2 * at + 1 - tgt_count // 2))
    tgt_order = [2 * at + side for at in pairs for side in range(2)]
    order = [src * tgt_count + tgt for src in range(src_count) for tgt in tgt_order]
    spots = [order.index(device) for device in range(devices)]
    place = jnp.asarray(spots)[lax.axis_index("src") * tgt_count + lax.axis_index("tgt")]

    def traded(state):
        return lax.all_to_all(
            state, ("src", "tgt"), 0, 0, axis_index_groups=[order], tiled=True
        )

    state = source_levels(box_weights, matrices_of(0, row_bits), slowness)

    state, slowness, dip_field = lax.optimization_barrier((state, slowness, dip_field))
    all_dip = gathered(dip_field, "src")
    all_slowness = gathered(slowness, "tgt")
    run_slowness = lax.dynamic_slice_in_dim(all_slowness, place * run, run, 1)

    state = state.reshape(devices, run * rows, WIDE)
    state = traded(state)
    levels = [(tgt_count << bit, True) for bit in range(src_bits)]
    levels += [(1 << bit, False) for bit in reversed(range(tgt_bits))]
    state = middle_levels(
        state,
        matrices_of(row_bits, first_target + tgt_bits),
        tables(run_slowness.reshape(-1)),
        tables(all_dip),
        levels,
        spots,
    )
    state = traded(state)

    return target_levels(
        state.reshape(cols, rows, WIDE),
        matrices_of(first_target + tgt_bits, total),
        tables(dip_field),
    )


def solution(mesh):
    in_specs = (P("src", "tgt", None), P("tgt"), P("src"))
    out_specs = P("src", "tgt", None)
    return jax.shard_map(local, mesh=mesh, in_specs=in_specs, out_specs=out_specs, check_vma=False)
```

```python
import functools
import math

import jax
import jax.numpy as jnp
import ml_dtypes
import numpy as np
from jax import lax
from jax.experimental import pallas as pl
from jax.experimental.pallas import tpu as pltpu
from jax.sharding import PartitionSpec as P

HALF = 64
WIDE = 128


def nodes():
    points = np.cos((2.0 * np.arange(8) + 1.0) * (math.pi / 16.0))
    return np.repeat(points, 8), np.tile(points, 8)


def node_weights():
    first, second = nodes()
    return (first * first + second * second).astype(np.float32)


def level_matrix(number):
    first, second = nodes()
    frequency = 9.0 + 3.0 * (number % 5)
    shifts = np.array([-0.5, 0.5])
    out_first = first[None, :] + shifts[:, None]
    in_second = second[None, :] + shifts[:, None]
    inner = (
        out_first[:, None, :, None] * first[None, None, None, :]
        + second[None, None, :, None] * in_second[None, :, None, :]
    )
    out_norm = np.sqrt(out_first**2 + second[None, :] ** 2)
    in_norm = np.sqrt(first[None, :] ** 2 + in_second**2)
    phases = frequency * (inner + 0.5 * out_norm[:, None, :, None] * in_norm[None, :, None, :])
    factor = 1.0 / math.sqrt(128.0)
    real = np.transpose(factor * np.cos(phases), (1, 3, 0, 2))
    imag = np.transpose(factor * np.sin(phases), (1, 3, 0, 2))
    upper = np.concatenate([real, imag], axis=3)
    return upper.reshape(WIDE, 2 * WIDE).astype(ml_dtypes.bfloat16)


def tables(scales):
    weights = np.tile(node_weights(), 2)
    angles = scales[..., None] * weights
    signs = np.repeat(np.array([-1.0, 1.0], np.float32), HALF)
    return jnp.cos(angles), jnp.sin(angles) * signs


def shuffle_matrix():
    to = lax.broadcasted_iota(jnp.int32, (256, 256), 0)
    source = lax.broadcasted_iota(jnp.int32, (256, 256), 1)
    here = source == (to & 15) * 16 + (to >> 4)
    return jnp.where(here, 1.0, 0.0).astype(jnp.bfloat16)


def cos_sin(angles):
    turns = jnp.floor(angles * (2.0 / math.pi) + 0.5)
    rest = angles - turns * 1.5703125
    rest = rest - turns * 4.837512969970703125e-4
    rest = rest - turns * 7.54978995489188e-8
    square = rest * rest
    sine = 1.0 / 362880.0
    for factor in (-1.0 / 5040.0, 1.0 / 120.0, -1.0 / 6.0, 1.0):
        sine = sine * square + factor
    sine = sine * rest
    cosine = -1.0 / 3628800.0
    for factor in (1.0 / 40320.0, -1.0 / 720.0, 1.0 / 24.0, -0.5, 1.0):
        cosine = cosine * square + factor
    quarter = turns.astype(jnp.int32)
    odd = (quarter & 1) == 1
    first = jnp.where(odd, sine, cosine)
    second = jnp.where(odd, cosine, sine)
    first = jnp.where(((quarter + 1) & 2) == 2, -first, first)
    second = jnp.where((quarter & 2) == 2, -second, second)
    return first, second


def node_row():
    lanes = lax.broadcasted_iota(jnp.int32, (1, WIDE), 1) % HALF
    points = [math.cos((2 * a + 1) * math.pi / 16) ** 2 for a in range(4)]

    def square(at):
        near = jnp.minimum(at, 7 - at)
        value = jnp.full(near.shape, points[3], jnp.float32)
        for a in range(3):
            value = jnp.where(near == a, jnp.float32(points[a]), value)
        return value

    return square(lanes // 8) + square(lanes % 8)


def rotation(column):
    cosine, sine = cos_sin(column * node_row())
    lanes = lax.broadcasted_iota(jnp.int32, cosine.shape, 1)
    return cosine, jnp.where(lanes < HALF, -sine, sine)


def column_of(row, count):
    shape = (count, WIDE)
    here = lax.broadcasted_iota(jnp.int32, shape, 0) == lax.broadcasted_iota(jnp.int32, shape, 1)
    return jnp.sum(jnp.where(here, jnp.broadcast_to(row, shape), 0.0), axis=1, keepdims=True)


def whole_matrix(upper):
    parts = [upper[:, at : at + HALF] for at in (HALF, 0, 3 * HALF, 2 * HALF)]
    traded = jnp.concatenate(parts, axis=1)
    im_lane = (lax.broadcasted_iota(jnp.int32, upper.shape, 1) & HALF) != 0
    below = jnp.where(im_lane, traded, -traded)
    traded_below = jnp.where(im_lane, -upper, upper)

    def stacked(first, second):
        children = (slice(0, HALF), slice(HALF, WIDE))
        return jnp.concatenate([half[rows] for rows in children for half in (first, second)], axis=0)

    return stacked(upper, below), stacked(traded, traded_below)


def butterfly(load, store, count, apart, matrix, swapped, phase_of, group, turn=0):
    lows = [i for i in range(count) if not i & apart]
    for start in range(0, len(lows), group):
        picked = lows[start : start + group]
        left = jnp.concatenate([load(i) for i in picked], axis=0)
        right = jnp.concatenate([load(i + apart) for i in picked], axis=0)
        rows = left.shape[0] // len(picked)
        pair = jnp.concatenate([left, right], axis=1)
        both = jnp.dot(pair, matrix, preferred_element_type=jnp.float32)
        if turn % 2 == 0:
            other = jnp.dot(pair, swapped, preferred_element_type=jnp.float32)
        for place, low in enumerate(picked):
            for child in range(2):
                index = low + child * apart
                cosine, sine = phase_of(index)
                mine = slice(place * rows, (place + 1) * rows)
                own = slice(child * WIDE, (child + 1) * WIDE)
                value = both[mine, own]
                turned = other[mine, own] if turn % 2 == 0 else pltpu.roll(value, HALF, 1)
                store(index, (value * cosine + turned * sine).astype(jnp.bfloat16))
        turn += 1


def swap_axes(load, store, outer, inner, shuffle):
    for low in range(0, outer, 2):
        for at in range(inner):
            sides = [load(low + side, at).reshape(256, WIDE) for side in range(2)]
            moved = jnp.dot(
                shuffle, jnp.concatenate(sides, axis=1), preferred_element_type=jnp.float32
            ).astype(jnp.bfloat16)
            for side in range(2):
                block = moved[:, side * WIDE : (side + 1) * WIDE]
                store(at, low + side, block.reshape(16, 16, WIDE))


def block_at(first, second):
    return (slice(first * 16, first * 16 + 16), slice(second * 16, second * 16 + 16))


PIECE = 64
BLOCK = 32
VMEM = pl.BlockSpec(memory_space=pltpu.VMEM)
FAR = pl.BlockSpec(memory_space=pltpu.HBM)
PARAMS = pltpu.CompilerParams(vmem_limit_bytes=32 << 20)


def source_kernel(a_hbm, x_hbm, m_hbm, o_ref, a_ref, x_ref, m_ref, w_ref, a_sem, x_sems, m_sems):
    rows, cols, _ = x_ref.shape
    levels = m_ref.shape[0]
    a_copy = pltpu.make_async_copy(a_hbm, a_ref, a_sem)
    x_copies = []
    for piece in range(cols // PIECE):
        own = (slice(None), pl.ds(piece * PIECE, PIECE))
        x_copies.append(pltpu.make_async_copy(x_hbm.at[own], x_ref.at[own], x_sems.at[piece]))
    m_copies = [
        pltpu.make_async_copy(m_hbm.at[i], m_ref.at[i], m_sems.at[i]) for i in range(levels)
    ]
    for copy in (a_copy, m_copies[0], *x_copies, *m_copies[1:]):
        copy.start()

    def expand(level):
        w_ref[2 * level], w_ref[2 * level + 1] = whole_matrix(m_ref[level])

    def level_on(level, begin):
        own = slice(begin, begin + BLOCK)

        def store(index, value):
            x_ref[index, own, :] = value

        butterfly(
            lambda index: x_ref[index, own, :],
            store,
            rows,
            1 << level,
            w_ref[2 * level],
            w_ref[2 * level + 1],
            lambda index: (cosines[own], sines[own]),
            8,
        )

    a_copy.wait()
    cosines, sines = rotation(column_of(a_ref[...], cols))
    m_copies[0].wait()
    expand(0)
    for piece, copy in enumerate(x_copies):
        copy.wait()
        for begin in range(piece * PIECE, (piece + 1) * PIECE, BLOCK):
            level_on(0, begin)
    for copy in m_copies[1:]:
        copy.wait()
    for level in range(1, levels):
        expand(level)
    for level in range(1, levels):
        for begin in range(0, cols, BLOCK):
            level_on(level, begin)

    def store_block(first, second, block):
        o_ref[block_at(first, second)] = block

    swap_axes(
        lambda first, second: x_ref[block_at(first, second)],
        store_block,
        rows // 16,
        cols // 16,
        shuffle_matrix(),
    )


def source_levels(x, matrices, slowness):
    rows, cols, _ = x.shape
    levels = matrices.shape[0]
    operands = (slowness[None, :], x, matrices)
    far = [pltpu.with_memory_space_constraint(value, pltpu.HBM) for value in operands]
    return pl.pallas_call(
        source_kernel,
        out_shape=jax.ShapeDtypeStruct((cols, rows, WIDE), x.dtype),
        in_specs=[FAR, FAR, FAR],
        out_specs=VMEM,
        scratch_shapes=[
            pltpu.VMEM((1, cols), jnp.float32),
            pltpu.VMEM(x.shape, x.dtype),
            pltpu.VMEM(matrices.shape, x.dtype),
            pltpu.VMEM((2 * levels, 2 * WIDE, 2 * WIDE), x.dtype),
            pltpu.SemaphoreType.DMA,
            pltpu.SemaphoreType.DMA((cols // PIECE,)),
            pltpu.SemaphoreType.DMA((levels,)),
        ],
        compiler_params=PARAMS,
    )(*far)


def middle_kernel(levels, rows, x_ref, m_ref, cs_ref, ss_ref, ct_ref, st_ref, o_ref):
    count, total, _ = x_ref.shape
    run = total // rows
    tgt_count = cs_ref.shape[0] // run
    for step, (apart, by_source) in enumerate(levels):
        source = x_ref if step == 0 else o_ref
        matrix, swapped = whole_matrix(m_ref[step])
        for col in range(run):
            own = slice(col * rows, (col + 1) * rows)

            def phase_of(index):
                if by_source:
                    at = index % tgt_count * run + col
                    return cs_ref[at : at + 1, :], ss_ref[at : at + 1, :]
                at = index // tgt_count
                return ct_ref[at], st_ref[at]

            def store(index, value):
                o_ref[index, own, :] = value

            butterfly(
                lambda index: source[index, own, :],
                store,
                count,
                apart,
                matrix,
                swapped,
                phase_of,
                8,
            )


def middle_levels(x, matrices, src_tables, tgt_tables, levels):
    rows = tgt_tables[0].shape[1]
    return pl.pallas_call(
        functools.partial(middle_kernel, levels, rows),
        out_shape=jax.ShapeDtypeStruct(x.shape, x.dtype),
        in_specs=[VMEM] * 6,
        out_specs=VMEM,
        compiler_params=PARAMS,
    )(x, matrices, *src_tables, *tgt_tables)


def target_kernel(m_ref, c_ref, s_ref, x_ref, o_hbm, state_ref, o_ref, o_sems):
    cols, rows, _ = x_ref.shape
    levels = m_ref.shape[0]

    def level_on(level, start, weights):
        source = x_ref if level == 0 else state_ref
        own = slice(start, start + 16)
        cosine, sine = c_ref[own, :], s_ref[own, :]

        def store(index, value):
            state_ref[index, own, :] = value

        butterfly(
            lambda index: source[index, own, :],
            store,
            cols,
            1 << (levels - 1 - level),
            *weights,
            lambda index: (cosine, sine),
            16,
        )

    for level in range(levels - 1):
        weights = whole_matrix(m_ref[level])
        for start in range(0, rows, 16):
            level_on(level, start, weights)

    weights = whole_matrix(m_ref[levels - 1])
    shuffle = shuffle_matrix()
    copies = []
    for piece in range(rows // 16):
        level_on(levels - 1, piece * 16, weights)
        own = pl.ds(piece * 16, 16)
        copies.append(pltpu.make_async_copy(o_ref.at[own], o_hbm.at[own], o_sems.at[piece]))

        def store_block(first, second, block):
            o_ref[block_at(piece, second)] = block

        swap_axes(
            lambda first, second: state_ref[block_at(first, piece)],
            store_block,
            cols // 16,
            1,
            shuffle,
        )
        copies[-1].start()
    for copy in copies:
        copy.wait()


def target_levels(x, matrices, angles):
    cols, rows, _ = x.shape
    shape = (rows, cols, WIDE)
    return pl.pallas_call(
        target_kernel,
        out_shape=jax.ShapeDtypeStruct(shape, x.dtype),
        in_specs=[VMEM] * 4,
        out_specs=FAR,
        scratch_shapes=[
            pltpu.VMEM(x.shape, x.dtype),
            pltpu.VMEM(shape, x.dtype),
            pltpu.SemaphoreType.DMA((rows // 16,)),
        ],
        compiler_params=PARAMS,
    )(matrices, *angles, x)


def gathered(values, axis):
    count = lax.axis_size(axis)
    place = lax.axis_index(axis)
    values = values[None]
    apart = 1
    while apart < count:
        other = lax.ppermute(values, axis, [(i, i ^ apart) for i in range(count)])
        mine_first = (place & apart) == 0
        values = jnp.concatenate(
            [jnp.where(mine_first, values, other), jnp.where(mine_first, other, values)]
        )
        apart *= 2
    return values


def local(box_weights, slowness, dip_field):
    rows, cols, _ = box_weights.shape
    src_count = lax.axis_size("src")
    tgt_count = lax.axis_size("tgt")
    devices = src_count * tgt_count
    row_bits, col_bits = rows.bit_length() - 1, cols.bit_length() - 1
    src_bits, tgt_bits = src_count.bit_length() - 1, tgt_count.bit_length() - 1
    first_target = row_bits + src_bits
    total = first_target + tgt_bits + col_bits
    matrices = [level_matrix(number) for number in range(total)]

    def matrices_of(low, high):
        return jnp.asarray(np.stack(matrices[low:high]))

    run = cols // devices
    place = lax.axis_index("src") * tgt_count + lax.axis_index("tgt")

    def traded(state):
        return lax.all_to_all(state, ("src", "tgt"), 0, 0, tiled=True)

    state = source_levels(box_weights, matrices_of(0, row_bits), slowness)

    state, slowness, dip_field = lax.optimization_barrier((state, slowness, dip_field))
    all_dip = gathered(dip_field, "src")
    all_slowness = gathered(slowness, "tgt")
    run_slowness = lax.dynamic_slice_in_dim(all_slowness, place * run, run, 1)

    state = state.reshape(devices, run * rows, WIDE)
    state = traded(state)
    levels = [(tgt_count << bit, True) for bit in range(src_bits)]
    levels += [(1 << bit, False) for bit in reversed(range(tgt_bits))]
    state = middle_levels(
        state,
        matrices_of(row_bits, first_target + tgt_bits),
        tables(run_slowness.reshape(-1)),
        tables(all_dip),
        levels,
    )
    state = traded(state)

    return target_levels(
        state.reshape(cols, rows, WIDE),
        matrices_of(first_target + tgt_bits, total),
        tables(dip_field),
    )


def solution(mesh):
    in_specs = (P("src", "tgt", None), P("tgt"), P("src"))
    out_specs = P("src", "tgt", None)
    return jax.shard_map(local, mesh=mesh, in_specs=in_specs, out_specs=out_specs, check_vma=False)
```

```python
import functools
import math

import jax
import jax.numpy as jnp
import ml_dtypes
import numpy as np
from jax import lax
from jax.experimental import pallas as pl
from jax.experimental.pallas import tpu as pltpu
from jax.sharding import PartitionSpec as P

HALF = 64
WIDE = 128


def nodes():
    points = np.cos((2.0 * np.arange(8) + 1.0) * (math.pi / 16.0))
    return np.repeat(points, 8), np.tile(points, 8)


def node_weights():
    first, second = nodes()
    return (first * first + second * second).astype(np.float32)


def level_matrix(number):
    first, second = nodes()
    frequency = 9.0 + 3.0 * (number % 5)
    shifts = np.array([-0.5, 0.5])
    out_first = first[None, :] + shifts[:, None]
    in_second = second[None, :] + shifts[:, None]
    inner = (
        out_first[:, None, :, None] * first[None, None, None, :]
        + second[None, None, :, None] * in_second[None, :, None, :]
    )
    out_norm = np.sqrt(out_first**2 + second[None, :] ** 2)
    in_norm = np.sqrt(first[None, :] ** 2 + in_second**2)
    phases = frequency * (inner + 0.5 * out_norm[:, None, :, None] * in_norm[None, :, None, :])
    factor = 1.0 / math.sqrt(128.0)
    real = np.transpose(factor * np.cos(phases), (1, 3, 0, 2))
    imag = np.transpose(factor * np.sin(phases), (1, 3, 0, 2))
    upper = np.concatenate([real, imag], axis=3)
    return upper.reshape(WIDE, 2 * WIDE).astype(ml_dtypes.bfloat16)


def tables(scales):
    weights = np.tile(node_weights(), 2)
    angles = scales[..., None] * weights
    signs = np.repeat(np.array([-1.0, 1.0], np.float32), HALF)
    return jnp.cos(angles), jnp.sin(angles) * signs


def shuffle_matrix():
    to = lax.broadcasted_iota(jnp.int32, (256, 256), 0)
    source = lax.broadcasted_iota(jnp.int32, (256, 256), 1)
    here = source == (to & 15) * 16 + (to >> 4)
    return jnp.where(here, 1.0, 0.0).astype(jnp.bfloat16)


def cos_sin(angles):
    turns = jnp.floor(angles * (2.0 / math.pi) + 0.5)
    rest = angles - turns * 1.5703125
    rest = rest - turns * 4.837512969970703125e-4
    rest = rest - turns * 7.54978995489188e-8
    square = rest * rest
    sine = 1.0 / 362880.0
    for factor in (-1.0 / 5040.0, 1.0 / 120.0, -1.0 / 6.0, 1.0):
        sine = sine * square + factor
    sine = sine * rest
    cosine = -1.0 / 3628800.0
    for factor in (1.0 / 40320.0, -1.0 / 720.0, 1.0 / 24.0, -0.5, 1.0):
        cosine = cosine * square + factor
    quarter = turns.astype(jnp.int32)
    odd = (quarter & 1) == 1
    first = jnp.where(odd, sine, cosine)
    second = jnp.where(odd, cosine, sine)
    first = jnp.where(((quarter + 1) & 2) == 2, -first, first)
    second = jnp.where((quarter & 2) == 2, -second, second)
    return first, second


def node_row():
    lanes = lax.broadcasted_iota(jnp.int32, (1, WIDE), 1) % HALF
    points = [math.cos((2 * a + 1) * math.pi / 16) ** 2 for a in range(4)]

    def square(at):
        near = jnp.minimum(at, 7 - at)
        value = jnp.full(near.shape, points[3], jnp.float32)
        for a in range(3):
            value = jnp.where(near == a, jnp.float32(points[a]), value)
        return value

    return square(lanes // 8) + square(lanes % 8)


def rotation(column):
    cosine, sine = cos_sin(column * node_row())
    lanes = lax.broadcasted_iota(jnp.int32, cosine.shape, 1)
    return cosine, jnp.where(lanes < HALF, -sine, sine)


def column_of(row, count):
    shape = (count, WIDE)
    here = lax.broadcasted_iota(jnp.int32, shape, 0) == lax.broadcasted_iota(jnp.int32, shape, 1)
    return jnp.sum(jnp.where(here, jnp.broadcast_to(row, shape), 0.0), axis=1, keepdims=True)


def whole_matrix(upper):
    parts = [upper[:, at : at + HALF] for at in (HALF, 0, 3 * HALF, 2 * HALF)]
    traded = jnp.concatenate(parts, axis=1)
    im_lane = (lax.broadcasted_iota(jnp.int32, upper.shape, 1) & HALF) != 0
    below = jnp.where(im_lane, traded, -traded)
    traded_below = jnp.where(im_lane, -upper, upper)

    def stacked(first, second):
        children = (slice(0, HALF), slice(HALF, WIDE))
        return jnp.concatenate([half[rows] for rows in children for half in (first, second)], axis=0)

    return stacked(upper, below), stacked(traded, traded_below)


def butterfly(load, store, count, apart, matrix, swapped, phase_of, group, turn=0):
    lows = [i for i in range(count) if not i & apart]
    for start in range(0, len(lows), group):
        picked = lows[start : start + group]
        left = jnp.concatenate([load(i) for i in picked], axis=0)
        right = jnp.concatenate([load(i + apart) for i in picked], axis=0)
        rows = left.shape[0] // len(picked)
        pair = jnp.concatenate([left, right], axis=1)
        both = jnp.dot(pair, matrix, preferred_element_type=jnp.float32)
        if turn % 2 == 0:
            other = jnp.dot(pair, swapped, preferred_element_type=jnp.float32)
        for place, low in enumerate(picked):
            for child in range(2):
                index = low + child * apart
                cosine, sine = phase_of(index)
                mine = slice(place * rows, (place + 1) * rows)
                own = slice(child * WIDE, (child + 1) * WIDE)
                value = both[mine, own]
                turned = other[mine, own] if turn % 2 == 0 else pltpu.roll(value, HALF, 1)
                store(index, (value * cosine + turned * sine).astype(jnp.bfloat16))
        turn += 1


def swap_axes(load, store, outer, inner, shuffle):
    for low in range(0, outer, 2):
        for at in range(inner):
            sides = [load(low + side, at).reshape(256, WIDE) for side in range(2)]
            moved = jnp.dot(
                shuffle, jnp.concatenate(sides, axis=1), preferred_element_type=jnp.float32
            ).astype(jnp.bfloat16)
            for side in range(2):
                block = moved[:, side * WIDE : (side + 1) * WIDE]
                store(at, low + side, block.reshape(16, 16, WIDE))


def block_at(first, second):
    return (slice(first * 16, first * 16 + 16), slice(second * 16, second * 16 + 16))


PIECE = 64
BLOCK = 32
VMEM = pl.BlockSpec(memory_space=pltpu.VMEM)
FAR = pl.BlockSpec(memory_space=pltpu.HBM)
PARAMS = pltpu.CompilerParams(vmem_limit_bytes=32 << 20)


def source_kernel(a_hbm, x_hbm, m_hbm, o_ref, a_ref, x_ref, m_ref, w_ref, a_sem, x_sems, m_sems):
    rows, cols, _ = x_ref.shape
    levels = m_ref.shape[0]
    a_copy = pltpu.make_async_copy(a_hbm, a_ref, a_sem)
    x_copies = []
    for piece in range(cols // PIECE):
        own = (slice(None), pl.ds(piece * PIECE, PIECE))
        x_copies.append(pltpu.make_async_copy(x_hbm.at[own], x_ref.at[own], x_sems.at[piece]))
    m_copies = [
        pltpu.make_async_copy(m_hbm.at[i], m_ref.at[i], m_sems.at[i]) for i in range(levels)
    ]
    for copy in (a_copy, m_copies[0], *x_copies, *m_copies[1:]):
        copy.start()

    def expand(level):
        w_ref[2 * level], w_ref[2 * level + 1] = whole_matrix(m_ref[level])

    def level_on(level, begin):
        own = slice(begin, begin + BLOCK)

        def store(index, value):
            x_ref[index, own, :] = value

        butterfly(
            lambda index: x_ref[index, own, :],
            store,
            rows,
            1 << level,
            w_ref[2 * level],
            w_ref[2 * level + 1],
            lambda index: (cosines[own], sines[own]),
            16,
            begin // BLOCK,
        )

    a_copy.wait()
    cosines, sines = rotation(column_of(a_ref[...], cols))
    m_copies[0].wait()
    expand(0)
    for piece, copy in enumerate(x_copies):
        copy.wait()
        for begin in range(piece * PIECE, (piece + 1) * PIECE, BLOCK):
            level_on(0, begin)
    for copy in m_copies[1:]:
        copy.wait()
    for level in range(1, levels):
        expand(level)
    for level in range(1, levels):
        for begin in range(0, cols, BLOCK):
            level_on(level, begin)

    def store_block(first, second, block):
        o_ref[block_at(first, second)] = block

    swap_axes(
        lambda first, second: x_ref[block_at(first, second)],
        store_block,
        rows // 16,
        cols // 16,
        shuffle_matrix(),
    )


def source_levels(x, matrices, slowness):
    rows, cols, _ = x.shape
    levels = matrices.shape[0]
    operands = (slowness[None, :], x, matrices)
    far = [pltpu.with_memory_space_constraint(value, pltpu.HBM) for value in operands]
    return pl.pallas_call(
        source_kernel,
        out_shape=jax.ShapeDtypeStruct((cols, rows, WIDE), x.dtype),
        in_specs=[FAR, FAR, FAR],
        out_specs=VMEM,
        scratch_shapes=[
            pltpu.VMEM((1, cols), jnp.float32),
            pltpu.VMEM(x.shape, x.dtype),
            pltpu.VMEM(matrices.shape, x.dtype),
            pltpu.VMEM((2 * levels, 2 * WIDE, 2 * WIDE), x.dtype),
            pltpu.SemaphoreType.DMA,
            pltpu.SemaphoreType.DMA((cols // PIECE,)),
            pltpu.SemaphoreType.DMA((levels,)),
        ],
        compiler_params=PARAMS,
    )(*far)


def middle_kernel(levels, rows, x_ref, m_ref, cs_ref, ss_ref, ct_ref, st_ref, o_ref):
    count, total, _ = x_ref.shape
    run = total // rows
    tgt_count = cs_ref.shape[0] // run
    for step, (apart, by_source) in enumerate(levels):
        source = x_ref if step == 0 else o_ref
        matrix, swapped = whole_matrix(m_ref[step])
        for col in range(run):
            own = slice(col * rows, (col + 1) * rows)

            def phase_of(index):
                if by_source:
                    at = index % tgt_count * run + col
                    return cs_ref[at : at + 1, :], ss_ref[at : at + 1, :]
                at = index // tgt_count
                return ct_ref[at], st_ref[at]

            def store(index, value):
                o_ref[index, own, :] = value

            butterfly(
                lambda index: source[index, own, :],
                store,
                count,
                apart,
                matrix,
                swapped,
                phase_of,
                16,
                col,
            )


def middle_levels(x, matrices, src_tables, tgt_tables, levels):
    rows = tgt_tables[0].shape[1]
    return pl.pallas_call(
        functools.partial(middle_kernel, levels, rows),
        out_shape=jax.ShapeDtypeStruct(x.shape, x.dtype),
        in_specs=[VMEM] * 6,
        out_specs=VMEM,
        compiler_params=PARAMS,
    )(x, matrices, *src_tables, *tgt_tables)


def target_kernel(m_ref, c_ref, s_ref, x_ref, o_hbm, state_ref, o_ref, o_sems):
    cols, rows, _ = x_ref.shape
    levels = m_ref.shape[0]

    for level in range(levels):
        source = x_ref if level == 0 else state_ref
        weights = whole_matrix(m_ref[level])
        for start in range(0, rows, 16):
            own = slice(start, start + 16)
            cosine, sine = c_ref[own, :], s_ref[own, :]

            def store(index, value):
                state_ref[index, own, :] = value

            butterfly(
                lambda index: source[index, own, :],
                store,
                cols,
                1 << (levels - 1 - level),
                *weights,
                lambda index: (cosine, sine),
                32,
            )

    shuffle = shuffle_matrix()
    copies = []
    for piece in range(rows // 16):
        own = pl.ds(piece * 16, 16)
        copies.append(pltpu.make_async_copy(o_ref.at[own], o_hbm.at[own], o_sems.at[piece]))

        def store_block(first, second, block):
            o_ref[block_at(piece, second)] = block

        swap_axes(
            lambda first, second: state_ref[block_at(first, piece)],
            store_block,
            cols // 16,
            1,
            shuffle,
        )
        copies[-1].start()
    for copy in copies:
        copy.wait()


def target_levels(x, matrices, angles):
    cols, rows, _ = x.shape
    shape = (rows, cols, WIDE)
    return pl.pallas_call(
        target_kernel,
        out_shape=jax.ShapeDtypeStruct(shape, x.dtype),
        in_specs=[VMEM] * 4,
        out_specs=FAR,
        scratch_shapes=[
            pltpu.VMEM(x.shape, x.dtype),
            pltpu.VMEM(shape, x.dtype),
            pltpu.SemaphoreType.DMA((rows // 16,)),
        ],
        compiler_params=PARAMS,
    )(matrices, *angles, x)


def gathered(values, axis):
    count = lax.axis_size(axis)
    place = lax.axis_index(axis)
    values = values[None]
    apart = 1
    while apart < count:
        other = lax.ppermute(values, axis, [(i, i ^ apart) for i in range(count)])
        mine_first = (place & apart) == 0
        values = jnp.concatenate(
            [jnp.where(mine_first, values, other), jnp.where(mine_first, other, values)]
        )
        apart *= 2
    return values


def local(box_weights, slowness, dip_field):
    rows, cols, _ = box_weights.shape
    src_count = lax.axis_size("src")
    tgt_count = lax.axis_size("tgt")
    devices = src_count * tgt_count
    row_bits, col_bits = rows.bit_length() - 1, cols.bit_length() - 1
    src_bits, tgt_bits = src_count.bit_length() - 1, tgt_count.bit_length() - 1
    first_target = row_bits + src_bits
    total = first_target + tgt_bits + col_bits
    matrices = [level_matrix(number) for number in range(total)]

    def matrices_of(low, high):
        return jnp.asarray(np.stack(matrices[low:high]))

    run = cols // devices
    place = lax.axis_index("src") * tgt_count + lax.axis_index("tgt")

    def traded(state):
        return lax.all_to_all(state, ("src", "tgt"), 0, 0, tiled=True)

    state = source_levels(box_weights, matrices_of(0, row_bits), slowness)

    state, slowness, dip_field = lax.optimization_barrier((state, slowness, dip_field))
    all_dip = gathered(dip_field, "src")
    all_slowness = gathered(slowness, "tgt")
    run_slowness = lax.dynamic_slice_in_dim(all_slowness, place * run, run, 1)

    state = state.reshape(devices, run * rows, WIDE)
    state = traded(state)
    levels = [(tgt_count << bit, True) for bit in range(src_bits)]
    levels += [(1 << bit, False) for bit in reversed(range(tgt_bits))]
    state = middle_levels(
        state,
        matrices_of(row_bits, first_target + tgt_bits),
        tables(run_slowness.reshape(-1)),
        tables(all_dip),
        levels,
    )
    state = traded(state)

    return target_levels(
        state.reshape(cols, rows, WIDE),
        matrices_of(first_target + tgt_bits, total),
        tables(dip_field),
    )


def solution(mesh):
    in_specs = (P("src", "tgt", None), P("tgt"), P("src"))
    out_specs = P("src", "tgt", None)
    return jax.shard_map(local, mesh=mesh, in_specs=in_specs, out_specs=out_specs, check_vma=False)
```

```python
import functools
import math

import jax
import jax.numpy as jnp
import ml_dtypes
import numpy as np
from jax import lax
from jax.experimental import pallas as pl
from jax.experimental.pallas import tpu as pltpu
from jax.sharding import PartitionSpec as P

HALF = 64
WIDE = 128


def nodes():
    points = np.cos((2.0 * np.arange(8) + 1.0) * (math.pi / 16.0))
    return np.repeat(points, 8), np.tile(points, 8)


def node_weights():
    first, second = nodes()
    return (first * first + second * second).astype(np.float32)


def level_matrix(number):
    first, second = nodes()
    frequency = 9.0 + 3.0 * (number % 5)
    shifts = np.array([-0.5, 0.5])
    out_first = first[None, :] + shifts[:, None]
    in_second = second[None, :] + shifts[:, None]
    inner = (
        out_first[:, None, :, None] * first[None, None, None, :]
        + second[None, None, :, None] * in_second[None, :, None, :]
    )
    out_norm = np.sqrt(out_first**2 + second[None, :] ** 2)
    in_norm = np.sqrt(first[None, :] ** 2 + in_second**2)
    phases = frequency * (inner + 0.5 * out_norm[:, None, :, None] * in_norm[None, :, None, :])
    factor = 1.0 / math.sqrt(128.0)
    real = np.transpose(factor * np.cos(phases), (1, 3, 0, 2))
    imag = np.transpose(factor * np.sin(phases), (1, 3, 0, 2))
    upper = np.concatenate([real, imag], axis=3)
    return upper.reshape(WIDE, 2 * WIDE).astype(ml_dtypes.bfloat16)


def tables(scales):
    weights = np.tile(node_weights(), 2)
    angles = scales[..., None] * weights
    signs = np.repeat(np.array([-1.0, 1.0], np.float32), HALF)
    return jnp.cos(angles), jnp.sin(angles) * signs


def shuffle_matrix():
    to = lax.broadcasted_iota(jnp.int32, (256, 256), 0)
    source = lax.broadcasted_iota(jnp.int32, (256, 256), 1)
    here = source == (to & 15) * 16 + (to >> 4)
    return jnp.where(here, 1.0, 0.0).astype(jnp.bfloat16)


def cos_sin(angles):
    turns = jnp.floor(angles * (2.0 / math.pi) + 0.5)
    rest = angles - turns * 1.5703125
    rest = rest - turns * 4.837512969970703125e-4
    rest = rest - turns * 7.54978995489188e-8
    square = rest * rest
    sine = 1.0 / 362880.0
    for factor in (-1.0 / 5040.0, 1.0 / 120.0, -1.0 / 6.0, 1.0):
        sine = sine * square + factor
    sine = sine * rest
    cosine = -1.0 / 3628800.0
    for factor in (1.0 / 40320.0, -1.0 / 720.0, 1.0 / 24.0, -0.5, 1.0):
        cosine = cosine * square + factor
    quarter = turns.astype(jnp.int32)
    odd = (quarter & 1) == 1
    first = jnp.where(odd, sine, cosine)
    second = jnp.where(odd, cosine, sine)
    first = jnp.where(((quarter + 1) & 2) == 2, -first, first)
    second = jnp.where((quarter & 2) == 2, -second, second)
    return first, second


def node_row():
    lanes = lax.broadcasted_iota(jnp.int32, (1, WIDE), 1) % HALF
    points = [math.cos((2 * a + 1) * math.pi / 16) ** 2 for a in range(4)]

    def square(at):
        near = jnp.minimum(at, 7 - at)
        value = jnp.full(near.shape, points[3], jnp.float32)
        for a in range(3):
            value = jnp.where(near == a, jnp.float32(points[a]), value)
        return value

    return square(lanes // 8) + square(lanes % 8)


def rotation(column):
    cosine, sine = cos_sin(column * node_row())
    lanes = lax.broadcasted_iota(jnp.int32, cosine.shape, 1)
    return cosine, jnp.where(lanes < HALF, -sine, sine)


def column_of(row, count):
    shape = (count, WIDE)
    here = lax.broadcasted_iota(jnp.int32, shape, 0) == lax.broadcasted_iota(jnp.int32, shape, 1)
    return jnp.sum(jnp.where(here, jnp.broadcast_to(row, shape), 0.0), axis=1, keepdims=True)


def whole_matrix(upper):
    parts = [upper[:, at : at + HALF] for at in (HALF, 0, 3 * HALF, 2 * HALF)]
    traded = jnp.concatenate(parts, axis=1)
    im_lane = (lax.broadcasted_iota(jnp.int32, upper.shape, 1) & HALF) != 0
    below = jnp.where(im_lane, traded, -traded)
    traded_below = jnp.where(im_lane, -upper, upper)

    def stacked(first, second):
        children = (slice(0, HALF), slice(HALF, WIDE))
        return jnp.concatenate([half[rows] for rows in children for half in (first, second)], axis=0)

    return stacked(upper, below), stacked(traded, traded_below)


def butterfly(load, store, count, apart, matrix, swapped, phase_of, group, turn=0):
    lows = [i for i in range(count) if not i & apart]
    for start in range(0, len(lows), group):
        picked = lows[start : start + group]
        left = jnp.concatenate([load(i) for i in picked], axis=0)
        right = jnp.concatenate([load(i + apart) for i in picked], axis=0)
        rows = left.shape[0] // len(picked)
        pair = jnp.concatenate([left, right], axis=1)
        both = jnp.dot(pair, matrix, preferred_element_type=jnp.float32)
        if turn % 2 == 0:
            other = jnp.dot(pair, swapped, preferred_element_type=jnp.float32)
        for place, low in enumerate(picked):
            for child in range(2):
                index = low + child * apart
                cosine, sine = phase_of(index)
                mine = slice(place * rows, (place + 1) * rows)
                own = slice(child * WIDE, (child + 1) * WIDE)
                value = both[mine, own]
                turned = other[mine, own] if turn % 2 == 0 else pltpu.roll(value, HALF, 1)
                store(index, (value * cosine + turned * sine).astype(jnp.bfloat16))
        turn += 1


def swap_axes(load, store, outer, inner, shuffle):
    for low in range(0, outer, 2):
        for at in range(inner):
            sides = [load(low + side, at).reshape(256, WIDE) for side in range(2)]
            moved = jnp.dot(
                shuffle, jnp.concatenate(sides, axis=1), preferred_element_type=jnp.float32
            ).astype(jnp.bfloat16)
            for side in range(2):
                block = moved[:, side * WIDE : (side + 1) * WIDE]
                store(at, low + side, block.reshape(16, 16, WIDE))


def block_at(first, second):
    return (slice(first * 16, first * 16 + 16), slice(second * 16, second * 16 + 16))


PIECE = 64
BLOCK = 32
VMEM = pl.BlockSpec(memory_space=pltpu.VMEM)
FAR = pl.BlockSpec(memory_space=pltpu.HBM)
PARAMS = pltpu.CompilerParams(vmem_limit_bytes=32 << 20)


def source_kernel(a_hbm, x_hbm, m_hbm, o_ref, a_ref, x_ref, m_ref, w_ref, a_sem, x_sems, m_sems):
    rows, cols, _ = x_ref.shape
    levels = m_ref.shape[0]
    a_copy = pltpu.make_async_copy(a_hbm, a_ref, a_sem)
    x_copies = []
    for piece in range(cols // PIECE):
        own = (slice(None), pl.ds(piece * PIECE, PIECE))
        x_copies.append(pltpu.make_async_copy(x_hbm.at[own], x_ref.at[own], x_sems.at[piece]))
    m_copies = [
        pltpu.make_async_copy(m_hbm.at[i], m_ref.at[i], m_sems.at[i]) for i in range(levels)
    ]
    for copy in (a_copy, m_copies[0], *x_copies, *m_copies[1:]):
        copy.start()

    def expand(level):
        w_ref[2 * level], w_ref[2 * level + 1] = whole_matrix(m_ref[level])

    def level_on(level, begin):
        own = slice(begin, begin + BLOCK)

        def store(index, value):
            x_ref[index, own, :] = value

        butterfly(
            lambda index: x_ref[index, own, :],
            store,
            rows,
            1 << level,
            w_ref[2 * level],
            w_ref[2 * level + 1],
            lambda index: (cosines[own], sines[own]),
            16,
            begin // BLOCK,
        )

    a_copy.wait()
    cosines, sines = rotation(column_of(a_ref[...], cols))
    m_copies[0].wait()
    expand(0)
    for piece, copy in enumerate(x_copies):
        copy.wait()
        for begin in range(piece * PIECE, (piece + 1) * PIECE, BLOCK):
            level_on(0, begin)
    for copy in m_copies[1:]:
        copy.wait()
    for level in range(1, levels):
        expand(level)
    for level in range(1, levels):
        for begin in range(0, cols, BLOCK):
            level_on(level, begin)

    def store_block(first, second, block):
        o_ref[block_at(first, second)] = block

    swap_axes(
        lambda first, second: x_ref[block_at(first, second)],
        store_block,
        rows // 16,
        cols // 16,
        shuffle_matrix(),
    )


def source_levels(x, matrices, slowness):
    rows, cols, _ = x.shape
    levels = matrices.shape[0]
    operands = (slowness[None, :], x, matrices)
    far = [pltpu.with_memory_space_constraint(value, pltpu.HBM) for value in operands]
    return pl.pallas_call(
        source_kernel,
        out_shape=jax.ShapeDtypeStruct((cols, rows, WIDE), x.dtype),
        in_specs=[FAR, FAR, FAR],
        out_specs=VMEM,
        scratch_shapes=[
            pltpu.VMEM((1, cols), jnp.float32),
            pltpu.VMEM(x.shape, x.dtype),
            pltpu.VMEM(matrices.shape, x.dtype),
            pltpu.VMEM((2 * levels, 2 * WIDE, 2 * WIDE), x.dtype),
            pltpu.SemaphoreType.DMA,
            pltpu.SemaphoreType.DMA((cols // PIECE,)),
            pltpu.SemaphoreType.DMA((levels,)),
        ],
        compiler_params=PARAMS,
    )(*far)


def middle_kernel(levels, cols, x_ref, m_ref, cs_ref, ss_ref, ct_ref, st_ref, o_ref):
    count = x_ref.shape[0]
    rows = ct_ref.shape[1]
    run = x_ref.shape[1] // rows
    tgt_chips = cs_ref.shape[0] // run
    for step, (apart, by_source) in enumerate(levels):
        weights = whole_matrix(m_ref[step])
        for turn, col in enumerate(cols):
            first = col if step == 0 else turn
            source = x_ref if step == 0 else o_ref
            taken = slice(first * rows, (first + 1) * rows)
            own = slice(turn * rows, (turn + 1) * rows)

            def phase_of(index):
                if by_source:
                    at = index % tgt_chips * run + col
                    return cs_ref[at : at + 1, :], ss_ref[at : at + 1, :]
                at = index // tgt_chips
                return ct_ref[at], st_ref[at]

            def store(index, value):
                o_ref[index, own, :] = value

            butterfly(
                lambda index: source[index, taken, :],
                store,
                count,
                apart,
                *weights,
                phase_of,
                8,
                turn,
            )


def middle_levels(x, matrices, src_tables, tgt_tables, levels, cols):
    rows = tgt_tables[0].shape[1]
    return pl.pallas_call(
        functools.partial(middle_kernel, levels, cols),
        out_shape=jax.ShapeDtypeStruct((x.shape[0], len(cols) * rows, WIDE), x.dtype),
        in_specs=[VMEM] * 6,
        out_specs=VMEM,
        compiler_params=PARAMS,
    )(x, matrices, *src_tables, *tgt_tables)


def core_kernel(parts, m_ref, ct_ref, st_ref, *rest):
    o_ref = rest[-1]
    matrix = m_ref[lax.rem(lax.axis_index("tgt"), 2)]
    count = o_ref.shape[0]
    rows = ct_ref.shape[1]
    tgt_chips = count // ct_ref.shape[0]
    at = 0
    for own_ref, other_ref in zip(rest[:parts], rest[parts : 2 * parts]):
        total = own_ref.shape[1]
        group = max(1, 512 // total)
        for start in range(0, count, group):
            picked = slice(start, start + group)
            pair = [ref[picked].reshape(-1, WIDE) for ref in (own_ref, other_ref)]
            both = jnp.dot(
                jnp.concatenate(pair, axis=1), matrix, preferred_element_type=jnp.float32
            )
            for begin in range(0, both.shape[0], rows):
                index, row = divmod(begin, total)
                src = (start + index) // tgt_chips
                mine = slice(begin, begin + rows)
                value = both[mine, :WIDE] * ct_ref[src] + both[mine, WIDE:] * st_ref[src]
                o_ref[start + index, at + row : at + row + rows, :] = value.astype(jnp.bfloat16)
        at += total


def core_level(owns, upper, tgt_tables):
    devices = lax.axis_size("tgt")
    others = [lax.ppermute(own, "tgt", [(i, i ^ 1) for i in range(devices)]) for own in owns]
    real, imag = upper[..., :HALF], upper[..., HALF:]
    below = np.concatenate([-imag, real], axis=3)
    whole = np.concatenate([upper, below], axis=1).reshape(2, WIDE, 2, 2, HALF)
    choices = []
    for core in range(2):
        picked = whole[[core, 1 - core], :, core].reshape(2 * WIDE, 2, HALF)
        both = np.concatenate([picked, picked[:, ::-1]], axis=1).reshape(2 * WIDE, -1)
        choices.append(both.astype(ml_dtypes.bfloat16))
    shape = owns[0].shape
    total = sum(own.shape[1] for own in owns)
    return pl.pallas_call(
        functools.partial(core_kernel, len(owns)),
        out_shape=jax.ShapeDtypeStruct((shape[0], total, WIDE), owns[0].dtype),
        in_specs=[VMEM] * (3 + 2 * len(owns)),
        out_specs=VMEM,
        compiler_params=PARAMS,
    )(jnp.asarray(np.stack(choices)), *tgt_tables, *owns, *others)


def target_kernel(m_ref, c_ref, s_ref, x_ref, o_hbm, state_ref, o_ref, o_sems):
    cols, rows, _ = x_ref.shape
    levels = m_ref.shape[0]

    for level in range(levels):
        source = x_ref if level == 0 else state_ref
        weights = whole_matrix(m_ref[level])
        for start in range(0, rows, 16):
            own = slice(start, start + 16)
            cosine, sine = c_ref[own, :], s_ref[own, :]

            def store(index, value):
                state_ref[index, own, :] = value

            butterfly(
                lambda index: source[index, own, :],
                store,
                cols,
                1 << (levels - 1 - level),
                *weights,
                lambda index: (cosine, sine),
                32,
            )

    shuffle = shuffle_matrix()
    copies = []
    for piece in range(rows // 16):
        own = pl.ds(piece * 16, 16)
        copies.append(pltpu.make_async_copy(o_ref.at[own], o_hbm.at[own], o_sems.at[piece]))

        def store_block(first, second, block):
            o_ref[block_at(piece, second)] = block

        swap_axes(
            lambda first, second: state_ref[block_at(first, piece)],
            store_block,
            cols // 16,
            1,
            shuffle,
        )
        copies[-1].start()
    for copy in copies:
        copy.wait()


def target_levels(x, matrices, angles):
    cols, rows, _ = x.shape
    shape = (rows, cols, WIDE)
    return pl.pallas_call(
        target_kernel,
        out_shape=jax.ShapeDtypeStruct(shape, x.dtype),
        in_specs=[VMEM] * 4,
        out_specs=FAR,
        scratch_shapes=[
            pltpu.VMEM(x.shape, x.dtype),
            pltpu.VMEM(shape, x.dtype),
            pltpu.SemaphoreType.DMA((rows // 16,)),
        ],
        compiler_params=PARAMS,
    )(matrices, *angles, x)


def gathered(values, axis, bits):
    count = lax.axis_size(axis)
    place = lax.axis_index(axis)
    values = values[None]
    for bit in bits:
        other = lax.ppermute(values, axis, [(i, i ^ 1 << bit) for i in range(count)])
        mine_first = (place >> bit & 1) == 0
        values = jnp.concatenate(
            [jnp.where(mine_first, values, other), jnp.where(mine_first, other, values)]
        )
    return values


def local(box_weights, slowness, dip_field):
    rows, cols, _ = box_weights.shape
    src_count = lax.axis_size("src")
    tgt_count = lax.axis_size("tgt")
    tgt_chips = tgt_count // 2
    chips = src_count * tgt_chips
    row_bits, col_bits = rows.bit_length() - 1, cols.bit_length() - 1
    src_bits, chip_bits = src_count.bit_length() - 1, tgt_chips.bit_length() - 1
    first_target = row_bits + src_bits
    core = first_target + chip_bits
    total = core + 1 + col_bits
    matrices = [level_matrix(number) for number in range(total)]

    def matrices_of(low, high):
        return jnp.asarray(np.stack(matrices[low:high]))

    run = cols // chips
    place = lax.axis_index("src") * tgt_chips + lax.axis_index("tgt") // 2
    groups = [
        [src * tgt_count + 2 * at + side for src in range(src_count) for at in range(tgt_chips)]
        for side in range(2)
    ]

    def traded(state):
        return lax.all_to_all(
            state, ("src", "tgt"), 0, 0, axis_index_groups=groups, tiled=True
        )

    state = source_levels(box_weights, matrices_of(0, row_bits), slowness)

    state, slowness, dip_field = lax.optimization_barrier((state, slowness, dip_field))
    all_dip = gathered(dip_field, "src", range(src_bits))
    all_slowness = gathered(slowness, "tgt", range(1, 1 + chip_bits))
    run_slowness = lax.dynamic_slice_in_dim(all_slowness, place * run, run, 1)
    src_tables, tgt_tables = tables(run_slowness.reshape(-1)), tables(all_dip)

    state = traded(state.reshape(chips, run * rows, WIDE))
    levels = [(tgt_chips << bit, True) for bit in range(src_bits)]
    levels += [(1 << bit, False) for bit in reversed(range(chip_bits))]
    half = max(1, run // 2)
    middle = matrices_of(row_bits, core)
    owns = [
        middle_levels(state, middle, src_tables, tgt_tables, levels, range(start, start + half))
        for start in range(0, run, half)
    ]
    upper = matrices[core].astype(np.float32).reshape(2, HALF, 2, WIDE)
    state = core_level(owns, upper, tgt_tables)
    state = traded(state)

    return target_levels(
        state.reshape(cols, rows, WIDE), matrices_of(core + 1, total), tables(dip_field)
    )


def solution(mesh):
    in_specs = (P("src", "tgt", None), P("tgt"), P("src"))
    out_specs = P("src", "tgt", None)
    return jax.shard_map(local, mesh=mesh, in_specs=in_specs, out_specs=out_specs, check_vma=False)
```

```python
import functools
import math

import jax
import jax.numpy as jnp
import ml_dtypes
import numpy as np
from jax import lax
from jax.experimental import pallas as pl
from jax.experimental.pallas import tpu as pltpu
from jax.sharding import PartitionSpec as P

HALF = 64
WIDE = 128


def nodes():
    points = np.cos((2.0 * np.arange(8) + 1.0) * (math.pi / 16.0))
    return np.repeat(points, 8), np.tile(points, 8)


def node_weights():
    first, second = nodes()
    return (first * first + second * second).astype(np.float32)


def level_matrix(number):
    first, second = nodes()
    frequency = 9.0 + 3.0 * (number % 5)
    shifts = np.array([-0.5, 0.5])
    out_first = first[None, :] + shifts[:, None]
    in_second = second[None, :] + shifts[:, None]
    inner = (
        out_first[:, None, :, None] * first[None, None, None, :]
        + second[None, None, :, None] * in_second[None, :, None, :]
    )
    out_norm = np.sqrt(out_first**2 + second[None, :] ** 2)
    in_norm = np.sqrt(first[None, :] ** 2 + in_second**2)
    phases = frequency * (inner + 0.5 * out_norm[:, None, :, None] * in_norm[None, :, None, :])
    factor = 1.0 / math.sqrt(128.0)
    real = np.transpose(factor * np.cos(phases), (1, 3, 0, 2))
    imag = np.transpose(factor * np.sin(phases), (1, 3, 0, 2))
    upper = np.concatenate([real, imag], axis=3)
    return upper.reshape(WIDE, 2 * WIDE).astype(ml_dtypes.bfloat16)


def tables(scales):
    weights = np.tile(node_weights(), 2)
    angles = scales[..., None] * weights
    signs = np.repeat(np.array([-1.0, 1.0], np.float32), HALF)
    return jnp.cos(angles), jnp.sin(angles) * signs


def shuffle_matrix():
    to = lax.broadcasted_iota(jnp.int32, (256, 256), 0)
    source = lax.broadcasted_iota(jnp.int32, (256, 256), 1)
    here = source == (to & 15) * 16 + (to >> 4)
    return jnp.where(here, 1.0, 0.0).astype(jnp.bfloat16)


def cos_sin(angles):
    turns = jnp.floor(angles * (2.0 / math.pi) + 0.5)
    rest = angles - turns * 1.5703125
    rest = rest - turns * 4.837512969970703125e-4
    rest = rest - turns * 7.54978995489188e-8
    square = rest * rest
    sine = 1.0 / 362880.0
    for factor in (-1.0 / 5040.0, 1.0 / 120.0, -1.0 / 6.0, 1.0):
        sine = sine * square + factor
    sine = sine * rest
    cosine = -1.0 / 3628800.0
    for factor in (1.0 / 40320.0, -1.0 / 720.0, 1.0 / 24.0, -0.5, 1.0):
        cosine = cosine * square + factor
    quarter = turns.astype(jnp.int32)
    odd = (quarter & 1) == 1
    first = jnp.where(odd, sine, cosine)
    second = jnp.where(odd, cosine, sine)
    first = jnp.where(((quarter + 1) & 2) == 2, -first, first)
    second = jnp.where((quarter & 2) == 2, -second, second)
    return first, second


def node_row():
    lanes = lax.broadcasted_iota(jnp.int32, (1, WIDE), 1) % HALF
    points = [math.cos((2 * a + 1) * math.pi / 16) ** 2 for a in range(4)]

    def square(at):
        near = jnp.minimum(at, 7 - at)
        value = jnp.full(near.shape, points[3], jnp.float32)
        for a in range(3):
            value = jnp.where(near == a, jnp.float32(points[a]), value)
        return value

    return square(lanes // 8) + square(lanes % 8)


def rotation(column):
    cosine, sine = cos_sin(column * node_row())
    lanes = lax.broadcasted_iota(jnp.int32, cosine.shape, 1)
    return cosine, jnp.where(lanes < HALF, -sine, sine)


def column_of(row, count):
    shape = (count, WIDE)
    here = lax.broadcasted_iota(jnp.int32, shape, 0) == lax.broadcasted_iota(jnp.int32, shape, 1)
    return jnp.sum(jnp.where(here, jnp.broadcast_to(row, shape), 0.0), axis=1, keepdims=True)


def whole_matrix(upper):
    parts = [upper[:, at : at + HALF] for at in (HALF, 0, 3 * HALF, 2 * HALF)]
    traded = jnp.concatenate(parts, axis=1)
    im_lane = (lax.broadcasted_iota(jnp.int32, upper.shape, 1) & HALF) != 0
    below = jnp.where(im_lane, traded, -traded)
    traded_below = jnp.where(im_lane, -upper, upper)

    def stacked(first, second):
        children = (slice(0, HALF), slice(HALF, WIDE))
        return jnp.concatenate([half[rows] for rows in children for half in (first, second)], axis=0)

    return stacked(upper, below), stacked(traded, traded_below)


def butterfly(load, store, count, apart, matrix, swapped, phase_of, group, turn=0):
    lows = [i for i in range(count) if not i & apart]
    for start in range(0, len(lows), group):
        picked = lows[start : start + group]
        left = jnp.concatenate([load(i) for i in picked], axis=0)
        right = jnp.concatenate([load(i + apart) for i in picked], axis=0)
        rows = left.shape[0] // len(picked)
        pair = jnp.concatenate([left, right], axis=1)
        both = jnp.dot(pair, matrix, preferred_element_type=jnp.float32)
        if turn % 2 == 0:
            other = jnp.dot(pair, swapped, preferred_element_type=jnp.float32)
        for place, low in enumerate(picked):
            for child in range(2):
                index = low + child * apart
                cosine, sine = phase_of(index)
                mine = slice(place * rows, (place + 1) * rows)
                own = slice(child * WIDE, (child + 1) * WIDE)
                value = both[mine, own]
                turned = other[mine, own] if turn % 2 == 0 else pltpu.roll(value, HALF, 1)
                store(index, (value * cosine + turned * sine).astype(jnp.bfloat16))
        turn += 1


def swap_axes(load, store, outer, inner, shuffle):
    for low in range(0, outer, 2):
        for at in range(inner):
            sides = [load(low + side, at).reshape(256, WIDE) for side in range(2)]
            moved = jnp.dot(
                shuffle, jnp.concatenate(sides, axis=1), preferred_element_type=jnp.float32
            ).astype(jnp.bfloat16)
            for side in range(2):
                block = moved[:, side * WIDE : (side + 1) * WIDE]
                store(at, low + side, block.reshape(16, 16, WIDE))


def block_at(first, second):
    return (slice(first * 16, first * 16 + 16), slice(second * 16, second * 16 + 16))


PIECE = 64
BLOCK = 32
NOTE = 8
VMEM = pl.BlockSpec(memory_space=pltpu.VMEM)
FAR = pl.BlockSpec(memory_space=pltpu.HBM)
PARAMS = pltpu.CompilerParams(vmem_limit_bytes=32 << 20)


def write_note(note_ref, dip_ref, slowness):
    note_ref[...] = jnp.zeros_like(note_ref)
    note_ref[0:1, : dip_ref.shape[1]] = dip_ref[...]
    note_ref[3:4, :] = slowness
    for at in (0, 3):
        left = note_ref[at : at + 1, :]
        for part in range(3):
            piece = left.astype(jnp.bfloat16).astype(jnp.float32)
            note_ref[at + part : at + part + 1, :] = piece
            left = left - piece


def source_kernel(keep, a_hbm, d_ref, x_hbm, m_hbm, *rest):
    outs, (a_ref, x_ref, m_ref, w_ref, note_ref, a_sem, x_sems, m_sems) = rest[:-8], rest[-8:]
    rows, cols, _ = x_ref.shape
    devices = outs[0].shape[0]
    levels = m_ref.shape[0]
    a_copy = pltpu.make_async_copy(a_hbm, a_ref, a_sem)
    x_copies = []
    for piece in range(cols // PIECE):
        own = (slice(None), pl.ds(piece * PIECE, PIECE))
        x_copies.append(pltpu.make_async_copy(x_hbm.at[own], x_ref.at[own], x_sems.at[piece]))
    m_copies = [
        pltpu.make_async_copy(m_hbm.at[i], m_ref.at[i], m_sems.at[i]) for i in range(levels)
    ]
    for copy in (a_copy, m_copies[0], *x_copies, *m_copies[1:]):
        copy.start()

    def expand(level):
        w_ref[2 * level], w_ref[2 * level + 1] = whole_matrix(m_ref[level])

    def level_on(level, begin):
        own = slice(begin, begin + BLOCK)

        def store(index, value):
            x_ref[index, own, :] = value

        butterfly(
            lambda index: x_ref[index, own, :],
            store,
            rows,
            1 << level,
            w_ref[2 * level],
            w_ref[2 * level + 1],
            lambda index: (cosines[own], sines[own]),
            8,
        )

    a_copy.wait()
    slowness = a_ref[...]
    cosines, sines = rotation(column_of(slowness, cols))
    write_note(note_ref, d_ref, slowness)
    note = note_ref[...].astype(jnp.bfloat16)
    for device in range(devices):
        outs[0][device, keep * rows :, :] = note
    m_copies[0].wait()
    expand(0)
    for piece, copy in enumerate(x_copies):
        copy.wait()
        for begin in range(piece * PIECE, (piece + 1) * PIECE, BLOCK):
            level_on(0, begin)
    for copy in m_copies[1:]:
        copy.wait()
    for level in range(1, levels):
        expand(level)
    for level in range(1, levels):
        for begin in range(0, cols, BLOCK):
            level_on(level, begin)

    def store_block(first, second, block):
        begin = second * 16
        for inner in range(16):
            col = first * 16 + inner
            if col < devices * keep:
                device, at = divmod(col, keep)
                at = at * rows + begin
                outs[0][device, at : at + 16, :] = block[inner]
            else:
                outs[1][col - devices * keep, begin : begin + 16, :] = block[inner]

    swap_axes(
        lambda first, second: x_ref[block_at(first, second)],
        store_block,
        rows // 16,
        cols // 16,
        shuffle_matrix(),
    )


def source_levels(x, matrices, slowness, dip_field, devices, keep):
    rows, cols, _ = x.shape
    levels = matrices.shape[0]
    out_shape = [jax.ShapeDtypeStruct((devices, keep * rows + NOTE, WIDE), x.dtype)]
    if devices * keep < cols:
        out_shape.append(jax.ShapeDtypeStruct((cols - devices * keep, rows, WIDE), x.dtype))
    a, x, matrices = (
        pltpu.with_memory_space_constraint(value, pltpu.HBM)
        for value in (slowness[None, :], x, matrices)
    )
    return pl.pallas_call(
        functools.partial(source_kernel, keep),
        out_shape=out_shape,
        in_specs=[FAR, VMEM, FAR, FAR],
        out_specs=[VMEM] * len(out_shape),
        scratch_shapes=[
            pltpu.VMEM((1, cols), jnp.float32),
            pltpu.VMEM(x.shape, x.dtype),
            pltpu.VMEM(matrices.shape, x.dtype),
            pltpu.VMEM((2 * levels, 2 * WIDE, 2 * WIDE), x.dtype),
            pltpu.VMEM((NOTE, WIDE), jnp.float32),
            pltpu.SemaphoreType.DMA,
            pltpu.SemaphoreType.DMA((cols // PIECE,)),
            pltpu.SemaphoreType.DMA((levels,)),
        ],
        compiler_params=PARAMS,
    )(a, dip_field[None, :], x, matrices)


def partner_kernel(first_col, a_ref, x_ref, m_ref, y_ref, o_ref, state_ref):
    rows, cols, _ = x_ref.shape
    o_ref[:cols] = y_ref[...]
    cosines, sines = rotation(column_of(a_ref[...], first_col + cols)[first_col:])
    for level in range(m_ref.shape[0]):
        source = x_ref if level == 0 else state_ref
        weights = whole_matrix(m_ref[level])

        def store(index, value):
            state_ref[index] = value

        butterfly(
            lambda index: source[index],
            store,
            rows,
            1 << level,
            *weights,
            lambda index: (cosines, sines),
            max(1, 256 // cols),
        )

    def store_block(first, second, block):
        o_ref[cols + first * 16 : cols + first * 16 + 16, second * 16 : second * 16 + 16] = block

    swap_axes(
        lambda first, second: state_ref[block_at(first, second)],
        store_block,
        rows // 16,
        cols // 16,
        shuffle_matrix(),
    )


def partner_levels(x, matrices, slowness, own, first_col):
    rows, cols, _ = x.shape
    return pl.pallas_call(
        functools.partial(partner_kernel, first_col),
        out_shape=jax.ShapeDtypeStruct((2 * cols, rows, WIDE), x.dtype),
        in_specs=[VMEM] * 4,
        out_specs=VMEM,
        scratch_shapes=[pltpu.VMEM(x.shape, x.dtype)],
        compiler_params=PARAMS,
    )(slowness[None, :], x, matrices, own)


def pair_kernel(axis, bit, by_row, x_ref, y_ref, m_ref, c_ref, s_ref, o_ref):
    count, rows, _ = x_ref.shape
    matrix = m_ref[lax.rem(lax.div(lax.axis_index(axis), 1 << bit), 2)]
    group = max(1, 512 // rows)
    for start in range(0, count, group):
        picked = slice(start, start + group)
        pair = [ref[picked].reshape(-1, WIDE) for ref in (x_ref, y_ref)]
        both = jnp.dot(
            jnp.concatenate(pair, axis=1), matrix, preferred_element_type=jnp.float32
        )
        for index in range(start, min(start + group, count)):
            own = slice((index - start) * rows, (index - start + 1) * rows)
            phase = slice(None) if by_row else slice(index, index + 1)
            value = both[own, :WIDE] * c_ref[phase, :] + both[own, WIDE:] * s_ref[phase, :]
            o_ref[index] = value.astype(jnp.bfloat16)


def joined(own, other, axis, bit, upper, angles, by_row):
    upper = upper.astype(np.float32).reshape(2, HALF, 2, WIDE)
    below = np.concatenate([-upper[..., HALF:], upper[..., :HALF]], axis=3)
    whole = np.concatenate([upper, below], axis=1).reshape(2, WIDE, 2, 2, HALF)
    choices = []
    for child in range(2):
        picked = whole[[child, 1 - child], :, child].reshape(2 * WIDE, 2, HALF)
        both = np.concatenate([picked, picked[:, ::-1]], axis=1).reshape(2 * WIDE, -1)
        choices.append(both.astype(ml_dtypes.bfloat16))
    return pl.pallas_call(
        functools.partial(pair_kernel, axis, bit, by_row),
        out_shape=jax.ShapeDtypeStruct(own.shape, own.dtype),
        in_specs=[VMEM] * 5,
        out_specs=VMEM,
        compiler_params=PARAMS,
    )(own, other, jnp.asarray(np.stack(choices)), *angles)


def exchanged(value, axis, bit):
    count = lax.axis_size(axis)
    return lax.ppermute(value, axis, [(i, i ^ 1 << bit) for i in range(count)])


def middle_kernel(levels, rows, tgt_count, x_ref, m_ref, o_ref):
    count, total, _ = x_ref.shape
    kept = (total - NOTE) // rows
    place = lax.axis_index("src") * tgt_count + lax.axis_index("tgt")

    def noted(device, at):
        note = x_ref[device, kept * rows :, :].astype(jnp.float32)
        return note[at : at + 1] + note[at + 1 : at + 2] + note[at + 2 : at + 3]

    slowness = jnp.concatenate([noted(at, 3) for at in range(tgt_count)], axis=0)
    lanes = lax.broadcasted_iota(jnp.int32, slowness.shape, 1)
    by_col = []
    for col in range(kept):
        picked = jnp.where(lanes == place * kept + col, slowness, 0.0)
        by_col.append(rotation(jnp.sum(picked, axis=1, keepdims=True)))
    by_src = [
        rotation(column_of(noted(at * tgt_count, 0), rows)) for at in range(count // tgt_count)
    ]

    for step, (apart, by_source) in enumerate(levels):
        source = x_ref if step == 0 else o_ref
        weights = whole_matrix(m_ref[step])
        for col in range(kept):
            own = slice(col * rows, (col + 1) * rows)

            def phase_of(index):
                if by_source:
                    at = index % tgt_count
                    return tuple(table[at : at + 1, :] for table in by_col[col])
                return by_src[index // tgt_count]

            def store(index, value):
                o_ref[index, own, :] = value

            butterfly(
                lambda index: source[index, own, :],
                store,
                count,
                apart,
                *weights,
                phase_of,
                8,
            )


def middle_levels(x, matrices, levels, rows, tgt_count):
    count, total, _ = x.shape
    return pl.pallas_call(
        functools.partial(middle_kernel, levels, rows, tgt_count),
        out_shape=jax.ShapeDtypeStruct((count, total - NOTE, WIDE), x.dtype),
        in_specs=[VMEM] * 2,
        out_specs=VMEM,
        compiler_params=PARAMS,
    )(x, matrices)


def target_kernel(m_ref, c_ref, s_ref, *rest):
    xs, (o_hbm, state_ref, o_ref, o_sems) = rest[:-4], rest[-4:]
    cols, rows, _ = state_ref.shape
    devices, kept = xs[0].shape[0], xs[0].shape[1] // rows

    def arrived(index, start):
        if index >= devices * kept:
            return xs[1][index - devices * kept, start : start + 16, :]
        device, col = divmod(index, kept)
        start += col * rows
        return xs[0][device, start : start + 16, :]

    levels = m_ref.shape[0]

    for level in range(levels):
        weights = whole_matrix(m_ref[level])
        for start in range(0, rows, 16):
            own = slice(start, start + 16)
            cosine, sine = c_ref[own, :], s_ref[own, :]

            def load(index):
                return arrived(index, start) if level == 0 else state_ref[index, own, :]

            def store(index, value):
                state_ref[index, own, :] = value

            butterfly(
                load,
                store,
                cols,
                1 << (levels - 1 - level),
                *weights,
                lambda index: (cosine, sine),
                32,
            )

    shuffle = shuffle_matrix()
    copies = []
    for piece in range(rows // 16):
        own = pl.ds(piece * 16, 16)
        copies.append(pltpu.make_async_copy(o_ref.at[own], o_hbm.at[own], o_sems.at[piece]))

        def store_block(first, second, block):
            o_ref[block_at(piece, second)] = block

        swap_axes(
            lambda first, second: state_ref[block_at(first, piece)],
            store_block,
            cols // 16,
            1,
            shuffle,
        )
        copies[-1].start()
    for copy in copies:
        copy.wait()


def target_levels(xs, matrices, angles, cols, rows):
    shape = (rows, cols, WIDE)
    return pl.pallas_call(
        target_kernel,
        out_shape=jax.ShapeDtypeStruct(shape, jnp.bfloat16),
        in_specs=[VMEM] * (3 + len(xs)),
        out_specs=FAR,
        scratch_shapes=[
            pltpu.VMEM((cols, rows, WIDE), jnp.bfloat16),
            pltpu.VMEM(shape, jnp.bfloat16),
            pltpu.SemaphoreType.DMA((rows // 16,)),
        ],
        compiler_params=PARAMS,
    )(matrices, *angles, *xs)


def local(box_weights, slowness, dip_field):
    rows, cols, _ = box_weights.shape
    src_count = lax.axis_size("src")
    tgt_count = lax.axis_size("tgt")
    devices = src_count * tgt_count
    row_bits, col_bits = rows.bit_length() - 1, cols.bit_length() - 1
    src_bits, tgt_bits = src_count.bit_length() - 1, tgt_count.bit_length() - 1
    first_target = row_bits + src_bits
    total = first_target + tgt_bits + col_bits
    matrices = [level_matrix(number) for number in range(total)]

    def matrices_of(low, high):
        return jnp.asarray(np.stack(matrices[low:high]))

    run = cols // devices
    keep = run - run // 4
    sent = devices * keep
    stays = sent < cols
    top = tgt_bits - 1

    if stays:
        raw = exchanged(box_weights[:, sent:], "tgt", top)
        far_slowness = exchanged(slowness, "tgt", top)

    first = matrices_of(0, row_bits)
    state, *stay = source_levels(box_weights, first, slowness, dip_field, devices, keep)
    state, slowness, dip_field = lax.optimization_barrier((state, slowness, dip_field))
    by_row = tables(dip_field)

    def traded(state):
        return lax.all_to_all(state, ("src", "tgt"), 0, 0, tiled=True)

    state = traded(state)

    if stays:
        by_col = tables(jnp.concatenate([slowness[sent:], far_slowness[sent:]]))
        both = partner_levels(raw, first, far_slowness, stay[0], sent)
        for bit in range(src_bits):
            other = exchanged(both, "src", bit)
            both = joined(both, other, "src", bit, matrices[row_bits + bit], by_col, False)
            if bit == 0:
                state, both = lax.optimization_barrier((state, both))
        here, there = both[: cols - sent], both[cols - sent :]
        here = joined(here, there, "tgt", top, matrices[first_target], by_row, True)
        for at, bit in enumerate(reversed(range(top))):
            other = exchanged(here, "tgt", bit)
            here = joined(here, other, "tgt", bit, matrices[first_target + 1 + at], by_row, True)
        stay = [here]

    levels = [(tgt_count << bit, True) for bit in range(src_bits)]
    levels += [(1 << bit, False) for bit in reversed(range(tgt_bits))]
    middle = matrices_of(row_bits, first_target + tgt_bits)
    state = traded(middle_levels(state, middle, levels, rows, tgt_count))

    last = matrices_of(first_target + tgt_bits, total)
    return target_levels([state, *stay], last, by_row, cols, rows)


def solution(mesh):
    in_specs = (P("src", "tgt", None), P("tgt"), P("src"))
    out_specs = P("src", "tgt", None)
    return jax.shard_map(local, mesh=mesh, in_specs=in_specs, out_specs=out_specs, check_vma=False)
```

```python
import functools
import math

import jax
import jax.numpy as jnp
import ml_dtypes
import numpy as np
from jax import lax
from jax.experimental import pallas as pl
from jax.experimental.pallas import tpu as pltpu
from jax.sharding import PartitionSpec as P

HALF = 64
WIDE = 128


def nodes():
    points = np.cos((2.0 * np.arange(8) + 1.0) * (math.pi / 16.0))
    return np.repeat(points, 8), np.tile(points, 8)


def node_weights():
    first, second = nodes()
    return (first * first + second * second).astype(np.float32)


def level_matrix(number):
    first, second = nodes()
    frequency = 9.0 + 3.0 * (number % 5)
    shifts = np.array([-0.5, 0.5])
    out_first = first[None, :] + shifts[:, None]
    in_second = second[None, :] + shifts[:, None]
    inner = (
        out_first[:, None, :, None] * first[None, None, None, :]
        + second[None, None, :, None] * in_second[None, :, None, :]
    )
    out_norm = np.sqrt(out_first**2 + second[None, :] ** 2)
    in_norm = np.sqrt(first[None, :] ** 2 + in_second**2)
    phases = frequency * (inner + 0.5 * out_norm[:, None, :, None] * in_norm[None, :, None, :])
    factor = 1.0 / math.sqrt(128.0)
    real = np.transpose(factor * np.cos(phases), (1, 3, 0, 2))
    imag = np.transpose(factor * np.sin(phases), (1, 3, 0, 2))
    upper = np.concatenate([real, imag], axis=3)
    return upper.reshape(WIDE, 2 * WIDE).astype(ml_dtypes.bfloat16)


def tables(scales):
    weights = np.tile(node_weights(), 2)
    angles = scales[..., None] * weights
    signs = np.repeat(np.array([-1.0, 1.0], np.float32), HALF)
    return jnp.cos(angles), jnp.sin(angles) * signs


def shuffle_matrix():
    to = lax.broadcasted_iota(jnp.int32, (256, 256), 0)
    source = lax.broadcasted_iota(jnp.int32, (256, 256), 1)
    here = source == (to & 15) * 16 + (to >> 4)
    return jnp.where(here, 1.0, 0.0).astype(jnp.bfloat16)


def cos_sin(angles):
    turns = jnp.floor(angles * (2.0 / math.pi) + 0.5)
    rest = angles - turns * 1.5703125
    rest = rest - turns * 4.837512969970703125e-4
    rest = rest - turns * 7.54978995489188e-8
    square = rest * rest
    sine = 1.0 / 362880.0
    for factor in (-1.0 / 5040.0, 1.0 / 120.0, -1.0 / 6.0, 1.0):
        sine = sine * square + factor
    sine = sine * rest
    cosine = -1.0 / 3628800.0
    for factor in (1.0 / 40320.0, -1.0 / 720.0, 1.0 / 24.0, -0.5, 1.0):
        cosine = cosine * square + factor
    quarter = turns.astype(jnp.int32)
    odd = (quarter & 1) == 1
    first = jnp.where(odd, sine, cosine)
    second = jnp.where(odd, cosine, sine)
    first = jnp.where(((quarter + 1) & 2) == 2, -first, first)
    second = jnp.where((quarter & 2) == 2, -second, second)
    return first, second


def node_row():
    lanes = lax.broadcasted_iota(jnp.int32, (1, WIDE), 1) % HALF
    points = [math.cos((2 * a + 1) * math.pi / 16) ** 2 for a in range(4)]

    def square(at):
        near = jnp.minimum(at, 7 - at)
        value = jnp.full(near.shape, points[3], jnp.float32)
        for a in range(3):
            value = jnp.where(near == a, jnp.float32(points[a]), value)
        return value

    return square(lanes // 8) + square(lanes % 8)


def rotation(column):
    cosine, sine = cos_sin(column * node_row())
    lanes = lax.broadcasted_iota(jnp.int32, cosine.shape, 1)
    return cosine, jnp.where(lanes < HALF, -sine, sine)


def column_of(row, count):
    shape = (count, WIDE)
    here = lax.broadcasted_iota(jnp.int32, shape, 0) == lax.broadcasted_iota(jnp.int32, shape, 1)
    return jnp.sum(jnp.where(here, jnp.broadcast_to(row, shape), 0.0), axis=1, keepdims=True)


def whole_matrix(upper):
    parts = [upper[:, at : at + HALF] for at in (HALF, 0, 3 * HALF, 2 * HALF)]
    traded = jnp.concatenate(parts, axis=1)
    im_lane = (lax.broadcasted_iota(jnp.int32, upper.shape, 1) & HALF) != 0
    below = jnp.where(im_lane, traded, -traded)
    traded_below = jnp.where(im_lane, -upper, upper)

    def stacked(first, second):
        children = (slice(0, HALF), slice(HALF, WIDE))
        return jnp.concatenate([half[rows] for rows in children for half in (first, second)], axis=0)

    return stacked(upper, below), stacked(traded, traded_below)


def butterfly(load, store, count, apart, matrix, swapped, phase_of, group, turn=0):
    lows = [i for i in range(count) if not i & apart]
    for start in range(0, len(lows), group):
        picked = lows[start : start + group]
        left = jnp.concatenate([load(i) for i in picked], axis=0)
        right = jnp.concatenate([load(i + apart) for i in picked], axis=0)
        rows = left.shape[0] // len(picked)
        pair = jnp.concatenate([left, right], axis=1)
        both = jnp.dot(pair, matrix, preferred_element_type=jnp.float32)
        if turn % 2 == 0:
            other = jnp.dot(pair, swapped, preferred_element_type=jnp.float32)
        for place, low in enumerate(picked):
            for child in range(2):
                index = low + child * apart
                cosine, sine = phase_of(index)
                mine = slice(place * rows, (place + 1) * rows)
                own = slice(child * WIDE, (child + 1) * WIDE)
                value = both[mine, own]
                turned = other[mine, own] if turn % 2 == 0 else pltpu.roll(value, HALF, 1)
                store(index, (value * cosine + turned * sine).astype(jnp.bfloat16))
        turn += 1


def swap_axes(load, store, outer, inner, shuffle):
    for low in range(0, outer, 2):
        for at in range(inner):
            sides = [load(low + side, at).reshape(256, WIDE) for side in range(2)]
            moved = jnp.dot(
                shuffle, jnp.concatenate(sides, axis=1), preferred_element_type=jnp.float32
            ).astype(jnp.bfloat16)
            for side in range(2):
                block = moved[:, side * WIDE : (side + 1) * WIDE]
                store(at, low + side, block.reshape(16, 16, WIDE))


def block_at(first, second):
    return (slice(first * 16, first * 16 + 16), slice(second * 16, second * 16 + 16))


PIECE = 64
SPAN = 8
BLOCK = 32
VMEM = pl.BlockSpec(memory_space=pltpu.VMEM)
FAR = pl.BlockSpec(memory_space=pltpu.HBM)
PARAMS = pltpu.CompilerParams(vmem_limit_bytes=32 << 20)


def source_kernel(a_hbm, x_hbm, m_hbm, o_ref, a_ref, x_ref, m_ref, w_ref, a_sem, x_sems, m_sems):
    rows, cols, _ = x_ref.shape
    levels = m_ref.shape[0]
    a_copy = pltpu.make_async_copy(a_hbm, a_ref, a_sem)
    x_copies = []
    for piece in range(cols // PIECE):
        for at in range(0, rows, SPAN):
            own = (pl.ds(at, SPAN), pl.ds(piece * PIECE, PIECE))
            sem = x_sems.at[len(x_copies)]
            x_copies.append(pltpu.make_async_copy(x_hbm.at[own], x_ref.at[own], sem))
    m_copies = [
        pltpu.make_async_copy(m_hbm.at[i], m_ref.at[i], m_sems.at[i]) for i in range(levels)
    ]
    for copy in (a_copy, m_copies[0], *x_copies, *m_copies[1:]):
        copy.start()

    def expand(level):
        w_ref[2 * level], w_ref[2 * level + 1] = whole_matrix(m_ref[level])

    def level_on(level, begin):
        own = slice(begin, begin + BLOCK)

        def store(index, value):
            x_ref[index, own, :] = value

        butterfly(
            lambda index: x_ref[index, own, :],
            store,
            rows,
            1 << level,
            w_ref[2 * level],
            w_ref[2 * level + 1],
            lambda index: (cosines[own], sines[own]),
            8,
        )

    a_copy.wait()
    cosines, sines = rotation(column_of(a_ref[...], cols))
    m_copies[0].wait()
    expand(0)
    each = rows // SPAN
    for piece in range(cols // PIECE):
        for copy in x_copies[piece * each : (piece + 1) * each]:
            copy.wait()
        for begin in range(piece * PIECE, (piece + 1) * PIECE, BLOCK):
            level_on(0, begin)
    for copy in m_copies[1:]:
        copy.wait()
    for level in range(1, levels):
        expand(level)
    for level in range(1, levels):
        for begin in range(0, cols, BLOCK):
            level_on(level, begin)

    def store_block(first, second, block):
        o_ref[block_at(first, second)] = block

    swap_axes(
        lambda first, second: x_ref[block_at(first, second)],
        store_block,
        rows // 16,
        cols // 16,
        shuffle_matrix(),
    )


def source_levels(x, matrices, slowness):
    rows, cols, _ = x.shape
    levels = matrices.shape[0]
    operands = (slowness[None, :], x, matrices)
    far = [pltpu.with_memory_space_constraint(value, pltpu.HBM) for value in operands]
    return pl.pallas_call(
        source_kernel,
        out_shape=jax.ShapeDtypeStruct((cols, rows, WIDE), x.dtype),
        in_specs=[FAR, FAR, FAR],
        out_specs=VMEM,
        scratch_shapes=[
            pltpu.VMEM((1, cols), jnp.float32),
            pltpu.VMEM(x.shape, x.dtype),
            pltpu.VMEM(matrices.shape, x.dtype),
            pltpu.VMEM((2 * levels, 2 * WIDE, 2 * WIDE), x.dtype),
            pltpu.SemaphoreType.DMA,
            pltpu.SemaphoreType.DMA((cols // PIECE * (rows // SPAN),)),
            pltpu.SemaphoreType.DMA((levels,)),
        ],
        compiler_params=PARAMS,
    )(*far)


def middle_kernel(levels, rows, x_ref, m_ref, cs_ref, ss_ref, ct_ref, st_ref, o_ref):
    count, total, _ = x_ref.shape
    run = total // rows
    tgt_count = cs_ref.shape[0] // run
    for step, (apart, by_source) in enumerate(levels):
        source = x_ref if step == 0 else o_ref
        matrix, swapped = whole_matrix(m_ref[step])
        for col in range(run):
            own = slice(col * rows, (col + 1) * rows)

            def phase_of(index):
                if by_source:
                    at = index % tgt_count * run + col
                    return cs_ref[at : at + 1, :], ss_ref[at : at + 1, :]
                at = index // tgt_count
                return ct_ref[at], st_ref[at]

            def store(index, value):
                o_ref[index, own, :] = value

            butterfly(
                lambda index: source[index, own, :],
                store,
                count,
                apart,
                matrix,
                swapped,
                phase_of,
                8,
            )


def middle_levels(x, matrices, src_tables, tgt_tables, levels):
    rows = tgt_tables[0].shape[1]
    return pl.pallas_call(
        functools.partial(middle_kernel, levels, rows),
        out_shape=jax.ShapeDtypeStruct(x.shape, x.dtype),
        in_specs=[VMEM] * 6,
        out_specs=VMEM,
        compiler_params=PARAMS,
    )(x, matrices, *src_tables, *tgt_tables)


def target_kernel(m_ref, c_ref, s_ref, x_ref, o_hbm, state_ref, o_ref, o_sems):
    cols, rows, _ = x_ref.shape
    levels = m_ref.shape[0]

    for level in range(levels):
        source = x_ref if level == 0 else state_ref
        weights = whole_matrix(m_ref[level])
        for start in range(0, rows, 16):
            own = slice(start, start + 16)
            cosine, sine = c_ref[own, :], s_ref[own, :]

            def store(index, value):
                state_ref[index, own, :] = value

            butterfly(
                lambda index: source[index, own, :],
                store,
                cols,
                1 << (levels - 1 - level),
                *weights,
                lambda index: (cosine, sine),
                32,
            )

    shuffle = shuffle_matrix()
    copies = []
    half = cols // 2
    for piece in range(rows // 16):
        for side in range(2):
            own = (pl.ds(piece * 16, 16), pl.ds(side * half, half))
            copies.append(
                pltpu.make_async_copy(o_ref.at[own], o_hbm.at[own], o_sems.at[len(copies)])
            )

            def store_block(first, second, block):
                o_ref[block_at(piece, side * half // 16 + second)] = block

            swap_axes(
                lambda first, second: state_ref[block_at(side * half // 16 + first, piece)],
                store_block,
                half // 16,
                1,
                shuffle,
            )
            copies[-1].start()
    for copy in copies:
        copy.wait()


def target_levels(x, matrices, angles):
    cols, rows, _ = x.shape
    shape = (rows, cols, WIDE)
    return pl.pallas_call(
        target_kernel,
        out_shape=jax.ShapeDtypeStruct(shape, x.dtype),
        in_specs=[VMEM] * 4,
        out_specs=FAR,
        scratch_shapes=[
            pltpu.VMEM(x.shape, x.dtype),
            pltpu.VMEM(shape, x.dtype),
            pltpu.SemaphoreType.DMA((rows // 8,)),
        ],
        compiler_params=PARAMS,
    )(matrices, *angles, x)


def gathered(values, axis):
    count = lax.axis_size(axis)
    place = lax.axis_index(axis)
    values = values[None]
    apart = 1
    while apart < count:
        other = lax.ppermute(values, axis, [(i, i ^ apart) for i in range(count)])
        mine_first = (place & apart) == 0
        values = jnp.concatenate(
            [jnp.where(mine_first, values, other), jnp.where(mine_first, other, values)]
        )
        apart *= 2
    return values


def local(box_weights, slowness, dip_field):
    rows, cols, _ = box_weights.shape
    src_count = lax.axis_size("src")
    tgt_count = lax.axis_size("tgt")
    devices = src_count * tgt_count
    row_bits, col_bits = rows.bit_length() - 1, cols.bit_length() - 1
    src_bits, tgt_bits = src_count.bit_length() - 1, tgt_count.bit_length() - 1
    first_target = row_bits + src_bits
    total = first_target + tgt_bits + col_bits
    matrices = [level_matrix(number) for number in range(total)]

    def matrices_of(low, high):
        return jnp.asarray(np.stack(matrices[low:high]))

    run = cols // devices
    place = lax.axis_index("src") * tgt_count + lax.axis_index("tgt")

    def traded(state):
        return lax.all_to_all(state, ("src", "tgt"), 0, 0, tiled=True)

    state = source_levels(box_weights, matrices_of(0, row_bits), slowness)

    state, slowness, dip_field = lax.optimization_barrier((state, slowness, dip_field))
    all_dip = gathered(dip_field, "src")
    all_slowness = gathered(slowness, "tgt")
    run_slowness = lax.dynamic_slice_in_dim(all_slowness, place * run, run, 1)

    state = state.reshape(devices, run * rows, WIDE)
    state = traded(state)
    levels = [(tgt_count << bit, True) for bit in range(src_bits)]
    levels += [(1 << bit, False) for bit in reversed(range(tgt_bits))]
    state = middle_levels(
        state,
        matrices_of(row_bits, first_target + tgt_bits),
        tables(run_slowness.reshape(-1)),
        tables(all_dip),
        levels,
    )
    state = traded(state)

    return target_levels(
        state.reshape(cols, rows, WIDE),
        matrices_of(first_target + tgt_bits, total),
        tables(dip_field),
    )


def solution(mesh):
    in_specs = (P("src", "tgt", None), P("tgt"), P("src"))
    out_specs = P("src", "tgt", None)
    return jax.shard_map(local, mesh=mesh, in_specs=in_specs, out_specs=out_specs, check_vma=False)
```

```python
import functools
import math

import jax
import jax.numpy as jnp
import ml_dtypes
import numpy as np
from jax import lax
from jax.experimental import pallas as pl
from jax.experimental.pallas import tpu as pltpu
from jax.sharding import PartitionSpec as P

HALF = 64
WIDE = 128


def nodes():
    points = np.cos((2.0 * np.arange(8) + 1.0) * (math.pi / 16.0))
    return np.repeat(points, 8), np.tile(points, 8)


def node_weights():
    first, second = nodes()
    return (first * first + second * second).astype(np.float32)


def level_matrix(number):
    first, second = nodes()
    frequency = 9.0 + 3.0 * (number % 5)
    shifts = np.array([-0.5, 0.5])
    out_first = first[None, :] + shifts[:, None]
    in_second = second[None, :] + shifts[:, None]
    inner = (
        out_first[:, None, :, None] * first[None, None, None, :]
        + second[None, None, :, None] * in_second[None, :, None, :]
    )
    out_norm = np.sqrt(out_first**2 + second[None, :] ** 2)
    in_norm = np.sqrt(first[None, :] ** 2 + in_second**2)
    phases = frequency * (inner + 0.5 * out_norm[:, None, :, None] * in_norm[None, :, None, :])
    factor = 1.0 / math.sqrt(128.0)
    real = np.transpose(factor * np.cos(phases), (1, 3, 0, 2))
    imag = np.transpose(factor * np.sin(phases), (1, 3, 0, 2))
    upper = np.concatenate([real, imag], axis=3)
    return upper.reshape(WIDE, 2 * WIDE).astype(ml_dtypes.bfloat16)


def tables(scales):
    weights = np.tile(node_weights(), 2)
    angles = scales[..., None] * weights
    signs = np.repeat(np.array([-1.0, 1.0], np.float32), HALF)
    return jnp.cos(angles), jnp.sin(angles) * signs


def shuffle_matrix():
    to = lax.broadcasted_iota(jnp.int32, (256, 256), 0)
    source = lax.broadcasted_iota(jnp.int32, (256, 256), 1)
    here = source == (to & 15) * 16 + (to >> 4)
    return jnp.where(here, 1.0, 0.0).astype(jnp.bfloat16)


def cos_sin(angles):
    turns = jnp.floor(angles * (2.0 / math.pi) + 0.5)
    rest = angles - turns * 1.5703125
    rest = rest - turns * 4.837512969970703125e-4
    rest = rest - turns * 7.54978995489188e-8
    square = rest * rest
    sine = 1.0 / 362880.0
    for factor in (-1.0 / 5040.0, 1.0 / 120.0, -1.0 / 6.0, 1.0):
        sine = sine * square + factor
    sine = sine * rest
    cosine = -1.0 / 3628800.0
    for factor in (1.0 / 40320.0, -1.0 / 720.0, 1.0 / 24.0, -0.5, 1.0):
        cosine = cosine * square + factor
    quarter = turns.astype(jnp.int32)
    odd = (quarter & 1) == 1
    first = jnp.where(odd, sine, cosine)
    second = jnp.where(odd, cosine, sine)
    first = jnp.where(((quarter + 1) & 2) == 2, -first, first)
    second = jnp.where((quarter & 2) == 2, -second, second)
    return first, second


def halved(table):
    return tuple(part.astype(jnp.bfloat16) for part in table)


def node_row():
    lanes = lax.broadcasted_iota(jnp.int32, (1, WIDE), 1) % HALF
    points = [math.cos((2 * a + 1) * math.pi / 16) ** 2 for a in range(4)]

    def square(at):
        near = jnp.minimum(at, 7 - at)
        value = jnp.full(near.shape, points[3], jnp.float32)
        for a in range(3):
            value = jnp.where(near == a, jnp.float32(points[a]), value)
        return value

    return square(lanes // 8) + square(lanes % 8)


def rotation(column):
    cosine, sine = cos_sin(column * node_row())
    lanes = lax.broadcasted_iota(jnp.int32, cosine.shape, 1)
    return cosine, jnp.where(lanes < HALF, -sine, sine)


def column_of(row, count):
    shape = (count, WIDE)
    here = lax.broadcasted_iota(jnp.int32, shape, 0) == lax.broadcasted_iota(jnp.int32, shape, 1)
    return jnp.sum(jnp.where(here, jnp.broadcast_to(row, shape), 0.0), axis=1, keepdims=True)


def whole_matrix(upper):
    parts = [upper[:, at : at + HALF] for at in (HALF, 0, 3 * HALF, 2 * HALF)]
    traded = jnp.concatenate(parts, axis=1)
    im_lane = (lax.broadcasted_iota(jnp.int32, upper.shape, 1) & HALF) != 0
    below = jnp.where(im_lane, traded, -traded)
    traded_below = jnp.where(im_lane, -upper, upper)

    def stacked(first, second):
        children = (slice(0, HALF), slice(HALF, WIDE))
        return jnp.concatenate([half[rows] for rows in children for half in (first, second)], axis=0)

    return stacked(upper, below), stacked(traded, traded_below)


def butterfly(load, store, count, apart, matrix, swapped, phase_of, group, turn=0):
    lows = [i for i in range(count) if not i & apart]
    for start in range(0, len(lows), group):
        picked = lows[start : start + group]
        left = jnp.concatenate([load(i) for i in picked], axis=0)
        right = jnp.concatenate([load(i + apart) for i in picked], axis=0)
        rows = left.shape[0] // len(picked)
        pair = jnp.concatenate([left, right], axis=1)
        both = jnp.dot(pair, matrix, preferred_element_type=jnp.float32).astype(jnp.bfloat16)
        if turn % 2 == 0:
            other = jnp.dot(pair, swapped, preferred_element_type=jnp.float32)
            other = other.astype(jnp.bfloat16)
        for place, low in enumerate(picked):
            for child in range(2):
                index = low + child * apart
                cosine, sine = phase_of(index)
                mine = slice(place * rows, (place + 1) * rows)
                own = slice(child * WIDE, (child + 1) * WIDE)
                value = both[mine, own]
                if turn % 2 == 0:
                    turned = other[mine, own]
                else:
                    turned = jnp.concatenate([value[:, HALF:], value[:, :HALF]], axis=1)
                store(index, value * cosine + turned * sine)
        turn += 1


def swap_axes(load, store, outer, inner, shuffle):
    for low in range(0, outer, 2):
        for at in range(inner):
            sides = [load(low + side, at).reshape(256, WIDE) for side in range(2)]
            moved = jnp.dot(
                shuffle, jnp.concatenate(sides, axis=1), preferred_element_type=jnp.float32
            ).astype(jnp.bfloat16)
            for side in range(2):
                block = moved[:, side * WIDE : (side + 1) * WIDE]
                store(at, low + side, block.reshape(16, 16, WIDE))


def block_at(first, second):
    return (slice(first * 16, first * 16 + 16), slice(second * 16, second * 16 + 16))


PIECE = 64
SPAN = 8
BLOCK = 32
VMEM = pl.BlockSpec(memory_space=pltpu.VMEM)
FAR = pl.BlockSpec(memory_space=pltpu.HBM)
PARAMS = pltpu.CompilerParams(vmem_limit_bytes=32 << 20)


def source_kernel(a_hbm, x_hbm, m_hbm, o_ref, a_ref, x_ref, m_ref, w_ref, a_sem, x_sems, m_sems):
    rows, cols, _ = x_ref.shape
    levels = m_ref.shape[0]
    a_copy = pltpu.make_async_copy(a_hbm, a_ref, a_sem)
    x_copies = []
    for piece in range(cols // PIECE):
        for at in range(0, rows, SPAN):
            own = (pl.ds(at, SPAN), pl.ds(piece * PIECE, PIECE))
            sem = x_sems.at[len(x_copies)]
            x_copies.append(pltpu.make_async_copy(x_hbm.at[own], x_ref.at[own], sem))
    m_copies = [
        pltpu.make_async_copy(m_hbm.at[i], m_ref.at[i], m_sems.at[i]) for i in range(levels)
    ]
    for copy in (a_copy, m_copies[0], *x_copies, *m_copies[1:]):
        copy.start()

    def expand(level):
        w_ref[2 * level], w_ref[2 * level + 1] = whole_matrix(m_ref[level])

    def level_on(level, begin):
        own = slice(begin, begin + BLOCK)

        def store(index, value):
            x_ref[index, own, :] = value

        butterfly(
            lambda index: x_ref[index, own, :],
            store,
            rows,
            1 << level,
            w_ref[2 * level],
            w_ref[2 * level + 1],
            lambda index: (cosines[own], sines[own]),
            8,
        )

    m_copies[0].wait()
    each = rows // SPAN
    for piece in range(cols // PIECE):
        for copy in x_copies[piece * each : (piece + 1) * each]:
            copy.wait()
        if piece == 0:
            a_copy.wait()
            expand(0)
            cosines, sines = halved(rotation(column_of(a_ref[...], cols)))
        for begin in range(piece * PIECE, (piece + 1) * PIECE, BLOCK):
            level_on(0, begin)
    for copy in m_copies[1:]:
        copy.wait()
    for level in range(1, levels):
        expand(level)
    for level in range(1, levels):
        for begin in range(0, cols, BLOCK):
            level_on(level, begin)

    def store_block(first, second, block):
        o_ref[block_at(first, second)] = block

    swap_axes(
        lambda first, second: x_ref[block_at(first, second)],
        store_block,
        rows // 16,
        cols // 16,
        shuffle_matrix(),
    )


def source_levels(x, matrices, slowness):
    rows, cols, _ = x.shape
    levels = matrices.shape[0]
    operands = (slowness[None, :], x, matrices)
    far = [pltpu.with_memory_space_constraint(value, pltpu.HBM) for value in operands]
    return pl.pallas_call(
        source_kernel,
        out_shape=jax.ShapeDtypeStruct((cols, rows, WIDE), x.dtype),
        in_specs=[FAR, FAR, FAR],
        out_specs=VMEM,
        scratch_shapes=[
            pltpu.VMEM((1, cols), jnp.float32),
            pltpu.VMEM(x.shape, x.dtype),
            pltpu.VMEM(matrices.shape, x.dtype),
            pltpu.VMEM((2 * levels, 2 * WIDE, 2 * WIDE), x.dtype),
            pltpu.SemaphoreType.DMA,
            pltpu.SemaphoreType.DMA((cols // PIECE * (rows // SPAN),)),
            pltpu.SemaphoreType.DMA((levels,)),
        ],
        compiler_params=PARAMS,
    )(*far)


def middle_kernel(levels, rows, x_ref, m_ref, cs_ref, ss_ref, ct_ref, st_ref, o_ref):
    count, total, _ = x_ref.shape
    run = total // rows
    tgt_count = cs_ref.shape[0] // run
    for step, (apart, by_source) in enumerate(levels):
        source = x_ref if step == 0 else o_ref
        matrix, swapped = whole_matrix(m_ref[step])
        for col in range(run):
            own = slice(col * rows, (col + 1) * rows)

            def phase_of(index):
                if by_source:
                    at = index % tgt_count * run + col
                    row = (cs_ref[at : at + 1, :], ss_ref[at : at + 1, :])
                    return halved(jnp.broadcast_to(part, (rows, WIDE)) for part in row)
                at = index // tgt_count
                return halved((ct_ref[at], st_ref[at]))

            def store(index, value):
                o_ref[index, own, :] = value

            butterfly(
                lambda index: source[index, own, :],
                store,
                count,
                apart,
                matrix,
                swapped,
                phase_of,
                8,
            )


def middle_levels(x, matrices, src_tables, tgt_tables, levels):
    rows = tgt_tables[0].shape[1]
    return pl.pallas_call(
        functools.partial(middle_kernel, levels, rows),
        out_shape=jax.ShapeDtypeStruct(x.shape, x.dtype),
        in_specs=[VMEM] * 6,
        out_specs=VMEM,
        compiler_params=PARAMS,
    )(x, matrices, *src_tables, *tgt_tables)


def target_kernel(m_ref, c_ref, s_ref, x_ref, o_hbm, state_ref, o_ref, o_sems):
    cols, rows, _ = x_ref.shape
    levels = m_ref.shape[0]

    for level in range(levels):
        source = x_ref if level == 0 else state_ref
        weights = whole_matrix(m_ref[level])
        for start in range(0, rows, 16):
            own = slice(start, start + 16)
            cosine, sine = halved((c_ref[own, :], s_ref[own, :]))

            def store(index, value):
                state_ref[index, own, :] = value

            butterfly(
                lambda index: source[index, own, :],
                store,
                cols,
                1 << (levels - 1 - level),
                *weights,
                lambda index: (cosine, sine),
                32,
            )

    shuffle = shuffle_matrix()
    copies = []
    half = cols // 2
    for piece in range(rows // 16):
        for side in range(2):
            own = (pl.ds(piece * 16, 16), pl.ds(side * half, half))
            copies.append(
                pltpu.make_async_copy(o_ref.at[own], o_hbm.at[own], o_sems.at[len(copies)])
            )

            def store_block(first, second, block):
                o_ref[block_at(piece, side * half // 16 + second)] = block

            swap_axes(
                lambda first, second: state_ref[block_at(side * half // 16 + first, piece)],
                store_block,
                half // 16,
                1,
                shuffle,
            )
            copies[-1].start()
    for copy in copies:
        copy.wait()


def target_levels(x, matrices, angles):
    cols, rows, _ = x.shape
    shape = (rows, cols, WIDE)
    return pl.pallas_call(
        target_kernel,
        out_shape=jax.ShapeDtypeStruct(shape, x.dtype),
        in_specs=[VMEM] * 4,
        out_specs=FAR,
        scratch_shapes=[
            pltpu.VMEM(x.shape, x.dtype),
            pltpu.VMEM(shape, x.dtype),
            pltpu.SemaphoreType.DMA((rows // 8,)),
        ],
        compiler_params=PARAMS,
    )(matrices, *angles, x)


def gathered(values, axis):
    count = lax.axis_size(axis)
    place = lax.axis_index(axis)
    values = values[None]
    apart = 1
    while apart < count:
        other = lax.ppermute(values, axis, [(i, i ^ apart) for i in range(count)])
        mine_first = (place & apart) == 0
        values = jnp.concatenate(
            [jnp.where(mine_first, values, other), jnp.where(mine_first, other, values)]
        )
        apart *= 2
    return values


def local(box_weights, slowness, dip_field):
    rows, cols, _ = box_weights.shape
    src_count = lax.axis_size("src")
    tgt_count = lax.axis_size("tgt")
    devices = src_count * tgt_count
    row_bits, col_bits = rows.bit_length() - 1, cols.bit_length() - 1
    src_bits, tgt_bits = src_count.bit_length() - 1, tgt_count.bit_length() - 1
    first_target = row_bits + src_bits
    total = first_target + tgt_bits + col_bits
    matrices = [level_matrix(number) for number in range(total)]

    def matrices_of(low, high):
        return jnp.asarray(np.stack(matrices[low:high]))

    run = cols // devices
    place = lax.axis_index("src") * tgt_count + lax.axis_index("tgt")

    def traded(state):
        return lax.all_to_all(state, ("src", "tgt"), 0, 0, tiled=True)

    state = source_levels(box_weights, matrices_of(0, row_bits), slowness)

    state, slowness, dip_field = lax.optimization_barrier((state, slowness, dip_field))
    all_dip = gathered(dip_field, "src")
    all_slowness = gathered(slowness, "tgt")
    run_slowness = lax.dynamic_slice_in_dim(all_slowness, place * run, run, 1)

    state = state.reshape(devices, run * rows, WIDE)
    state = traded(state)
    levels = [(tgt_count << bit, True) for bit in range(src_bits)]
    levels += [(1 << bit, False) for bit in reversed(range(tgt_bits))]
    state = middle_levels(
        state,
        matrices_of(row_bits, first_target + tgt_bits),
        tables(run_slowness.reshape(-1)),
        tables(all_dip),
        levels,
    )
    state = traded(state)

    return target_levels(
        state.reshape(cols, rows, WIDE),
        matrices_of(first_target + tgt_bits, total),
        tables(dip_field),
    )


def solution(mesh):
    in_specs = (P("src", "tgt", None), P("tgt"), P("src"))
    out_specs = P("src", "tgt", None)
    return jax.shard_map(local, mesh=mesh, in_specs=in_specs, out_specs=out_specs, check_vma=False)
```

```python
import functools
import math

import jax
import jax.numpy as jnp
import ml_dtypes
import numpy as np
from jax import lax
from jax.experimental import pallas as pl
from jax.experimental.pallas import tpu as pltpu
from jax.sharding import PartitionSpec as P

HALF = 64
WIDE = 128


def nodes():
    points = np.cos((2.0 * np.arange(8) + 1.0) * (math.pi / 16.0))
    return np.repeat(points, 8), np.tile(points, 8)


def node_weights():
    first, second = nodes()
    return (first * first + second * second).astype(np.float32)


def level_matrix(number):
    first, second = nodes()
    frequency = 9.0 + 3.0 * (number % 5)
    shifts = np.array([-0.5, 0.5])
    out_first = first[None, :] + shifts[:, None]
    in_second = second[None, :] + shifts[:, None]
    inner = (
        out_first[:, None, :, None] * first[None, None, None, :]
        + second[None, None, :, None] * in_second[None, :, None, :]
    )
    out_norm = np.sqrt(out_first**2 + second[None, :] ** 2)
    in_norm = np.sqrt(first[None, :] ** 2 + in_second**2)
    phases = frequency * (inner + 0.5 * out_norm[:, None, :, None] * in_norm[None, :, None, :])
    factor = 1.0 / math.sqrt(128.0)
    real = np.transpose(factor * np.cos(phases), (1, 3, 0, 2))
    imag = np.transpose(factor * np.sin(phases), (1, 3, 0, 2))
    upper = np.concatenate([real, imag], axis=3)
    return upper.reshape(WIDE, 2 * WIDE).astype(ml_dtypes.bfloat16)


def tables(scales):
    weights = np.tile(node_weights(), 2)
    angles = scales[..., None] * weights
    signs = np.repeat(np.array([-1.0, 1.0], np.float32), HALF)
    return jnp.cos(angles), jnp.sin(angles) * signs


def shuffle_matrix():
    to = lax.broadcasted_iota(jnp.int32, (256, 256), 0)
    source = lax.broadcasted_iota(jnp.int32, (256, 256), 1)
    here = source == (to & 15) * 16 + (to >> 4)
    return jnp.where(here, 1.0, 0.0).astype(jnp.bfloat16)


def cos_sin(angles):
    turns = jnp.floor(angles * (2.0 / math.pi) + 0.5)
    rest = angles - turns * 1.5703125
    rest = rest - turns * 4.837512969970703125e-4
    rest = rest - turns * 7.54978995489188e-8
    square = rest * rest
    sine = 1.0 / 362880.0
    for factor in (-1.0 / 5040.0, 1.0 / 120.0, -1.0 / 6.0, 1.0):
        sine = sine * square + factor
    sine = sine * rest
    cosine = -1.0 / 3628800.0
    for factor in (1.0 / 40320.0, -1.0 / 720.0, 1.0 / 24.0, -0.5, 1.0):
        cosine = cosine * square + factor
    quarter = turns.astype(jnp.int32)
    odd = (quarter & 1) == 1
    first = jnp.where(odd, sine, cosine)
    second = jnp.where(odd, cosine, sine)
    first = jnp.where(((quarter + 1) & 2) == 2, -first, first)
    second = jnp.where((quarter & 2) == 2, -second, second)
    return first, second


def halved(table):
    return tuple(part.astype(jnp.bfloat16) for part in table)


def node_row():
    lanes = lax.broadcasted_iota(jnp.int32, (1, WIDE), 1) % HALF
    points = [math.cos((2 * a + 1) * math.pi / 16) ** 2 for a in range(4)]

    def square(at):
        near = jnp.minimum(at, 7 - at)
        value = jnp.full(near.shape, points[3], jnp.float32)
        for a in range(3):
            value = jnp.where(near == a, jnp.float32(points[a]), value)
        return value

    return square(lanes // 8) + square(lanes % 8)


def rotation(column):
    cosine, sine = cos_sin(column * node_row())
    lanes = lax.broadcasted_iota(jnp.int32, cosine.shape, 1)
    return cosine, jnp.where(lanes < HALF, -sine, sine)


def column_of(row, count):
    shape = (count, WIDE)
    here = lax.broadcasted_iota(jnp.int32, shape, 0) == lax.broadcasted_iota(jnp.int32, shape, 1)
    return jnp.sum(jnp.where(here, jnp.broadcast_to(row, shape), 0.0), axis=1, keepdims=True)


def whole_matrix(upper):
    parts = [upper[:, at : at + HALF] for at in (HALF, 0, 3 * HALF, 2 * HALF)]
    traded = jnp.concatenate(parts, axis=1)
    im_lane = (lax.broadcasted_iota(jnp.int32, upper.shape, 1) & HALF) != 0
    below = jnp.where(im_lane, traded, -traded)
    traded_below = jnp.where(im_lane, -upper, upper)

    def stacked(first, second):
        children = (slice(0, HALF), slice(HALF, WIDE))
        return jnp.concatenate([half[rows] for rows in children for half in (first, second)], axis=0)

    return stacked(upper, below), stacked(traded, traded_below)


def butterfly(load, store, count, apart, matrix, swapped, phase_of, group, turn=0):
    lows = [i for i in range(count) if not i & apart]
    for start in range(0, len(lows), group):
        picked = lows[start : start + group]
        left = jnp.concatenate([load(i) for i in picked], axis=0)
        right = jnp.concatenate([load(i + apart) for i in picked], axis=0)
        rows = left.shape[0] // len(picked)
        pair = jnp.concatenate([left, right], axis=1)
        both = jnp.dot(pair, matrix, preferred_element_type=jnp.float32).astype(jnp.bfloat16)
        if turn % 4 == 0:
            other = jnp.dot(pair, swapped, preferred_element_type=jnp.float32)
            other = other.astype(jnp.bfloat16)
        for place, low in enumerate(picked):
            for child in range(2):
                index = low + child * apart
                cosine, sine = phase_of(index)
                mine = slice(place * rows, (place + 1) * rows)
                own = slice(child * WIDE, (child + 1) * WIDE)
                value = both[mine, own]
                if turn % 4 == 0:
                    turned = other[mine, own]
                else:
                    turned = jnp.concatenate([value[:, HALF:], value[:, :HALF]], axis=1)
                store(index, value * cosine + turned * sine)
        turn += 1


def swap_axes(load, store, outer, inner, shuffle):
    for low in range(0, outer, 2):
        for at in range(inner):
            sides = [load(low + side, at).reshape(256, WIDE) for side in range(2)]
            moved = jnp.dot(
                shuffle, jnp.concatenate(sides, axis=1), preferred_element_type=jnp.float32
            ).astype(jnp.bfloat16)
            for side in range(2):
                block = moved[:, side * WIDE : (side + 1) * WIDE]
                store(at, low + side, block.reshape(16, 16, WIDE))


def block_at(first, second):
    return (slice(first * 16, first * 16 + 16), slice(second * 16, second * 16 + 16))


PIECE = 64
SPAN = 8
BLOCK = 32
VMEM = pl.BlockSpec(memory_space=pltpu.VMEM)
FAR = pl.BlockSpec(memory_space=pltpu.HBM)
PARAMS = pltpu.CompilerParams(vmem_limit_bytes=32 << 20)


def source_kernel(a_hbm, x_hbm, m_hbm, o_ref, a_ref, x_ref, m_ref, w_ref, a_sem, x_sems, m_sems):
    rows, cols, _ = x_ref.shape
    levels = m_ref.shape[0]
    a_copy = pltpu.make_async_copy(a_hbm, a_ref, a_sem)
    x_copies = []
    for piece in range(cols // PIECE):
        for at in range(0, rows, SPAN):
            own = (pl.ds(at, SPAN), pl.ds(piece * PIECE, PIECE))
            sem = x_sems.at[len(x_copies)]
            x_copies.append(pltpu.make_async_copy(x_hbm.at[own], x_ref.at[own], sem))
    m_copies = [
        pltpu.make_async_copy(m_hbm.at[i], m_ref.at[i], m_sems.at[i]) for i in range(levels)
    ]
    for copy in (a_copy, m_copies[0], *x_copies, *m_copies[1:]):
        copy.start()

    def expand(level):
        w_ref[2 * level], w_ref[2 * level + 1] = whole_matrix(m_ref[level])

    def level_on(level, begin):
        own = slice(begin, begin + BLOCK)

        def store(index, value):
            x_ref[index, own, :] = value

        butterfly(
            lambda index: x_ref[index, own, :],
            store,
            rows,
            1 << level,
            w_ref[2 * level],
            w_ref[2 * level + 1],
            lambda index: (cosines[own], sines[own]),
            8,
            begin // BLOCK * 2,
        )

    m_copies[0].wait()
    each = rows // SPAN
    for piece in range(cols // PIECE):
        for copy in x_copies[piece * each : (piece + 1) * each]:
            copy.wait()
        if piece == 0:
            a_copy.wait()
            expand(0)
            cosines, sines = halved(rotation(column_of(a_ref[...], cols)))
        for begin in range(piece * PIECE, (piece + 1) * PIECE, BLOCK):
            level_on(0, begin)
    for copy in m_copies[1:]:
        copy.wait()
    for level in range(1, levels):
        expand(level)
    for level in range(1, levels):
        for begin in range(0, cols, BLOCK):
            level_on(level, begin)

    def store_block(first, second, block):
        o_ref[block_at(first, second)] = block

    swap_axes(
        lambda first, second: x_ref[block_at(first, second)],
        store_block,
        rows // 16,
        cols // 16,
        shuffle_matrix(),
    )


def source_levels(x, matrices, slowness):
    rows, cols, _ = x.shape
    levels = matrices.shape[0]
    operands = (slowness[None, :], x, matrices)
    far = [pltpu.with_memory_space_constraint(value, pltpu.HBM) for value in operands]
    return pl.pallas_call(
        source_kernel,
        out_shape=jax.ShapeDtypeStruct((cols, rows, WIDE), x.dtype),
        in_specs=[FAR, FAR, FAR],
        out_specs=VMEM,
        scratch_shapes=[
            pltpu.VMEM((1, cols), jnp.float32),
            pltpu.VMEM(x.shape, x.dtype),
            pltpu.VMEM(matrices.shape, x.dtype),
            pltpu.VMEM((2 * levels, 2 * WIDE, 2 * WIDE), x.dtype),
            pltpu.SemaphoreType.DMA,
            pltpu.SemaphoreType.DMA((cols // PIECE * (rows // SPAN),)),
            pltpu.SemaphoreType.DMA((levels,)),
        ],
        compiler_params=PARAMS,
    )(*far)


def middle_kernel(levels, rows, x_ref, m_ref, cs_ref, ss_ref, ct_ref, st_ref, o_ref):
    count, total, _ = x_ref.shape
    run = total // rows
    tgt_count = cs_ref.shape[0] // run
    for step, (apart, by_source) in enumerate(levels):
        source = x_ref if step == 0 else o_ref
        matrix, swapped = whole_matrix(m_ref[step])
        for col in range(run):
            own = slice(col * rows, (col + 1) * rows)

            def phase_of(index):
                if by_source:
                    at = index % tgt_count * run + col
                    row = (cs_ref[at : at + 1, :], ss_ref[at : at + 1, :])
                    return halved(jnp.broadcast_to(part, (rows, WIDE)) for part in row)
                at = index // tgt_count
                return halved((ct_ref[at], st_ref[at]))

            def store(index, value):
                o_ref[index, own, :] = value

            butterfly(
                lambda index: source[index, own, :],
                store,
                count,
                apart,
                matrix,
                swapped,
                phase_of,
                8,
                col * 2,
            )


def middle_levels(x, matrices, src_tables, tgt_tables, levels):
    rows = tgt_tables[0].shape[1]
    return pl.pallas_call(
        functools.partial(middle_kernel, levels, rows),
        out_shape=jax.ShapeDtypeStruct(x.shape, x.dtype),
        in_specs=[VMEM] * 6,
        out_specs=VMEM,
        compiler_params=PARAMS,
    )(x, matrices, *src_tables, *tgt_tables)


def target_kernel(m_ref, c_ref, s_ref, x_ref, o_hbm, state_ref, o_ref, o_sems):
    cols, rows, _ = x_ref.shape
    levels = m_ref.shape[0]

    for level in range(levels):
        source = x_ref if level == 0 else state_ref
        weights = whole_matrix(m_ref[level])
        for start in range(0, rows, 16):
            own = slice(start, start + 16)
            cosine, sine = halved((c_ref[own, :], s_ref[own, :]))

            def store(index, value):
                state_ref[index, own, :] = value

            butterfly(
                lambda index: source[index, own, :],
                store,
                cols,
                1 << (levels - 1 - level),
                *weights,
                lambda index: (cosine, sine),
                16,
            )

    shuffle = shuffle_matrix()
    copies = []
    half = cols // 2
    for piece in range(rows // 16):
        for side in range(2):
            own = (pl.ds(piece * 16, 16), pl.ds(side * half, half))
            copies.append(
                pltpu.make_async_copy(o_ref.at[own], o_hbm.at[own], o_sems.at[len(copies)])
            )

            def store_block(first, second, block):
                o_ref[block_at(piece, side * half // 16 + second)] = block

            swap_axes(
                lambda first, second: state_ref[block_at(side * half // 16 + first, piece)],
                store_block,
                half // 16,
                1,
                shuffle,
            )
            copies[-1].start()
    for copy in copies:
        copy.wait()


def target_levels(x, matrices, angles):
    cols, rows, _ = x.shape
    shape = (rows, cols, WIDE)
    return pl.pallas_call(
        target_kernel,
        out_shape=jax.ShapeDtypeStruct(shape, x.dtype),
        in_specs=[VMEM] * 4,
        out_specs=FAR,
        scratch_shapes=[
            pltpu.VMEM(x.shape, x.dtype),
            pltpu.VMEM(shape, x.dtype),
            pltpu.SemaphoreType.DMA((rows // 8,)),
        ],
        compiler_params=PARAMS,
    )(matrices, *angles, x)


def gathered(values, axis):
    count = lax.axis_size(axis)
    place = lax.axis_index(axis)
    values = values[None]
    apart = 1
    while apart < count:
        other = lax.ppermute(values, axis, [(i, i ^ apart) for i in range(count)])
        mine_first = (place & apart) == 0
        values = jnp.concatenate(
            [jnp.where(mine_first, values, other), jnp.where(mine_first, other, values)]
        )
        apart *= 2
    return values


def local(box_weights, slowness, dip_field):
    rows, cols, _ = box_weights.shape
    src_count = lax.axis_size("src")
    tgt_count = lax.axis_size("tgt")
    devices = src_count * tgt_count
    row_bits, col_bits = rows.bit_length() - 1, cols.bit_length() - 1
    src_bits, tgt_bits = src_count.bit_length() - 1, tgt_count.bit_length() - 1
    first_target = row_bits + src_bits
    total = first_target + tgt_bits + col_bits
    matrices = [level_matrix(number) for number in range(total)]

    def matrices_of(low, high):
        return jnp.asarray(np.stack(matrices[low:high]))

    run = cols // devices
    place = lax.axis_index("src") * tgt_count + lax.axis_index("tgt")

    def traded(state):
        return lax.all_to_all(state, ("src", "tgt"), 0, 0, tiled=True)

    state = source_levels(box_weights, matrices_of(0, row_bits), slowness)

    state, slowness, dip_field = lax.optimization_barrier((state, slowness, dip_field))
    all_dip = gathered(dip_field, "src")
    all_slowness = gathered(slowness, "tgt")
    run_slowness = lax.dynamic_slice_in_dim(all_slowness, place * run, run, 1)

    state = state.reshape(devices, run * rows, WIDE)
    state = traded(state)
    levels = [(tgt_count << bit, True) for bit in range(src_bits)]
    levels += [(1 << bit, False) for bit in reversed(range(tgt_bits))]
    state = middle_levels(
        state,
        matrices_of(row_bits, first_target + tgt_bits),
        tables(run_slowness.reshape(-1)),
        tables(all_dip),
        levels,
    )
    state = traded(state)

    return target_levels(
        state.reshape(cols, rows, WIDE),
        matrices_of(first_target + tgt_bits, total),
        tables(dip_field),
    )


def solution(mesh):
    in_specs = (P("src", "tgt", None), P("tgt"), P("src"))
    out_specs = P("src", "tgt", None)
    return jax.shard_map(local, mesh=mesh, in_specs=in_specs, out_specs=out_specs, check_vma=False)
```

```python
import functools
import math

import jax
import jax.numpy as jnp
import ml_dtypes
import numpy as np
from jax import lax
from jax.experimental import pallas as pl
from jax.experimental.pallas import tpu as pltpu
from jax.sharding import PartitionSpec as P

HALF = 64
WIDE = 128


def nodes():
    points = np.cos((2.0 * np.arange(8) + 1.0) * (math.pi / 16.0))
    return np.repeat(points, 8), np.tile(points, 8)


def node_weights():
    first, second = nodes()
    return (first * first + second * second).astype(np.float32)


def level_matrix(number):
    first, second = nodes()
    frequency = 9.0 + 3.0 * (number % 5)
    shifts = np.array([-0.5, 0.5])
    out_first = first[None, :] + shifts[:, None]
    in_second = second[None, :] + shifts[:, None]
    inner = (
        out_first[:, None, :, None] * first[None, None, None, :]
        + second[None, None, :, None] * in_second[None, :, None, :]
    )
    out_norm = np.sqrt(out_first**2 + second[None, :] ** 2)
    in_norm = np.sqrt(first[None, :] ** 2 + in_second**2)
    phases = frequency * (inner + 0.5 * out_norm[:, None, :, None] * in_norm[None, :, None, :])
    factor = 1.0 / math.sqrt(128.0)
    real = np.transpose(factor * np.cos(phases), (1, 3, 0, 2))
    imag = np.transpose(factor * np.sin(phases), (1, 3, 0, 2))
    upper = np.concatenate([real, imag], axis=3)
    return upper.reshape(WIDE, 2 * WIDE).astype(ml_dtypes.bfloat16)


def tables(scales):
    weights = np.tile(node_weights(), 2)
    angles = scales[..., None] * weights
    signs = np.repeat(np.array([-1.0, 1.0], np.float32), HALF)
    return jnp.cos(angles), jnp.sin(angles) * signs


def shuffle_matrix():
    to = lax.broadcasted_iota(jnp.int32, (256, 256), 0)
    source = lax.broadcasted_iota(jnp.int32, (256, 256), 1)
    here = source == (to & 15) * 16 + (to >> 4)
    return jnp.where(here, 1.0, 0.0).astype(jnp.bfloat16)


def cos_sin(angles):
    turns = jnp.floor(angles * (2.0 / math.pi) + 0.5)
    rest = angles - turns * 1.5703125
    rest = rest - turns * 4.837512969970703125e-4
    rest = rest - turns * 7.54978995489188e-8
    square = rest * rest
    sine = 1.0 / 362880.0
    for factor in (-1.0 / 5040.0, 1.0 / 120.0, -1.0 / 6.0, 1.0):
        sine = sine * square + factor
    sine = sine * rest
    cosine = -1.0 / 3628800.0
    for factor in (1.0 / 40320.0, -1.0 / 720.0, 1.0 / 24.0, -0.5, 1.0):
        cosine = cosine * square + factor
    quarter = turns.astype(jnp.int32)
    odd = (quarter & 1) == 1
    first = jnp.where(odd, sine, cosine)
    second = jnp.where(odd, cosine, sine)
    first = jnp.where(((quarter + 1) & 2) == 2, -first, first)
    second = jnp.where((quarter & 2) == 2, -second, second)
    return first, second


def halved(table):
    return tuple(part.astype(jnp.bfloat16) for part in table)


def node_row():
    lanes = lax.broadcasted_iota(jnp.int32, (1, WIDE), 1) % HALF
    points = [math.cos((2 * a + 1) * math.pi / 16) ** 2 for a in range(4)]

    def square(at):
        near = jnp.minimum(at, 7 - at)
        value = jnp.full(near.shape, points[3], jnp.float32)
        for a in range(3):
            value = jnp.where(near == a, jnp.float32(points[a]), value)
        return value

    return square(lanes // 8) + square(lanes % 8)


def rotation(column):
    cosine, sine = cos_sin(column * node_row())
    lanes = lax.broadcasted_iota(jnp.int32, cosine.shape, 1)
    return cosine, jnp.where(lanes < HALF, -sine, sine)


def column_of(row, count):
    shape = (count, WIDE)
    here = lax.broadcasted_iota(jnp.int32, shape, 0) == lax.broadcasted_iota(jnp.int32, shape, 1)
    return jnp.sum(jnp.where(here, jnp.broadcast_to(row, shape), 0.0), axis=1, keepdims=True)


def whole_matrix(upper):
    parts = [upper[:, at : at + HALF] for at in (HALF, 0, 3 * HALF, 2 * HALF)]
    traded = jnp.concatenate(parts, axis=1)
    im_lane = (lax.broadcasted_iota(jnp.int32, upper.shape, 1) & HALF) != 0
    below = jnp.where(im_lane, traded, -traded)
    children = (slice(0, HALF), slice(HALF, WIDE))
    return jnp.concatenate([half[rows] for rows in children for half in (upper, below)], axis=0)


def butterfly(load, store, count, apart, matrix, phase_of, group):
    lows = [i for i in range(count) if not i & apart]
    for start in range(0, len(lows), group):
        picked = lows[start : start + group]
        left = jnp.concatenate([load(i) for i in picked], axis=0)
        right = jnp.concatenate([load(i + apart) for i in picked], axis=0)
        rows = left.shape[0] // len(picked)
        pair = jnp.concatenate([left, right], axis=1)
        both = jnp.dot(pair, matrix, preferred_element_type=jnp.float32).astype(jnp.bfloat16)
        for place, low in enumerate(picked):
            for child in range(2):
                index = low + child * apart
                cosine, sine = phase_of(index)
                value = both[
                    place * rows : (place + 1) * rows, child * WIDE : (child + 1) * WIDE
                ]
                turned = jnp.concatenate([value[:, HALF:], value[:, :HALF]], axis=1)
                store(index, value * cosine + turned * sine)


def swap_axes(load, store, outer, inner, shuffle):
    for low in range(0, outer, 2):
        for at in range(inner):
            sides = [load(low + side, at).reshape(256, WIDE) for side in range(2)]
            moved = jnp.dot(
                shuffle, jnp.concatenate(sides, axis=1), preferred_element_type=jnp.float32
            ).astype(jnp.bfloat16)
            for side in range(2):
                block = moved[:, side * WIDE : (side + 1) * WIDE]
                store(at, low + side, block.reshape(16, 16, WIDE))


def block_at(first, second):
    return (slice(first * 16, first * 16 + 16), slice(second * 16, second * 16 + 16))


PIECE = 64
SPAN = 8
BLOCK = 32
VMEM = pl.BlockSpec(memory_space=pltpu.VMEM)
FAR = pl.BlockSpec(memory_space=pltpu.HBM)
PARAMS = pltpu.CompilerParams(vmem_limit_bytes=32 << 20)


def source_kernel(a_hbm, x_hbm, m_hbm, o_ref, a_ref, x_ref, m_ref, w_ref, a_sem, x_sems, m_sems):
    rows, cols, _ = x_ref.shape
    levels = m_ref.shape[0]
    a_copy = pltpu.make_async_copy(a_hbm, a_ref, a_sem)
    x_copies = []
    for piece in range(cols // PIECE):
        for at in range(0, rows, SPAN):
            own = (pl.ds(at, SPAN), pl.ds(piece * PIECE, PIECE))
            sem = x_sems.at[len(x_copies)]
            x_copies.append(pltpu.make_async_copy(x_hbm.at[own], x_ref.at[own], sem))
    m_copies = [
        pltpu.make_async_copy(m_hbm.at[i], m_ref.at[i], m_sems.at[i]) for i in range(levels)
    ]
    for copy in (a_copy, m_copies[0], *x_copies, *m_copies[1:]):
        copy.start()

    def expand(level):
        w_ref[level] = whole_matrix(m_ref[level])

    def level_on(level, begin):
        own = slice(begin, begin + BLOCK)

        def store(index, value):
            x_ref[index, own, :] = value

        butterfly(
            lambda index: x_ref[index, own, :],
            store,
            rows,
            1 << level,
            w_ref[level],
            lambda index: (cosines[own], sines[own]),
            8,
        )

    m_copies[0].wait()
    each = rows // SPAN
    for piece in range(cols // PIECE):
        for copy in x_copies[piece * each : (piece + 1) * each]:
            copy.wait()
        if piece == 0:
            a_copy.wait()
            expand(0)
            cosines, sines = halved(rotation(column_of(a_ref[...], cols)))
        for begin in range(piece * PIECE, (piece + 1) * PIECE, BLOCK):
            level_on(0, begin)
    for copy in m_copies[1:]:
        copy.wait()
    for level in range(1, levels):
        expand(level)
    for level in range(1, levels):
        for begin in range(0, cols, BLOCK):
            level_on(level, begin)

    def store_block(first, second, block):
        o_ref[block_at(first, second)] = block

    swap_axes(
        lambda first, second: x_ref[block_at(first, second)],
        store_block,
        rows // 16,
        cols // 16,
        shuffle_matrix(),
    )


def source_levels(x, matrices, slowness):
    rows, cols, _ = x.shape
    levels = matrices.shape[0]
    operands = (slowness[None, :], x, matrices)
    far = [pltpu.with_memory_space_constraint(value, pltpu.HBM) for value in operands]
    return pl.pallas_call(
        source_kernel,
        out_shape=jax.ShapeDtypeStruct((cols, rows, WIDE), x.dtype),
        in_specs=[FAR, FAR, FAR],
        out_specs=VMEM,
        scratch_shapes=[
            pltpu.VMEM((1, cols), jnp.float32),
            pltpu.VMEM(x.shape, x.dtype),
            pltpu.VMEM(matrices.shape, x.dtype),
            pltpu.VMEM((levels, 2 * WIDE, 2 * WIDE), x.dtype),
            pltpu.SemaphoreType.DMA,
            pltpu.SemaphoreType.DMA((cols // PIECE * (rows // SPAN),)),
            pltpu.SemaphoreType.DMA((levels,)),
        ],
        compiler_params=PARAMS,
    )(*far)


def middle_kernel(levels, rows, x_ref, m_ref, cs_ref, ss_ref, ct_ref, st_ref, o_ref):
    count, total, _ = x_ref.shape
    run = total // rows
    tgt_count = cs_ref.shape[0] // run
    for step, (apart, by_source) in enumerate(levels):
        source = x_ref if step == 0 else o_ref
        matrix = whole_matrix(m_ref[step])
        for col in range(run):
            own = slice(col * rows, (col + 1) * rows)

            def phase_of(index):
                if by_source:
                    at = index % tgt_count * run + col
                    row = (cs_ref[at : at + 1, :], ss_ref[at : at + 1, :])
                    return halved(jnp.broadcast_to(part, (rows, WIDE)) for part in row)
                at = index // tgt_count
                return halved((ct_ref[at], st_ref[at]))

            def store(index, value):
                o_ref[index, own, :] = value

            butterfly(
                lambda index: source[index, own, :],
                store,
                count,
                apart,
                matrix,
                phase_of,
                8,
            )


def middle_levels(x, matrices, src_tables, tgt_tables, levels):
    rows = tgt_tables[0].shape[1]
    return pl.pallas_call(
        functools.partial(middle_kernel, levels, rows),
        out_shape=jax.ShapeDtypeStruct(x.shape, x.dtype),
        in_specs=[VMEM] * 6,
        out_specs=VMEM,
        compiler_params=PARAMS,
    )(x, matrices, *src_tables, *tgt_tables)


def target_kernel(m_ref, c_ref, s_ref, x_ref, o_hbm, state_ref, o_ref, o_sems):
    cols, rows, _ = x_ref.shape
    levels = m_ref.shape[0]

    for level in range(levels):
        source = x_ref if level == 0 else state_ref
        matrix = whole_matrix(m_ref[level])
        for start in range(0, rows, 16):
            own = slice(start, start + 16)
            cosine, sine = halved((c_ref[own, :], s_ref[own, :]))

            def store(index, value):
                state_ref[index, own, :] = value

            butterfly(
                lambda index: source[index, own, :],
                store,
                cols,
                1 << (levels - 1 - level),
                matrix,
                lambda index: (cosine, sine),
                16,
            )

    shuffle = shuffle_matrix()
    copies = []
    half = cols // 2
    for piece in range(rows // 16):
        for side in range(2):
            own = (pl.ds(piece * 16, 16), pl.ds(side * half, half))
            copies.append(
                pltpu.make_async_copy(o_ref.at[own], o_hbm.at[own], o_sems.at[len(copies)])
            )

            def store_block(first, second, block):
                o_ref[block_at(piece, side * half // 16 + second)] = block

            swap_axes(
                lambda first, second: state_ref[block_at(side * half // 16 + first, piece)],
                store_block,
                half // 16,
                1,
                shuffle,
            )
            copies[-1].start()
    for copy in copies:
        copy.wait()


def target_levels(x, matrices, angles):
    cols, rows, _ = x.shape
    shape = (rows, cols, WIDE)
    return pl.pallas_call(
        target_kernel,
        out_shape=jax.ShapeDtypeStruct(shape, x.dtype),
        in_specs=[VMEM] * 4,
        out_specs=FAR,
        scratch_shapes=[
            pltpu.VMEM(x.shape, x.dtype),
            pltpu.VMEM(shape, x.dtype),
            pltpu.SemaphoreType.DMA((rows // 8,)),
        ],
        compiler_params=PARAMS,
    )(matrices, *angles, x)


def gathered(values, axis):
    count = lax.axis_size(axis)
    place = lax.axis_index(axis)
    values = values[None]
    apart = 1
    while apart < count:
        other = lax.ppermute(values, axis, [(i, i ^ apart) for i in range(count)])
        mine_first = (place & apart) == 0
        values = jnp.concatenate(
            [jnp.where(mine_first, values, other), jnp.where(mine_first, other, values)]
        )
        apart *= 2
    return values


def local(box_weights, slowness, dip_field):
    rows, cols, _ = box_weights.shape
    src_count = lax.axis_size("src")
    tgt_count = lax.axis_size("tgt")
    devices = src_count * tgt_count
    row_bits, col_bits = rows.bit_length() - 1, cols.bit_length() - 1
    src_bits, tgt_bits = src_count.bit_length() - 1, tgt_count.bit_length() - 1
    first_target = row_bits + src_bits
    total = first_target + tgt_bits + col_bits
    matrices = [level_matrix(number) for number in range(total)]

    def matrices_of(low, high):
        return jnp.asarray(np.stack(matrices[low:high]))

    run = cols // devices
    place = lax.axis_index("src") * tgt_count + lax.axis_index("tgt")

    def traded(state):
        return lax.all_to_all(state, ("src", "tgt"), 0, 0, tiled=True)

    state = source_levels(box_weights, matrices_of(0, row_bits), slowness)

    state, slowness, dip_field = lax.optimization_barrier((state, slowness, dip_field))
    all_dip = gathered(dip_field, "src")
    all_slowness = gathered(slowness, "tgt")
    run_slowness = lax.dynamic_slice_in_dim(all_slowness, place * run, run, 1)

    state = state.reshape(devices, run * rows, WIDE)
    state = traded(state)
    levels = [(tgt_count << bit, True) for bit in range(src_bits)]
    levels += [(1 << bit, False) for bit in reversed(range(tgt_bits))]
    state = middle_levels(
        state,
        matrices_of(row_bits, first_target + tgt_bits),
        tables(run_slowness.reshape(-1)),
        tables(all_dip),
        levels,
    )
    state = traded(state)

    return target_levels(
        state.reshape(cols, rows, WIDE),
        matrices_of(first_target + tgt_bits, total),
        tables(dip_field),
    )


def solution(mesh):
    in_specs = (P("src", "tgt", None), P("tgt"), P("src"))
    out_specs = P("src", "tgt", None)
    return jax.shard_map(local, mesh=mesh, in_specs=in_specs, out_specs=out_specs, check_vma=False)
```

```python
import functools
import math

import jax
import jax.numpy as jnp
import ml_dtypes
import numpy as np
from jax import lax
from jax.experimental import pallas as pl
from jax.experimental.pallas import tpu as pltpu
from jax.sharding import PartitionSpec as P

HALF = 64
WIDE = 128


def nodes():
    points = np.cos((2.0 * np.arange(8) + 1.0) * (math.pi / 16.0))
    return np.repeat(points, 8), np.tile(points, 8)


def node_weights():
    first, second = nodes()
    return (first * first + second * second).astype(np.float32)


def level_matrix(number):
    first, second = nodes()
    frequency = 9.0 + 3.0 * (number % 5)
    shifts = np.array([-0.5, 0.5])
    out_first = first[None, :] + shifts[:, None]
    in_second = second[None, :] + shifts[:, None]
    inner = (
        out_first[:, None, :, None] * first[None, None, None, :]
        + second[None, None, :, None] * in_second[None, :, None, :]
    )
    out_norm = np.sqrt(out_first**2 + second[None, :] ** 2)
    in_norm = np.sqrt(first[None, :] ** 2 + in_second**2)
    phases = frequency * (inner + 0.5 * out_norm[:, None, :, None] * in_norm[None, :, None, :])
    factor = 1.0 / math.sqrt(128.0)
    real = np.transpose(factor * np.cos(phases), (1, 3, 0, 2))
    imag = np.transpose(factor * np.sin(phases), (1, 3, 0, 2))
    upper = np.concatenate([real, imag], axis=3)
    return upper.reshape(WIDE, 2 * WIDE).astype(ml_dtypes.bfloat16)


def tables(scales):
    weights = np.tile(node_weights(), 2)
    angles = scales[..., None] * weights
    signs = np.repeat(np.array([-1.0, 1.0], np.float32), HALF)
    return jnp.cos(angles), jnp.sin(angles) * signs


def shuffle_matrix():
    to = lax.broadcasted_iota(jnp.int32, (256, 256), 0)
    source = lax.broadcasted_iota(jnp.int32, (256, 256), 1)
    here = source == (to & 15) * 16 + (to >> 4)
    return jnp.where(here, 1.0, 0.0).astype(jnp.bfloat16)


def cos_sin(angles):
    turns = jnp.floor(angles * (2.0 / math.pi) + 0.5)
    rest = angles - turns * 1.5703125
    rest = rest - turns * 4.837512969970703125e-4
    rest = rest - turns * 7.54978995489188e-8
    square = rest * rest
    sine = 1.0 / 362880.0
    for factor in (-1.0 / 5040.0, 1.0 / 120.0, -1.0 / 6.0, 1.0):
        sine = sine * square + factor
    sine = sine * rest
    cosine = -1.0 / 3628800.0
    for factor in (1.0 / 40320.0, -1.0 / 720.0, 1.0 / 24.0, -0.5, 1.0):
        cosine = cosine * square + factor
    quarter = turns.astype(jnp.int32)
    odd = (quarter & 1) == 1
    first = jnp.where(odd, sine, cosine)
    second = jnp.where(odd, cosine, sine)
    first = jnp.where(((quarter + 1) & 2) == 2, -first, first)
    second = jnp.where((quarter & 2) == 2, -second, second)
    return first, second


def halved(table):
    return tuple(part.astype(jnp.bfloat16) for part in table)


def node_row():
    lanes = lax.broadcasted_iota(jnp.int32, (1, WIDE), 1) % HALF
    points = [math.cos((2 * a + 1) * math.pi / 16) ** 2 for a in range(4)]

    def square(at):
        near = jnp.minimum(at, 7 - at)
        value = jnp.full(near.shape, points[3], jnp.float32)
        for a in range(3):
            value = jnp.where(near == a, jnp.float32(points[a]), value)
        return value

    return square(lanes // 8) + square(lanes % 8)


def rotation(column):
    cosine, sine = cos_sin(column * node_row())
    lanes = lax.broadcasted_iota(jnp.int32, cosine.shape, 1)
    return cosine, jnp.where(lanes < HALF, -sine, sine)


def column_of(row, count):
    shape = (count, WIDE)
    here = lax.broadcasted_iota(jnp.int32, shape, 0) == lax.broadcasted_iota(jnp.int32, shape, 1)
    return jnp.sum(jnp.where(here, jnp.broadcast_to(row, shape), 0.0), axis=1, keepdims=True)


def whole_matrix(upper):
    parts = [upper[:, at : at + HALF] for at in (HALF, 0, 3 * HALF, 2 * HALF)]
    traded = jnp.concatenate(parts, axis=1)
    im_lane = (lax.broadcasted_iota(jnp.int32, upper.shape, 1) & HALF) != 0
    below = jnp.where(im_lane, traded, -traded)
    children = (slice(0, HALF), slice(HALF, WIDE))
    return jnp.concatenate([half[rows] for rows in children for half in (upper, below)], axis=0)


def whole_matrices(uppers):
    upper = np.stack(uppers).astype(np.float32).reshape(-1, 2, HALF, 2, 2, HALF)
    below = np.stack([-upper[:, :, :, :, 1], upper[:, :, :, :, 0]], axis=4)
    both = np.concatenate([upper, below], axis=2)
    return jnp.asarray(both.reshape(-1, 2 * WIDE, 2 * WIDE).astype(ml_dtypes.bfloat16))


def butterfly(load, store, count, apart, matrix, phase_of, group):
    lows = [i for i in range(count) if not i & apart]
    for start in range(0, len(lows), group):
        picked = lows[start : start + group]
        left = jnp.concatenate([load(i) for i in picked], axis=0)
        right = jnp.concatenate([load(i + apart) for i in picked], axis=0)
        rows = left.shape[0] // len(picked)
        pair = jnp.concatenate([left, right], axis=1)
        both = jnp.dot(pair, matrix, preferred_element_type=jnp.float32).astype(jnp.bfloat16)
        for place, low in enumerate(picked):
            for child in range(2):
                index = low + child * apart
                cosine, sine = phase_of(index)
                value = both[
                    place * rows : (place + 1) * rows, child * WIDE : (child + 1) * WIDE
                ]
                turned = jnp.concatenate([value[:, HALF:], value[:, :HALF]], axis=1)
                store(index, value * cosine + turned * sine)


def swap_axes(load, store, outer, inner, shuffle):
    for low in range(0, outer, 2):
        for at in range(inner):
            sides = [load(low + side, at).reshape(256, WIDE) for side in range(2)]
            moved = jnp.dot(
                shuffle, jnp.concatenate(sides, axis=1), preferred_element_type=jnp.float32
            ).astype(jnp.bfloat16)
            for side in range(2):
                block = moved[:, side * WIDE : (side + 1) * WIDE]
                store(at, low + side, block.reshape(16, 16, WIDE))


def block_at(first, second):
    return (slice(first * 16, first * 16 + 16), slice(second * 16, second * 16 + 16))


PIECE = 64
SPAN = 8
BLOCK = 32
VMEM = pl.BlockSpec(memory_space=pltpu.VMEM)
FAR = pl.BlockSpec(memory_space=pltpu.HBM)
PARAMS = pltpu.CompilerParams(vmem_limit_bytes=32 << 20)


def source_kernel(a_hbm, x_hbm, m_hbm, o_ref, a_ref, x_ref, m_ref, w_ref, a_sem, x_sems, m_sems):
    rows, cols, _ = x_ref.shape
    levels = m_ref.shape[0]
    a_copy = pltpu.make_async_copy(a_hbm, a_ref, a_sem)
    x_copies = []
    for piece in range(cols // PIECE):
        for at in range(0, rows, SPAN):
            own = (pl.ds(at, SPAN), pl.ds(piece * PIECE, PIECE))
            sem = x_sems.at[len(x_copies)]
            x_copies.append(pltpu.make_async_copy(x_hbm.at[own], x_ref.at[own], sem))
    m_copies = [
        pltpu.make_async_copy(m_hbm.at[i], m_ref.at[i], m_sems.at[i]) for i in range(levels)
    ]
    for copy in (a_copy, m_copies[0], *x_copies, *m_copies[1:]):
        copy.start()

    def expand(level):
        w_ref[level] = whole_matrix(m_ref[level])

    def level_on(level, begin):
        own = slice(begin, begin + BLOCK)

        def store(index, value):
            x_ref[index, own, :] = value

        butterfly(
            lambda index: x_ref[index, own, :],
            store,
            rows,
            1 << level,
            w_ref[level],
            lambda index: (cosines[own], sines[own]),
            8,
        )

    shuffle = shuffle_matrix()
    m_copies[0].wait()
    each = rows // SPAN
    for piece in range(cols // PIECE):
        for copy in x_copies[piece * each : (piece + 1) * each]:
            copy.wait()
        if piece == 0:
            a_copy.wait()
            expand(0)
            cosines, sines = halved(rotation(column_of(a_ref[...], cols)))
        for begin in range(piece * PIECE, (piece + 1) * PIECE, BLOCK):
            level_on(0, begin)
    for copy in m_copies[1:]:
        copy.wait()
    for level in range(1, levels):
        expand(level)
    for level in range(1, levels):
        for begin in range(0, cols, BLOCK):
            level_on(level, begin)

    def store_block(first, second, block):
        o_ref[block_at(first, second)] = block

    swap_axes(
        lambda first, second: x_ref[block_at(first, second)],
        store_block,
        rows // 16,
        cols // 16,
        shuffle,
    )


def source_levels(x, matrices, slowness):
    rows, cols, _ = x.shape
    levels = matrices.shape[0]
    operands = (slowness[None, :], x, matrices)
    far = [pltpu.with_memory_space_constraint(value, pltpu.HBM) for value in operands]
    return pl.pallas_call(
        source_kernel,
        out_shape=jax.ShapeDtypeStruct((cols, rows, WIDE), x.dtype),
        in_specs=[FAR, FAR, FAR],
        out_specs=VMEM,
        scratch_shapes=[
            pltpu.VMEM((1, cols), jnp.float32),
            pltpu.VMEM(x.shape, x.dtype),
            pltpu.VMEM(matrices.shape, x.dtype),
            pltpu.VMEM((levels, 2 * WIDE, 2 * WIDE), x.dtype),
            pltpu.SemaphoreType.DMA,
            pltpu.SemaphoreType.DMA((cols // PIECE * (rows // SPAN),)),
            pltpu.SemaphoreType.DMA((levels,)),
        ],
        compiler_params=PARAMS,
    )(*far)


def middle_kernel(levels, rows, x_ref, m_ref, cs_ref, ss_ref, ct_ref, st_ref, o_ref):
    count, total, _ = x_ref.shape
    run = total // rows
    tgt_count = cs_ref.shape[0] // run
    for step, (apart, by_source) in enumerate(levels):
        source = x_ref if step == 0 else o_ref
        matrix = m_ref[step]
        for col in range(run):
            own = slice(col * rows, (col + 1) * rows)

            def phase_of(index):
                if by_source:
                    at = index % tgt_count * run + col
                    row = (cs_ref[at : at + 1, :], ss_ref[at : at + 1, :])
                    return halved(jnp.broadcast_to(part, (rows, WIDE)) for part in row)
                at = index // tgt_count
                return halved((ct_ref[at], st_ref[at]))

            def store(index, value):
                o_ref[index, own, :] = value

            butterfly(
                lambda index: source[index, own, :],
                store,
                count,
                apart,
                matrix,
                phase_of,
                8,
            )


def middle_levels(x, matrices, src_tables, tgt_tables, levels):
    rows = tgt_tables[0].shape[1]
    return pl.pallas_call(
        functools.partial(middle_kernel, levels, rows),
        out_shape=jax.ShapeDtypeStruct(x.shape, x.dtype),
        in_specs=[VMEM] * 6,
        out_specs=VMEM,
        compiler_params=PARAMS,
    )(x, matrices, *src_tables, *tgt_tables)


def target_kernel(m_ref, c_ref, s_ref, x_ref, o_hbm, state_ref, o_ref, o_sems):
    cols, rows, _ = x_ref.shape
    levels = m_ref.shape[0]

    for level in range(levels):
        source = x_ref if level == 0 else state_ref
        matrix = m_ref[level]
        for start in range(0, rows, 16):
            own = slice(start, start + 16)
            cosine, sine = halved((c_ref[own, :], s_ref[own, :]))

            def store(index, value):
                state_ref[index, own, :] = value

            butterfly(
                lambda index: source[index, own, :],
                store,
                cols,
                1 << (levels - 1 - level),
                matrix,
                lambda index: (cosine, sine),
                16,
            )

    shuffle = shuffle_matrix()
    copies = []
    half = cols // 2
    for piece in range(rows // 16):
        for side in range(2):
            own = (pl.ds(piece * 16, 16), pl.ds(side * half, half))
            copies.append(
                pltpu.make_async_copy(o_ref.at[own], o_hbm.at[own], o_sems.at[len(copies)])
            )

            def store_block(first, second, block):
                o_ref[block_at(piece, side * half // 16 + second)] = block

            swap_axes(
                lambda first, second: state_ref[block_at(side * half // 16 + first, piece)],
                store_block,
                half // 16,
                1,
                shuffle,
            )
            copies[-1].start()
    for copy in copies:
        copy.wait()


def target_levels(x, matrices, angles):
    cols, rows, _ = x.shape
    shape = (rows, cols, WIDE)
    return pl.pallas_call(
        target_kernel,
        out_shape=jax.ShapeDtypeStruct(shape, x.dtype),
        in_specs=[VMEM] * 4,
        out_specs=FAR,
        scratch_shapes=[
            pltpu.VMEM(x.shape, x.dtype),
            pltpu.VMEM(shape, x.dtype),
            pltpu.SemaphoreType.DMA((rows // 8,)),
        ],
        compiler_params=PARAMS,
    )(matrices, *angles, x)


def gathered(values, axis):
    count = lax.axis_size(axis)
    place = lax.axis_index(axis)
    values = values[None]
    apart = 1
    while apart < count:
        other = lax.ppermute(values, axis, [(i, i ^ apart) for i in range(count)])
        mine_first = (place & apart) == 0
        values = jnp.concatenate(
            [jnp.where(mine_first, values, other), jnp.where(mine_first, other, values)]
        )
        apart *= 2
    return values


def local(box_weights, slowness, dip_field):
    rows, cols, _ = box_weights.shape
    src_count = lax.axis_size("src")
    tgt_count = lax.axis_size("tgt")
    devices = src_count * tgt_count
    row_bits, col_bits = rows.bit_length() - 1, cols.bit_length() - 1
    src_bits, tgt_bits = src_count.bit_length() - 1, tgt_count.bit_length() - 1
    first_target = row_bits + src_bits
    total = first_target + tgt_bits + col_bits
    matrices = [level_matrix(number) for number in range(total)]

    run = cols // devices
    place = lax.axis_index("src") * tgt_count + lax.axis_index("tgt")

    def traded(state):
        return lax.all_to_all(state, ("src", "tgt"), 0, 0, tiled=True)

    state = source_levels(box_weights, jnp.asarray(np.stack(matrices[:row_bits])), slowness)

    state, slowness, dip_field = lax.optimization_barrier((state, slowness, dip_field))
    all_dip = gathered(dip_field, "src")
    all_slowness = gathered(slowness, "tgt")
    run_slowness = lax.dynamic_slice_in_dim(all_slowness, place * run, run, 1)

    state = state.reshape(devices, run * rows, WIDE)
    state = traded(state)
    levels = [(tgt_count << bit, True) for bit in range(src_bits)]
    levels += [(1 << bit, False) for bit in reversed(range(tgt_bits))]
    state = middle_levels(
        state,
        whole_matrices(matrices[row_bits : first_target + tgt_bits]),
        tables(run_slowness.reshape(-1)),
        tables(all_dip),
        levels,
    )
    state = traded(state)

    return target_levels(
        state.reshape(cols, rows, WIDE),
        whole_matrices(matrices[first_target + tgt_bits :]),
        tables(dip_field),
    )


def solution(mesh):
    in_specs = (P("src", "tgt", None), P("tgt"), P("src"))
    out_specs = P("src", "tgt", None)
    return jax.shard_map(local, mesh=mesh, in_specs=in_specs, out_specs=out_specs, check_vma=False)
```

```python
import functools
import math

import jax
import jax.numpy as jnp
import ml_dtypes
import numpy as np
from jax import lax
from jax.experimental import pallas as pl
from jax.experimental.pallas import tpu as pltpu
from jax.sharding import PartitionSpec as P

HALF = 64
WIDE = 128


def nodes():
    points = np.cos((2.0 * np.arange(8) + 1.0) * (math.pi / 16.0))
    return np.repeat(points, 8), np.tile(points, 8)


def node_weights():
    first, second = nodes()
    return (first * first + second * second).astype(np.float32)


def level_matrix(number):
    first, second = nodes()
    frequency = 9.0 + 3.0 * (number % 5)
    shifts = np.array([-0.5, 0.5])
    out_first = first[None, :] + shifts[:, None]
    in_second = second[None, :] + shifts[:, None]
    inner = (
        out_first[:, None, :, None] * first[None, None, None, :]
        + second[None, None, :, None] * in_second[None, :, None, :]
    )
    out_norm = np.sqrt(out_first**2 + second[None, :] ** 2)
    in_norm = np.sqrt(first[None, :] ** 2 + in_second**2)
    phases = frequency * (inner + 0.5 * out_norm[:, None, :, None] * in_norm[None, :, None, :])
    factor = 1.0 / math.sqrt(128.0)
    real = np.transpose(factor * np.cos(phases), (1, 3, 0, 2))
    imag = np.transpose(factor * np.sin(phases), (1, 3, 0, 2))
    upper = np.concatenate([real, imag], axis=3)
    return upper.reshape(WIDE, 2 * WIDE).astype(ml_dtypes.bfloat16)


def tables(scales):
    weights = np.tile(node_weights(), 2)
    angles = scales[..., None] * weights
    signs = np.repeat(np.array([-1.0, 1.0], np.float32), HALF)
    return jnp.cos(angles), jnp.sin(angles) * signs


def shuffle_matrix():
    to = lax.broadcasted_iota(jnp.int32, (256, 256), 0)
    source = lax.broadcasted_iota(jnp.int32, (256, 256), 1)
    here = source == (to & 15) * 16 + (to >> 4)
    return jnp.where(here, 1.0, 0.0).astype(jnp.bfloat16)


def cos_sin(angles):
    turns = jnp.floor(angles * (2.0 / math.pi) + 0.5)
    rest = angles - turns * 1.5703125
    rest = rest - turns * 4.837512969970703125e-4
    rest = rest - turns * 7.54978995489188e-8
    square = rest * rest
    sine = 1.0 / 362880.0
    for factor in (-1.0 / 5040.0, 1.0 / 120.0, -1.0 / 6.0, 1.0):
        sine = sine * square + factor
    sine = sine * rest
    cosine = -1.0 / 3628800.0
    for factor in (1.0 / 40320.0, -1.0 / 720.0, 1.0 / 24.0, -0.5, 1.0):
        cosine = cosine * square + factor
    quarter = turns.astype(jnp.int32)
    odd = (quarter & 1) == 1
    first = jnp.where(odd, sine, cosine)
    second = jnp.where(odd, cosine, sine)
    first = jnp.where(((quarter + 1) & 2) == 2, -first, first)
    second = jnp.where((quarter & 2) == 2, -second, second)
    return first, second


def halved(table):
    return tuple(part.astype(jnp.bfloat16) for part in table)


def node_row():
    lanes = lax.broadcasted_iota(jnp.int32, (1, WIDE), 1) % HALF
    points = [math.cos((2 * a + 1) * math.pi / 16) ** 2 for a in range(4)]

    def square(at):
        near = jnp.minimum(at, 7 - at)
        value = jnp.full(near.shape, points[3], jnp.float32)
        for a in range(3):
            value = jnp.where(near == a, jnp.float32(points[a]), value)
        return value

    return square(lanes // 8) + square(lanes % 8)


def rotation(column):
    cosine, sine = cos_sin(column * node_row())
    lanes = lax.broadcasted_iota(jnp.int32, cosine.shape, 1)
    return cosine, jnp.where(lanes < HALF, -sine, sine)


def column_of(row, count):
    shape = (count, WIDE)
    here = lax.broadcasted_iota(jnp.int32, shape, 0) == lax.broadcasted_iota(jnp.int32, shape, 1)
    return jnp.sum(jnp.where(here, jnp.broadcast_to(row, shape), 0.0), axis=1, keepdims=True)


def whole_matrix(upper):
    parts = [upper[:, at : at + HALF] for at in (HALF, 0, 3 * HALF, 2 * HALF)]
    traded = jnp.concatenate(parts, axis=1)
    im_lane = (lax.broadcasted_iota(jnp.int32, upper.shape, 1) & HALF) != 0
    below = jnp.where(im_lane, traded, -traded)
    children = (slice(0, HALF), slice(HALF, WIDE))
    return jnp.concatenate([half[rows] for rows in children for half in (upper, below)], axis=0)


def whole_matrices(uppers):
    upper = np.stack(uppers).astype(np.float32).reshape(-1, 2, HALF, 2, 2, HALF)
    below = np.stack([-upper[:, :, :, :, 1], upper[:, :, :, :, 0]], axis=4)
    both = np.concatenate([upper, below], axis=2)
    return jnp.asarray(both.reshape(-1, 2 * WIDE, 2 * WIDE).astype(ml_dtypes.bfloat16))


def butterfly(load, store, count, apart, matrix, phase_of, group):
    lows = [i for i in range(count) if not i & apart]
    for start in range(0, len(lows), group):
        picked = lows[start : start + group]
        left = jnp.concatenate([load(i) for i in picked], axis=0)
        right = jnp.concatenate([load(i + apart) for i in picked], axis=0)
        rows = left.shape[0] // len(picked)
        pair = jnp.concatenate([left, right], axis=1)
        both = jnp.dot(pair, matrix, preferred_element_type=jnp.float32).astype(jnp.bfloat16)
        for place, low in enumerate(picked):
            for child in range(2):
                index = low + child * apart
                cosine, sine = phase_of(index)
                value = both[
                    place * rows : (place + 1) * rows, child * WIDE : (child + 1) * WIDE
                ]
                turned = jnp.concatenate([value[:, HALF:], value[:, :HALF]], axis=1)
                store(index, value * cosine + turned * sine)


def swap_axes(load, store, outer, inner, shuffle):
    for low in range(0, outer, 2):
        for at in range(inner):
            sides = [load(low + side, at).reshape(256, WIDE) for side in range(2)]
            moved = jnp.dot(
                shuffle, jnp.concatenate(sides, axis=1), preferred_element_type=jnp.float32
            ).astype(jnp.bfloat16)
            for side in range(2):
                block = moved[:, side * WIDE : (side + 1) * WIDE]
                store(at, low + side, block.reshape(16, 16, WIDE))


def block_at(first, second):
    return (slice(first * 16, first * 16 + 16), slice(second * 16, second * 16 + 16))


PIECE = 32
SPAN = 16
BLOCK = 32
VMEM = pl.BlockSpec(memory_space=pltpu.VMEM)
FAR = pl.BlockSpec(memory_space=pltpu.HBM)
PARAMS = pltpu.CompilerParams(vmem_limit_bytes=32 << 20)


def source_kernel(a_hbm, x_hbm, m_hbm, o_ref, a_ref, x_ref, m_ref, w_ref, a_sem, x_sems, m_sems):
    rows, cols, _ = x_ref.shape
    levels = m_ref.shape[0]
    a_copy = pltpu.make_async_copy(a_hbm, a_ref, a_sem)
    x_copies = []
    for piece in range(cols // PIECE):
        for at in range(0, rows, SPAN):
            own = (pl.ds(at, SPAN), pl.ds(piece * PIECE, PIECE))
            sem = x_sems.at[len(x_copies)]
            x_copies.append(pltpu.make_async_copy(x_hbm.at[own], x_ref.at[own], sem))
    m_copies = [
        pltpu.make_async_copy(m_hbm.at[i], m_ref.at[i], m_sems.at[i]) for i in range(levels)
    ]
    for copy in (a_copy, m_copies[0], *x_copies, *m_copies[1:]):
        copy.start()

    def expand(level):
        w_ref[level] = whole_matrix(m_ref[level])

    def level_on(level, begin):
        own = slice(begin, begin + BLOCK)

        def store(index, value):
            x_ref[index, own, :] = value

        butterfly(
            lambda index: x_ref[index, own, :],
            store,
            rows,
            1 << level,
            w_ref[level],
            lambda index: (cosines[own], sines[own]),
            8,
        )

    shuffle = shuffle_matrix()
    a_copy.wait()
    cosines, sines = halved(rotation(column_of(a_ref[...], cols)))
    m_copies[0].wait()
    expand(0)
    each = rows // SPAN
    for piece in range(cols // PIECE):
        for copy in x_copies[piece * each : (piece + 1) * each]:
            copy.wait()
        for begin in range(piece * PIECE, (piece + 1) * PIECE, BLOCK):
            level_on(0, begin)
    for copy in m_copies[1:]:
        copy.wait()
    for level in range(1, levels):
        expand(level)
    for level in range(1, levels):
        for begin in range(0, cols, BLOCK):
            level_on(level, begin)

    def store_block(first, second, block):
        o_ref[block_at(first, second)] = block

    swap_axes(
        lambda first, second: x_ref[block_at(first, second)],
        store_block,
        rows // 16,
        cols // 16,
        shuffle,
    )


def source_levels(x, matrices, slowness):
    rows, cols, _ = x.shape
    levels = matrices.shape[0]
    operands = (slowness[None, :], x, matrices)
    far = [pltpu.with_memory_space_constraint(value, pltpu.HBM) for value in operands]
    return pl.pallas_call(
        source_kernel,
        out_shape=jax.ShapeDtypeStruct((cols, rows, WIDE), x.dtype),
        in_specs=[FAR, FAR, FAR],
        out_specs=VMEM,
        scratch_shapes=[
            pltpu.VMEM((1, cols), jnp.float32),
            pltpu.VMEM(x.shape, x.dtype),
            pltpu.VMEM(matrices.shape, x.dtype),
            pltpu.VMEM((levels, 2 * WIDE, 2 * WIDE), x.dtype),
            pltpu.SemaphoreType.DMA,
            pltpu.SemaphoreType.DMA((cols // PIECE * (rows // SPAN),)),
            pltpu.SemaphoreType.DMA((levels,)),
        ],
        compiler_params=PARAMS,
    )(*far)


def middle_kernel(levels, rows, x_ref, m_ref, cs_ref, ss_ref, ct_ref, st_ref, o_ref):
    count, total, _ = x_ref.shape
    run = total // rows
    tgt_count = cs_ref.shape[0] // run
    for step, (apart, by_source) in enumerate(levels):
        source = x_ref if step == 0 else o_ref
        matrix = m_ref[step]
        for col in range(run):
            own = slice(col * rows, (col + 1) * rows)

            def phase_of(index):
                if by_source:
                    at = index % tgt_count * run + col
                    row = (cs_ref[at : at + 1, :], ss_ref[at : at + 1, :])
                    return halved(jnp.broadcast_to(part, (rows, WIDE)) for part in row)
                at = index // tgt_count
                return halved((ct_ref[at], st_ref[at]))

            def store(index, value):
                o_ref[index, own, :] = value

            butterfly(
                lambda index: source[index, own, :],
                store,
                count,
                apart,
                matrix,
                phase_of,
                8,
            )


def middle_levels(x, matrices, src_tables, tgt_tables, levels):
    rows = tgt_tables[0].shape[1]
    return pl.pallas_call(
        functools.partial(middle_kernel, levels, rows),
        out_shape=jax.ShapeDtypeStruct(x.shape, x.dtype),
        in_specs=[VMEM] * 6,
        out_specs=VMEM,
        compiler_params=PARAMS,
    )(x, matrices, *src_tables, *tgt_tables)


def target_kernel(m_ref, c_ref, s_ref, x_ref, o_hbm, state_ref, o_ref, o_sems):
    cols, rows, _ = x_ref.shape
    levels = m_ref.shape[0]

    for level in range(levels):
        source = x_ref if level == 0 else state_ref
        matrix = m_ref[level]
        for start in range(0, rows, 16):
            own = slice(start, start + 16)
            cosine, sine = halved((c_ref[own, :], s_ref[own, :]))

            def store(index, value):
                state_ref[index, own, :] = value

            butterfly(
                lambda index: source[index, own, :],
                store,
                cols,
                1 << (levels - 1 - level),
                matrix,
                lambda index: (cosine, sine),
                16,
            )

    shuffle = shuffle_matrix()
    copies = []
    half = cols // 2
    for piece in range(rows // 16):
        for side in range(2):
            own = (pl.ds(piece * 16, 16), pl.ds(side * half, half))
            copies.append(
                pltpu.make_async_copy(o_ref.at[own], o_hbm.at[own], o_sems.at[len(copies)])
            )

            def store_block(first, second, block):
                o_ref[block_at(piece, side * half // 16 + second)] = block

            swap_axes(
                lambda first, second: state_ref[block_at(side * half // 16 + first, piece)],
                store_block,
                half // 16,
                1,
                shuffle,
            )
            copies[-1].start()
    for copy in copies:
        copy.wait()


def target_levels(x, matrices, angles):
    cols, rows, _ = x.shape
    shape = (rows, cols, WIDE)
    return pl.pallas_call(
        target_kernel,
        out_shape=jax.ShapeDtypeStruct(shape, x.dtype),
        in_specs=[VMEM] * 4,
        out_specs=FAR,
        scratch_shapes=[
            pltpu.VMEM(x.shape, x.dtype),
            pltpu.VMEM(shape, x.dtype),
            pltpu.SemaphoreType.DMA((rows // 8,)),
        ],
        compiler_params=PARAMS,
    )(matrices, *angles, x)


def gathered(values, axis):
    count = lax.axis_size(axis)
    place = lax.axis_index(axis)
    values = values[None]
    apart = 1
    while apart < count:
        other = lax.ppermute(values, axis, [(i, i ^ apart) for i in range(count)])
        mine_first = (place & apart) == 0
        values = jnp.concatenate(
            [jnp.where(mine_first, values, other), jnp.where(mine_first, other, values)]
        )
        apart *= 2
    return values


def local(box_weights, slowness, dip_field):
    rows, cols, _ = box_weights.shape
    src_count = lax.axis_size("src")
    tgt_count = lax.axis_size("tgt")
    devices = src_count * tgt_count
    row_bits, col_bits = rows.bit_length() - 1, cols.bit_length() - 1
    src_bits, tgt_bits = src_count.bit_length() - 1, tgt_count.bit_length() - 1
    first_target = row_bits + src_bits
    total = first_target + tgt_bits + col_bits
    matrices = [level_matrix(number) for number in range(total)]

    run = cols // devices
    place = lax.axis_index("src") * tgt_count + lax.axis_index("tgt")

    def traded(state):
        return lax.all_to_all(state, ("src", "tgt"), 0, 0, tiled=True)

    state = source_levels(box_weights, jnp.asarray(np.stack(matrices[:row_bits])), slowness)

    state, slowness, dip_field = lax.optimization_barrier((state, slowness, dip_field))
    all_dip = gathered(dip_field, "src")
    all_slowness = gathered(slowness, "tgt")
    run_slowness = lax.dynamic_slice_in_dim(all_slowness, place * run, run, 1)

    state = state.reshape(devices, run * rows, WIDE)
    state = traded(state)
    levels = [(tgt_count << bit, True) for bit in range(src_bits)]
    levels += [(1 << bit, False) for bit in reversed(range(tgt_bits))]
    state = middle_levels(
        state,
        whole_matrices(matrices[row_bits : first_target + tgt_bits]),
        tables(run_slowness.reshape(-1)),
        tables(all_dip),
        levels,
    )
    state = traded(state)

    return target_levels(
        state.reshape(cols, rows, WIDE),
        whole_matrices(matrices[first_target + tgt_bits :]),
        tables(dip_field),
    )


def solution(mesh):
    in_specs = (P("src", "tgt", None), P("tgt"), P("src"))
    out_specs = P("src", "tgt", None)
    return jax.shard_map(local, mesh=mesh, in_specs=in_specs, out_specs=out_specs, check_vma=False)
```

```python
import functools
import math

import jax
import jax.numpy as jnp
import ml_dtypes
import numpy as np
from jax import lax
from jax.experimental import pallas as pl
from jax.experimental.pallas import tpu as pltpu
from jax.sharding import PartitionSpec as P

HALF = 64
WIDE = 128


def nodes():
    points = np.cos((2.0 * np.arange(8) + 1.0) * (math.pi / 16.0))
    return np.repeat(points, 8), np.tile(points, 8)


def node_weights():
    first, second = nodes()
    return (first * first + second * second).astype(np.float32)


def level_matrix(number):
    first, second = nodes()
    frequency = 9.0 + 3.0 * (number % 5)
    shifts = np.array([-0.5, 0.5])
    out_first = first[None, :] + shifts[:, None]
    in_second = second[None, :] + shifts[:, None]
    inner = (
        out_first[:, None, :, None] * first[None, None, None, :]
        + second[None, None, :, None] * in_second[None, :, None, :]
    )
    out_norm = np.sqrt(out_first**2 + second[None, :] ** 2)
    in_norm = np.sqrt(first[None, :] ** 2 + in_second**2)
    phases = frequency * (inner + 0.5 * out_norm[:, None, :, None] * in_norm[None, :, None, :])
    factor = 1.0 / math.sqrt(128.0)
    real = np.transpose(factor * np.cos(phases), (1, 3, 0, 2))
    imag = np.transpose(factor * np.sin(phases), (1, 3, 0, 2))
    upper = np.concatenate([real, imag], axis=3)
    return upper.reshape(WIDE, 2 * WIDE).astype(ml_dtypes.bfloat16)


def tables(scales):
    weights = np.tile(node_weights(), 2)
    angles = scales[..., None] * weights
    signs = np.repeat(np.array([-1.0, 1.0], np.float32), HALF)
    return jnp.cos(angles), jnp.sin(angles) * signs


def shuffle_matrix():
    to = lax.broadcasted_iota(jnp.int32, (256, 256), 0)
    source = lax.broadcasted_iota(jnp.int32, (256, 256), 1)
    here = source == (to & 15) * 16 + (to >> 4)
    return jnp.where(here, 1.0, 0.0).astype(jnp.bfloat16)


def cos_sin(angles):
    turns = jnp.floor(angles * (2.0 / math.pi) + 0.5)
    rest = angles - turns * 1.5703125
    rest = rest - turns * 4.837512969970703125e-4
    rest = rest - turns * 7.54978995489188e-8
    square = rest * rest
    sine = 1.0 / 362880.0
    for factor in (-1.0 / 5040.0, 1.0 / 120.0, -1.0 / 6.0, 1.0):
        sine = sine * square + factor
    sine = sine * rest
    cosine = -1.0 / 3628800.0
    for factor in (1.0 / 40320.0, -1.0 / 720.0, 1.0 / 24.0, -0.5, 1.0):
        cosine = cosine * square + factor
    quarter = turns.astype(jnp.int32)
    odd = (quarter & 1) == 1
    first = jnp.where(odd, sine, cosine)
    second = jnp.where(odd, cosine, sine)
    first = jnp.where(((quarter + 1) & 2) == 2, -first, first)
    second = jnp.where((quarter & 2) == 2, -second, second)
    return first, second


def halved(table):
    return tuple(part.astype(jnp.bfloat16) for part in table)


def node_row():
    lanes = lax.broadcasted_iota(jnp.int32, (1, WIDE), 1) % HALF
    points = [math.cos((2 * a + 1) * math.pi / 16) ** 2 for a in range(4)]

    def square(at):
        near = jnp.minimum(at, 7 - at)
        value = jnp.full(near.shape, points[3], jnp.float32)
        for a in range(3):
            value = jnp.where(near == a, jnp.float32(points[a]), value)
        return value

    return square(lanes // 8) + square(lanes % 8)


def rotation(column):
    cosine, sine = cos_sin(column * node_row())
    lanes = lax.broadcasted_iota(jnp.int32, cosine.shape, 1)
    return cosine, jnp.where(lanes < HALF, -sine, sine)


def column_of(row, count):
    shape = (count, WIDE)
    here = lax.broadcasted_iota(jnp.int32, shape, 0) == lax.broadcasted_iota(jnp.int32, shape, 1)
    return jnp.sum(jnp.where(here, jnp.broadcast_to(row, shape), 0.0), axis=1, keepdims=True)


def whole_matrix(upper):
    parts = [upper[:, at : at + HALF] for at in (HALF, 0, 3 * HALF, 2 * HALF)]
    traded = jnp.concatenate(parts, axis=1)
    im_lane = (lax.broadcasted_iota(jnp.int32, upper.shape, 1) & HALF) != 0
    below = jnp.where(im_lane, traded, -traded)
    children = (slice(0, HALF), slice(HALF, WIDE))
    return jnp.concatenate([half[rows] for rows in children for half in (upper, below)], axis=0)


def whole_matrices(uppers):
    upper = np.stack(uppers).astype(np.float32).reshape(-1, 2, HALF, 2, 2, HALF)
    below = np.stack([-upper[:, :, :, :, 1], upper[:, :, :, :, 0]], axis=4)
    both = np.concatenate([upper, below], axis=2)
    return jnp.asarray(both.reshape(-1, 2 * WIDE, 2 * WIDE).astype(ml_dtypes.bfloat16))


def butterfly(load, store, count, apart, matrix, phase_of, group):
    lows = [i for i in range(count) if not i & apart]
    for start in range(0, len(lows), group):
        picked = lows[start : start + group]
        left = jnp.concatenate([load(i) for i in picked], axis=0)
        right = jnp.concatenate([load(i + apart) for i in picked], axis=0)
        rows = left.shape[0] // len(picked)
        pair = jnp.concatenate([left, right], axis=1)
        both = jnp.dot(pair, matrix, preferred_element_type=jnp.float32).astype(jnp.bfloat16)
        for place, low in enumerate(picked):
            for child in range(2):
                index = low + child * apart
                cosine, sine = phase_of(index)
                value = both[
                    place * rows : (place + 1) * rows, child * WIDE : (child + 1) * WIDE
                ]
                turned = jnp.concatenate([value[:, HALF:], value[:, :HALF]], axis=1)
                store(index, value * cosine + turned * sine)


def swap_axes(load, store, outer, inner, shuffle):
    for low in range(0, outer, 2):
        for at in range(inner):
            sides = [load(low + side, at).reshape(256, WIDE) for side in range(2)]
            moved = jnp.dot(
                shuffle, jnp.concatenate(sides, axis=1), preferred_element_type=jnp.float32
            ).astype(jnp.bfloat16)
            for side in range(2):
                block = moved[:, side * WIDE : (side + 1) * WIDE]
                store(at, low + side, block.reshape(16, 16, WIDE))


def block_at(first, second):
    return (slice(first * 16, first * 16 + 16), slice(second * 16, second * 16 + 16))


SPAN = 8
BLOCK = 32
VMEM = pl.BlockSpec(memory_space=pltpu.VMEM)
FAR = pl.BlockSpec(memory_space=pltpu.HBM)
PARAMS = pltpu.CompilerParams(vmem_limit_bytes=32 << 20)


def source_kernel(a_hbm, x_hbm, m_hbm, o_ref, a_ref, x_ref, m_ref, w_ref, a_sem, x_sems, m_sems):
    rows, cols, _ = x_ref.shape
    levels = m_ref.shape[0]
    a_copy = pltpu.make_async_copy(a_hbm, a_ref, a_sem)
    x_copies = []
    for piece in range(rows // SPAN):
        own = pl.ds(piece * SPAN, SPAN)
        x_copies.append(pltpu.make_async_copy(x_hbm.at[own], x_ref.at[own], x_sems.at[piece]))
    m_copies = [
        pltpu.make_async_copy(m_hbm.at[i], m_ref.at[i], m_sems.at[i]) for i in range(levels)
    ]
    loads = (a_copy, *m_copies, *x_copies)
    for copy in loads:
        copy.start()

    def expand(level):
        w_ref[level] = whole_matrix(m_ref[level])

    def level_on(level, begin):
        own = slice(begin, begin + BLOCK)

        def store(index, value):
            x_ref[index, own, :] = value

        butterfly(
            lambda index: x_ref[index, own, :],
            store,
            rows,
            1 << level,
            w_ref[level],
            lambda index: (cosines[own], sines[own]),
            8,
        )

    shuffle = shuffle_matrix()
    for copy in loads:
        copy.wait()
    cosines, sines = halved(rotation(column_of(a_ref[...], cols)))
    for level in range(levels):
        expand(level)
        for begin in range(0, cols, BLOCK):
            level_on(level, begin)

    def store_block(first, second, block):
        o_ref[block_at(first, second)] = block

    swap_axes(
        lambda first, second: x_ref[block_at(first, second)],
        store_block,
        rows // 16,
        cols // 16,
        shuffle,
    )


def source_levels(x, matrices, slowness):
    rows, cols, _ = x.shape
    levels = matrices.shape[0]
    operands = (slowness[None, :], x, matrices)
    far = [pltpu.with_memory_space_constraint(value, pltpu.HBM) for value in operands]
    return pl.pallas_call(
        source_kernel,
        out_shape=jax.ShapeDtypeStruct((cols, rows, WIDE), x.dtype),
        in_specs=[FAR, FAR, FAR],
        out_specs=VMEM,
        scratch_shapes=[
            pltpu.VMEM((1, cols), jnp.float32),
            pltpu.VMEM(x.shape, x.dtype),
            pltpu.VMEM(matrices.shape, x.dtype),
            pltpu.VMEM((levels, 2 * WIDE, 2 * WIDE), x.dtype),
            pltpu.SemaphoreType.DMA,
            pltpu.SemaphoreType.DMA((rows // SPAN,)),
            pltpu.SemaphoreType.DMA((levels,)),
        ],
        compiler_params=PARAMS,
    )(*far)


def middle_kernel(levels, rows, x_ref, m_ref, cs_ref, ss_ref, ct_ref, st_ref, o_ref):
    count, total, _ = x_ref.shape
    run = total // rows
    tgt_count = cs_ref.shape[0] // run
    for step, (apart, by_source) in enumerate(levels):
        source = x_ref if step == 0 else o_ref
        matrix = m_ref[step]
        for col in range(run):
            own = slice(col * rows, (col + 1) * rows)

            def phase_of(index):
                if by_source:
                    at = index % tgt_count * run + col
                    row = (cs_ref[at : at + 1, :], ss_ref[at : at + 1, :])
                    return halved(jnp.broadcast_to(part, (rows, WIDE)) for part in row)
                at = index // tgt_count
                return halved((ct_ref[at], st_ref[at]))

            def store(index, value):
                o_ref[index, own, :] = value

            butterfly(
                lambda index: source[index, own, :],
                store,
                count,
                apart,
                matrix,
                phase_of,
                8,
            )


def middle_levels(x, matrices, src_tables, tgt_tables, levels):
    rows = tgt_tables[0].shape[1]
    return pl.pallas_call(
        functools.partial(middle_kernel, levels, rows),
        out_shape=jax.ShapeDtypeStruct(x.shape, x.dtype),
        in_specs=[VMEM] * 6,
        out_specs=VMEM,
        compiler_params=PARAMS,
    )(x, matrices, *src_tables, *tgt_tables)


def target_kernel(m_ref, c_ref, s_ref, x_ref, o_hbm, state_ref, o_ref, o_sems):
    cols, rows, _ = x_ref.shape
    levels = m_ref.shape[0]

    for level in range(levels):
        source = x_ref if level == 0 else state_ref
        matrix = m_ref[level]
        for start in range(0, rows, 16):
            own = slice(start, start + 16)
            cosine, sine = halved((c_ref[own, :], s_ref[own, :]))

            def store(index, value):
                state_ref[index, own, :] = value

            butterfly(
                lambda index: source[index, own, :],
                store,
                cols,
                1 << (levels - 1 - level),
                matrix,
                lambda index: (cosine, sine),
                16,
            )

    shuffle = shuffle_matrix()
    copies = []
    half = cols // 2
    for piece in range(rows // 16):
        for side in range(2):
            own = (pl.ds(piece * 16, 16), pl.ds(side * half, half))
            copies.append(
                pltpu.make_async_copy(o_ref.at[own], o_hbm.at[own], o_sems.at[len(copies)])
            )

            def store_block(first, second, block):
                o_ref[block_at(piece, side * half // 16 + second)] = block

            swap_axes(
                lambda first, second: state_ref[block_at(side * half // 16 + first, piece)],
                store_block,
                half // 16,
                1,
                shuffle,
            )
            copies[-1].start()
    for copy in copies:
        copy.wait()


def target_levels(x, matrices, angles):
    cols, rows, _ = x.shape
    shape = (rows, cols, WIDE)
    return pl.pallas_call(
        target_kernel,
        out_shape=jax.ShapeDtypeStruct(shape, x.dtype),
        in_specs=[VMEM] * 4,
        out_specs=FAR,
        scratch_shapes=[
            pltpu.VMEM(x.shape, x.dtype),
            pltpu.VMEM(shape, x.dtype),
            pltpu.SemaphoreType.DMA((rows // 8,)),
        ],
        compiler_params=PARAMS,
    )(matrices, *angles, x)


def gathered(values, axis):
    count = lax.axis_size(axis)
    place = lax.axis_index(axis)
    values = values[None]
    apart = 1
    while apart < count:
        other = lax.ppermute(values, axis, [(i, i ^ apart) for i in range(count)])
        mine_first = (place & apart) == 0
        values = jnp.concatenate(
            [jnp.where(mine_first, values, other), jnp.where(mine_first, other, values)]
        )
        apart *= 2
    return values


def local(box_weights, slowness, dip_field):
    rows, cols, _ = box_weights.shape
    src_count = lax.axis_size("src")
    tgt_count = lax.axis_size("tgt")
    devices = src_count * tgt_count
    row_bits, col_bits = rows.bit_length() - 1, cols.bit_length() - 1
    src_bits, tgt_bits = src_count.bit_length() - 1, tgt_count.bit_length() - 1
    first_target = row_bits + src_bits
    total = first_target + tgt_bits + col_bits
    matrices = [level_matrix(number) for number in range(total)]

    run = cols // devices
    place = lax.axis_index("src") * tgt_count + lax.axis_index("tgt")

    def traded(state):
        return lax.all_to_all(state, ("src", "tgt"), 0, 0, tiled=True)

    state = source_levels(box_weights, jnp.asarray(np.stack(matrices[:row_bits])), slowness)

    state, slowness, dip_field = lax.optimization_barrier((state, slowness, dip_field))
    all_dip = gathered(dip_field, "src")
    all_slowness = gathered(slowness, "tgt")
    run_slowness = lax.dynamic_slice_in_dim(all_slowness, place * run, run, 1)

    state = state.reshape(devices, run * rows, WIDE)
    state = traded(state)
    levels = [(tgt_count << bit, True) for bit in range(src_bits)]
    levels += [(1 << bit, False) for bit in reversed(range(tgt_bits))]
    state = middle_levels(
        state,
        whole_matrices(matrices[row_bits : first_target + tgt_bits]),
        tables(run_slowness.reshape(-1)),
        tables(all_dip),
        levels,
    )
    state = traded(state)

    return target_levels(
        state.reshape(cols, rows, WIDE),
        whole_matrices(matrices[first_target + tgt_bits :]),
        tables(dip_field),
    )


def solution(mesh):
    in_specs = (P("src", "tgt", None), P("tgt"), P("src"))
    out_specs = P("src", "tgt", None)
    return jax.shard_map(local, mesh=mesh, in_specs=in_specs, out_specs=out_specs, check_vma=False)
```

```python
import functools
import math

import jax
import jax.numpy as jnp
import ml_dtypes
import numpy as np
from jax import lax
from jax.experimental import pallas as pl
from jax.experimental.pallas import tpu as pltpu
from jax.sharding import PartitionSpec as P

HALF = 64
WIDE = 128


def nodes():
    points = np.cos((2.0 * np.arange(8) + 1.0) * (math.pi / 16.0))
    return np.repeat(points, 8), np.tile(points, 8)


def node_weights():
    first, second = nodes()
    return (first * first + second * second).astype(np.float32)


def level_matrix(number):
    first, second = nodes()
    frequency = 9.0 + 3.0 * (number % 5)
    shifts = np.array([-0.5, 0.5])
    out_first = first[None, :] + shifts[:, None]
    in_second = second[None, :] + shifts[:, None]
    inner = (
        out_first[:, None, :, None] * first[None, None, None, :]
        + second[None, None, :, None] * in_second[None, :, None, :]
    )
    out_norm = np.sqrt(out_first**2 + second[None, :] ** 2)
    in_norm = np.sqrt(first[None, :] ** 2 + in_second**2)
    phases = frequency * (inner + 0.5 * out_norm[:, None, :, None] * in_norm[None, :, None, :])
    factor = 1.0 / math.sqrt(128.0)
    real = np.transpose(factor * np.cos(phases), (1, 3, 0, 2))
    imag = np.transpose(factor * np.sin(phases), (1, 3, 0, 2))
    upper = np.concatenate([real, imag], axis=3)
    return upper.reshape(WIDE, 2 * WIDE).astype(ml_dtypes.bfloat16)


def tables(scales):
    weights = np.tile(node_weights(), 2)
    angles = scales[..., None] * weights
    signs = np.repeat(np.array([-1.0, 1.0], np.float32), HALF)
    return jnp.cos(angles), jnp.sin(angles) * signs


def shuffle_matrix():
    to = lax.broadcasted_iota(jnp.int32, (256, 256), 0)
    source = lax.broadcasted_iota(jnp.int32, (256, 256), 1)
    here = source == (to & 15) * 16 + (to >> 4)
    return jnp.where(here, 1.0, 0.0).astype(jnp.bfloat16)


def cos_sin(angles):
    turns = jnp.floor(angles * (2.0 / math.pi) + 0.5)
    rest = angles - turns * 1.5703125
    rest = rest - turns * 4.837512969970703125e-4
    rest = rest - turns * 7.54978995489188e-8
    square = rest * rest
    sine = 1.0 / 362880.0
    for factor in (-1.0 / 5040.0, 1.0 / 120.0, -1.0 / 6.0, 1.0):
        sine = sine * square + factor
    sine = sine * rest
    cosine = -1.0 / 3628800.0
    for factor in (1.0 / 40320.0, -1.0 / 720.0, 1.0 / 24.0, -0.5, 1.0):
        cosine = cosine * square + factor
    quarter = turns.astype(jnp.int32)
    odd = (quarter & 1) == 1
    first = jnp.where(odd, sine, cosine)
    second = jnp.where(odd, cosine, sine)
    first = jnp.where(((quarter + 1) & 2) == 2, -first, first)
    second = jnp.where((quarter & 2) == 2, -second, second)
    return first, second


def halved(table):
    return tuple(part.astype(jnp.bfloat16) for part in table)


def node_row():
    lanes = lax.broadcasted_iota(jnp.int32, (1, WIDE), 1) % HALF
    points = [math.cos((2 * a + 1) * math.pi / 16) ** 2 for a in range(4)]

    def square(at):
        near = jnp.minimum(at, 7 - at)
        value = jnp.full(near.shape, points[3], jnp.float32)
        for a in range(3):
            value = jnp.where(near == a, jnp.float32(points[a]), value)
        return value

    return square(lanes // 8) + square(lanes % 8)


def rotation(column):
    cosine, sine = cos_sin(column * node_row())
    lanes = lax.broadcasted_iota(jnp.int32, cosine.shape, 1)
    return cosine, jnp.where(lanes < HALF, -sine, sine)


def column_of(row, count):
    shape = (count, WIDE)
    here = lax.broadcasted_iota(jnp.int32, shape, 0) == lax.broadcasted_iota(jnp.int32, shape, 1)
    return jnp.sum(jnp.where(here, jnp.broadcast_to(row, shape), 0.0), axis=1, keepdims=True)


def whole_matrix(upper):
    parts = [upper[:, at : at + HALF] for at in (HALF, 0, 3 * HALF, 2 * HALF)]
    traded = jnp.concatenate(parts, axis=1)
    im_lane = (lax.broadcasted_iota(jnp.int32, upper.shape, 1) & HALF) != 0
    below = jnp.where(im_lane, traded, -traded)
    children = (slice(0, HALF), slice(HALF, WIDE))
    return jnp.concatenate([half[rows] for rows in children for half in (upper, below)], axis=0)


def whole_matrices(uppers):
    upper = np.stack(uppers).astype(np.float32).reshape(-1, 2, HALF, 2, 2, HALF)
    below = np.stack([-upper[:, :, :, :, 1], upper[:, :, :, :, 0]], axis=4)
    both = np.concatenate([upper, below], axis=2)
    return jnp.asarray(both.reshape(-1, 2 * WIDE, 2 * WIDE).astype(ml_dtypes.bfloat16))


def butterfly(load, store, count, apart, matrix, phase_of, group):
    lows = [i for i in range(count) if not i & apart]
    for start in range(0, len(lows), group):
        picked = lows[start : start + group]
        left = jnp.concatenate([load(i) for i in picked], axis=0)
        right = jnp.concatenate([load(i + apart) for i in picked], axis=0)
        rows = left.shape[0] // len(picked)
        pair = jnp.concatenate([left, right], axis=1)
        both = jnp.dot(pair, matrix, preferred_element_type=jnp.float32).astype(jnp.bfloat16)
        for place, low in enumerate(picked):
            for child in range(2):
                index = low + child * apart
                cosine, sine = phase_of(index)
                value = both[
                    place * rows : (place + 1) * rows, child * WIDE : (child + 1) * WIDE
                ]
                turned = jnp.concatenate([value[:, HALF:], value[:, :HALF]], axis=1)
                store(index, value * cosine + turned * sine)


def swap_axes(load, store, outer, inner, shuffle):
    for low in range(0, outer, 2):
        for at in range(inner):
            sides = [load(low + side, at).reshape(256, WIDE) for side in range(2)]
            moved = jnp.dot(
                shuffle, jnp.concatenate(sides, axis=1), preferred_element_type=jnp.float32
            ).astype(jnp.bfloat16)
            for side in range(2):
                block = moved[:, side * WIDE : (side + 1) * WIDE]
                store(at, low + side, block.reshape(16, 16, WIDE))


def block_at(first, second):
    return (slice(first * 16, first * 16 + 16), slice(second * 16, second * 16 + 16))


SPAN = 8
BLOCK = 32
VMEM = pl.BlockSpec(memory_space=pltpu.VMEM)
FAR = pl.BlockSpec(memory_space=pltpu.HBM)
PARAMS = pltpu.CompilerParams(vmem_limit_bytes=32 << 20)


def source_kernel(a_hbm, x_hbm, m_hbm, o_ref, a_ref, x_ref, m_ref, w_ref, a_sem, x_sems, m_sems):
    rows, cols, _ = x_ref.shape
    levels = m_ref.shape[0]
    a_copy = pltpu.make_async_copy(a_hbm, a_ref, a_sem)
    x_copies = []
    for piece in range(rows // SPAN):
        own = pl.ds(piece * SPAN, SPAN)
        x_copies.append(pltpu.make_async_copy(x_hbm.at[own], x_ref.at[own], x_sems.at[piece]))
    m_copies = [
        pltpu.make_async_copy(m_hbm.at[i], m_ref.at[i], m_sems.at[i]) for i in range(levels)
    ]
    for copy in (a_copy, *m_copies, *x_copies):
        copy.start()

    def expand(level):
        w_ref[level] = whole_matrix(m_ref[level])

    def level_on(level, begin):
        own = slice(begin, begin + BLOCK)

        def store(index, value):
            x_ref[index, own, :] = value

        butterfly(
            lambda index: x_ref[index, own, :],
            store,
            rows,
            1 << level,
            w_ref[level],
            lambda index: (cosines[own], sines[own]),
            8,
        )

    shuffle = shuffle_matrix()
    for copy in (a_copy, *m_copies):
        copy.wait()
    cosines, sines = halved(rotation(column_of(a_ref[...], cols)))
    for level in range(levels):
        expand(level)
    for copy in x_copies:
        copy.wait()
    for level in range(levels):
        for begin in range(0, cols, BLOCK):
            level_on(level, begin)

    def store_block(first, second, block):
        o_ref[block_at(first, second)] = block

    swap_axes(
        lambda first, second: x_ref[block_at(first, second)],
        store_block,
        rows // 16,
        cols // 16,
        shuffle,
    )


def source_levels(x, matrices, slowness):
    rows, cols, _ = x.shape
    levels = matrices.shape[0]
    operands = (slowness[None, :], x, matrices)
    far = [pltpu.with_memory_space_constraint(value, pltpu.HBM) for value in operands]
    return pl.pallas_call(
        source_kernel,
        out_shape=jax.ShapeDtypeStruct((cols, rows, WIDE), x.dtype),
        in_specs=[FAR, FAR, FAR],
        out_specs=VMEM,
        scratch_shapes=[
            pltpu.VMEM((1, cols), jnp.float32),
            pltpu.VMEM(x.shape, x.dtype),
            pltpu.VMEM(matrices.shape, x.dtype),
            pltpu.VMEM((levels, 2 * WIDE, 2 * WIDE), x.dtype),
            pltpu.SemaphoreType.DMA,
            pltpu.SemaphoreType.DMA((rows // SPAN,)),
            pltpu.SemaphoreType.DMA((levels,)),
        ],
        compiler_params=PARAMS,
    )(*far)


def middle_kernel(levels, rows, x_ref, m_ref, cs_ref, ss_ref, ct_ref, st_ref, o_ref):
    count, total, _ = x_ref.shape
    run = total // rows
    tgt_count = cs_ref.shape[0] // run
    for step, (apart, by_source) in enumerate(levels):
        source = x_ref if step == 0 else o_ref
        matrix = m_ref[step]
        for col in range(run):
            own = slice(col * rows, (col + 1) * rows)

            def phase_of(index):
                if by_source:
                    at = index % tgt_count * run + col
                    row = (cs_ref[at : at + 1, :], ss_ref[at : at + 1, :])
                    return halved(jnp.broadcast_to(part, (rows, WIDE)) for part in row)
                at = index // tgt_count
                return halved((ct_ref[at], st_ref[at]))

            def store(index, value):
                o_ref[index, own, :] = value

            butterfly(
                lambda index: source[index, own, :],
                store,
                count,
                apart,
                matrix,
                phase_of,
                8,
            )


def middle_levels(x, matrices, src_tables, tgt_tables, levels):
    rows = tgt_tables[0].shape[1]
    return pl.pallas_call(
        functools.partial(middle_kernel, levels, rows),
        out_shape=jax.ShapeDtypeStruct(x.shape, x.dtype),
        in_specs=[VMEM] * 6,
        out_specs=VMEM,
        compiler_params=PARAMS,
    )(x, matrices, *src_tables, *tgt_tables)


def target_kernel(m_ref, c_ref, s_ref, x_ref, o_hbm, state_ref, o_ref, o_sems):
    cols, rows, _ = x_ref.shape
    levels = m_ref.shape[0]

    for level in range(levels):
        source = x_ref if level == 0 else state_ref
        matrix = m_ref[level]
        for start in range(0, rows, 16):
            own = slice(start, start + 16)
            cosine, sine = halved((c_ref[own, :], s_ref[own, :]))

            def store(index, value):
                state_ref[index, own, :] = value

            butterfly(
                lambda index: source[index, own, :],
                store,
                cols,
                1 << (levels - 1 - level),
                matrix,
                lambda index: (cosine, sine),
                16,
            )

    shuffle = shuffle_matrix()
    copies = []
    half = cols // 2
    for piece in range(rows // 16):
        for side in range(2):
            own = (pl.ds(piece * 16, 16), pl.ds(side * half, half))
            copies.append(
                pltpu.make_async_copy(o_ref.at[own], o_hbm.at[own], o_sems.at[len(copies)])
            )

            def store_block(first, second, block):
                o_ref[block_at(piece, side * half // 16 + second)] = block

            swap_axes(
                lambda first, second: state_ref[block_at(side * half // 16 + first, piece)],
                store_block,
                half // 16,
                1,
                shuffle,
            )
            copies[-1].start()
    for copy in copies:
        copy.wait()


def target_levels(x, matrices, angles):
    cols, rows, _ = x.shape
    shape = (rows, cols, WIDE)
    return pl.pallas_call(
        target_kernel,
        out_shape=jax.ShapeDtypeStruct(shape, x.dtype),
        in_specs=[VMEM] * 4,
        out_specs=FAR,
        scratch_shapes=[
            pltpu.VMEM(x.shape, x.dtype),
            pltpu.VMEM(shape, x.dtype),
            pltpu.SemaphoreType.DMA((rows // 8,)),
        ],
        compiler_params=PARAMS,
    )(matrices, *angles, x)


def gathered(values, axis):
    count = lax.axis_size(axis)
    place = lax.axis_index(axis)
    values = values[None]
    apart = 1
    while apart < count:
        other = lax.ppermute(values, axis, [(i, i ^ apart) for i in range(count)])
        mine_first = (place & apart) == 0
        values = jnp.concatenate(
            [jnp.where(mine_first, values, other), jnp.where(mine_first, other, values)]
        )
        apart *= 2
    return values


def local(box_weights, slowness, dip_field):
    rows, cols, _ = box_weights.shape
    src_count = lax.axis_size("src")
    tgt_count = lax.axis_size("tgt")
    devices = src_count * tgt_count
    row_bits, col_bits = rows.bit_length() - 1, cols.bit_length() - 1
    src_bits, tgt_bits = src_count.bit_length() - 1, tgt_count.bit_length() - 1
    first_target = row_bits + src_bits
    total = first_target + tgt_bits + col_bits
    matrices = [level_matrix(number) for number in range(total)]

    run = cols // devices
    place = lax.axis_index("src") * tgt_count + lax.axis_index("tgt")

    def traded(state):
        return lax.all_to_all(state, ("src", "tgt"), 0, 0, tiled=True)

    state = source_levels(box_weights, jnp.asarray(np.stack(matrices[:row_bits])), slowness)

    state, slowness, dip_field = lax.optimization_barrier((state, slowness, dip_field))
    all_dip = gathered(dip_field, "src")
    all_slowness = gathered(slowness, "tgt")
    run_slowness = lax.dynamic_slice_in_dim(all_slowness, place * run, run, 1)

    state = state.reshape(devices, run * rows, WIDE)
    state = traded(state)
    levels = [(tgt_count << bit, True) for bit in range(src_bits)]
    levels += [(1 << bit, False) for bit in reversed(range(tgt_bits))]
    state = middle_levels(
        state,
        whole_matrices(matrices[row_bits : first_target + tgt_bits]),
        tables(run_slowness.reshape(-1)),
        tables(all_dip),
        levels,
    )
    state = traded(state)

    return target_levels(
        state.reshape(cols, rows, WIDE),
        whole_matrices(matrices[first_target + tgt_bits :]),
        tables(dip_field),
    )


def solution(mesh):
    in_specs = (P("src", "tgt", None), P("tgt"), P("src"))
    out_specs = P("src", "tgt", None)
    return jax.shard_map(local, mesh=mesh, in_specs=in_specs, out_specs=out_specs, check_vma=False)
```

```python
import functools
import math

import jax
import jax.numpy as jnp
import ml_dtypes
import numpy as np
from jax import lax
from jax.experimental import pallas as pl
from jax.experimental.pallas import tpu as pltpu
from jax.sharding import PartitionSpec as P

HALF = 64
WIDE = 128


def nodes():
    points = np.cos((2.0 * np.arange(8) + 1.0) * (math.pi / 16.0))
    return np.repeat(points, 8), np.tile(points, 8)


def node_weights():
    first, second = nodes()
    return (first * first + second * second).astype(np.float32)


def level_matrix(number):
    first, second = nodes()
    frequency = 9.0 + 3.0 * (number % 5)
    shifts = np.array([-0.5, 0.5])
    out_first = first[None, :] + shifts[:, None]
    in_second = second[None, :] + shifts[:, None]
    inner = (
        out_first[:, None, :, None] * first[None, None, None, :]
        + second[None, None, :, None] * in_second[None, :, None, :]
    )
    out_norm = np.sqrt(out_first**2 + second[None, :] ** 2)
    in_norm = np.sqrt(first[None, :] ** 2 + in_second**2)
    phases = frequency * (inner + 0.5 * out_norm[:, None, :, None] * in_norm[None, :, None, :])
    factor = 1.0 / math.sqrt(128.0)
    real = np.transpose(factor * np.cos(phases), (1, 3, 0, 2))
    imag = np.transpose(factor * np.sin(phases), (1, 3, 0, 2))
    upper = np.concatenate([real, imag], axis=3)
    return upper.reshape(WIDE, 2 * WIDE).astype(ml_dtypes.bfloat16)


def tables(scales):
    weights = np.tile(node_weights(), 2)
    angles = scales[..., None] * weights
    signs = np.repeat(np.array([-1.0, 1.0], np.float32), HALF)
    return jnp.cos(angles), jnp.sin(angles) * signs


def shuffle_matrix():
    to = lax.broadcasted_iota(jnp.int32, (256, 256), 0)
    source = lax.broadcasted_iota(jnp.int32, (256, 256), 1)
    here = source == (to & 15) * 16 + (to >> 4)
    return jnp.where(here, 1.0, 0.0).astype(jnp.bfloat16)


def cos_sin(angles):
    turns = jnp.floor(angles * (2.0 / math.pi) + 0.5)
    rest = angles - turns * 1.5703125
    rest = rest - turns * 4.837512969970703125e-4
    rest = rest - turns * 7.54978995489188e-8
    square = rest * rest
    sine = 1.0 / 362880.0
    for factor in (-1.0 / 5040.0, 1.0 / 120.0, -1.0 / 6.0, 1.0):
        sine = sine * square + factor
    sine = sine * rest
    cosine = -1.0 / 3628800.0
    for factor in (1.0 / 40320.0, -1.0 / 720.0, 1.0 / 24.0, -0.5, 1.0):
        cosine = cosine * square + factor
    quarter = turns.astype(jnp.int32)
    odd = (quarter & 1) == 1
    first = jnp.where(odd, sine, cosine)
    second = jnp.where(odd, cosine, sine)
    first = jnp.where(((quarter + 1) & 2) == 2, -first, first)
    second = jnp.where((quarter & 2) == 2, -second, second)
    return first, second


def halved(table):
    return tuple(part.astype(jnp.bfloat16) for part in table)


def node_row():
    lanes = lax.broadcasted_iota(jnp.int32, (1, WIDE), 1) % HALF
    points = [math.cos((2 * a + 1) * math.pi / 16) ** 2 for a in range(4)]

    def square(at):
        near = jnp.minimum(at, 7 - at)
        value = jnp.full(near.shape, points[3], jnp.float32)
        for a in range(3):
            value = jnp.where(near == a, jnp.float32(points[a]), value)
        return value

    return square(lanes // 8) + square(lanes % 8)


def rotation(column):
    cosine, sine = cos_sin(column * node_row())
    lanes = lax.broadcasted_iota(jnp.int32, cosine.shape, 1)
    return cosine, jnp.where(lanes < HALF, -sine, sine)


def column_of(row, count):
    shape = (count, WIDE)
    here = lax.broadcasted_iota(jnp.int32, shape, 0) == lax.broadcasted_iota(jnp.int32, shape, 1)
    return jnp.sum(jnp.where(here, jnp.broadcast_to(row, shape), 0.0), axis=1, keepdims=True)


def whole_matrix(upper):
    parts = [upper[:, at : at + HALF] for at in (HALF, 0, 3 * HALF, 2 * HALF)]
    traded = jnp.concatenate(parts, axis=1)
    im_lane = (lax.broadcasted_iota(jnp.int32, upper.shape, 1) & HALF) != 0
    below = jnp.where(im_lane, traded, -traded)
    children = (slice(0, HALF), slice(HALF, WIDE))
    return jnp.concatenate([half[rows] for rows in children for half in (upper, below)], axis=0)


def whole_matrices(uppers):
    upper = np.stack(uppers).astype(np.float32).reshape(-1, 2, HALF, 2, 2, HALF)
    below = np.stack([-upper[:, :, :, :, 1], upper[:, :, :, :, 0]], axis=4)
    both = np.concatenate([upper, below], axis=2)
    return jnp.asarray(both.reshape(-1, 2 * WIDE, 2 * WIDE).astype(ml_dtypes.bfloat16))


def butterfly(load, store, count, apart, matrix, phase_of, group):
    lows = [i for i in range(count) if not i & apart]
    for start in range(0, len(lows), group):
        picked = lows[start : start + group]
        left = jnp.concatenate([load(i) for i in picked], axis=0)
        right = jnp.concatenate([load(i + apart) for i in picked], axis=0)
        rows = left.shape[0] // len(picked)
        pair = jnp.concatenate([left, right], axis=1)
        both = jnp.dot(pair, matrix, preferred_element_type=jnp.float32).astype(jnp.bfloat16)
        for place, low in enumerate(picked):
            for child in range(2):
                index = low + child * apart
                cosine, sine = phase_of(index)
                value = both[
                    place * rows : (place + 1) * rows, child * WIDE : (child + 1) * WIDE
                ]
                turned = jnp.concatenate([value[:, HALF:], value[:, :HALF]], axis=1)
                store(index, value * cosine + turned * sine)


def swap_axes(load, store, outer, inner, shuffle):
    for low in range(0, outer, 2):
        for at in range(inner):
            sides = [load(low + side, at).reshape(256, WIDE) for side in range(2)]
            moved = jnp.dot(
                shuffle, jnp.concatenate(sides, axis=1), preferred_element_type=jnp.float32
            ).astype(jnp.bfloat16)
            for side in range(2):
                block = moved[:, side * WIDE : (side + 1) * WIDE]
                store(at, low + side, block.reshape(16, 16, WIDE))


def block_at(first, second):
    return (slice(first * 16, first * 16 + 16), slice(second * 16, second * 16 + 16))


SPAN = 8
BLOCK = 32
VMEM = pl.BlockSpec(memory_space=pltpu.VMEM)
FAR = pl.BlockSpec(memory_space=pltpu.HBM)
PARAMS = pltpu.CompilerParams(vmem_limit_bytes=32 << 20)


def source_kernel(a_hbm, x_hbm, m_hbm, o_ref, a_ref, x_ref, m_ref, w_ref, a_sem, x_sems, m_sem):
    rows, cols, _ = x_ref.shape
    levels = m_ref.shape[0]
    a_copy = pltpu.make_async_copy(a_hbm, a_ref, a_sem)
    x_copies = []
    for piece in range(rows // SPAN):
        own = pl.ds(piece * SPAN, SPAN)
        x_copies.append(pltpu.make_async_copy(x_hbm.at[own], x_ref.at[own], x_sems.at[piece]))
    m_copy = pltpu.make_async_copy(m_hbm, m_ref, m_sem)
    for copy in (a_copy, m_copy, *x_copies):
        copy.start()

    def expand(level):
        w_ref[level] = whole_matrix(m_ref[level])

    def level_on(level, begin):
        own = slice(begin, begin + BLOCK)

        def store(index, value):
            x_ref[index, own, :] = value

        butterfly(
            lambda index: x_ref[index, own, :],
            store,
            rows,
            1 << level,
            w_ref[level],
            lambda index: (cosines[own], sines[own]),
            8,
        )

    shuffle = shuffle_matrix()
    for copy in (a_copy, m_copy):
        copy.wait()
    cosines, sines = halved(rotation(column_of(a_ref[...], cols)))
    for level in range(levels):
        expand(level)
    for copy in x_copies:
        copy.wait()
    for level in range(levels):
        for begin in range(0, cols, BLOCK):
            level_on(level, begin)

    def store_block(first, second, block):
        o_ref[block_at(first, second)] = block

    swap_axes(
        lambda first, second: x_ref[block_at(first, second)],
        store_block,
        rows // 16,
        cols // 16,
        shuffle,
    )


def source_levels(x, matrices, slowness):
    rows, cols, _ = x.shape
    levels = matrices.shape[0]
    operands = (slowness[None, :], x, matrices)
    far = [pltpu.with_memory_space_constraint(value, pltpu.HBM) for value in operands]
    return pl.pallas_call(
        source_kernel,
        out_shape=jax.ShapeDtypeStruct((cols, rows, WIDE), x.dtype),
        in_specs=[FAR, FAR, FAR],
        out_specs=VMEM,
        scratch_shapes=[
            pltpu.VMEM((1, cols), jnp.float32),
            pltpu.VMEM(x.shape, x.dtype),
            pltpu.VMEM(matrices.shape, x.dtype),
            pltpu.VMEM((levels, 2 * WIDE, 2 * WIDE), x.dtype),
            pltpu.SemaphoreType.DMA,
            pltpu.SemaphoreType.DMA((rows // SPAN,)),
            pltpu.SemaphoreType.DMA,
        ],
        compiler_params=PARAMS,
    )(*far)


def middle_kernel(levels, rows, x_ref, m_ref, cs_ref, ss_ref, ct_ref, st_ref, o_ref):
    count, total, _ = x_ref.shape
    run = total // rows
    tgt_count = cs_ref.shape[0] // run
    for step, (apart, by_source) in enumerate(levels):
        source = x_ref if step == 0 else o_ref
        matrix = m_ref[step]
        for col in range(run):
            own = slice(col * rows, (col + 1) * rows)

            def phase_of(index):
                if by_source:
                    at = index % tgt_count * run + col
                    row = (cs_ref[at : at + 1, :], ss_ref[at : at + 1, :])
                    return halved(jnp.broadcast_to(part, (rows, WIDE)) for part in row)
                at = index // tgt_count
                return halved((ct_ref[at], st_ref[at]))

            def store(index, value):
                o_ref[index, own, :] = value

            butterfly(
                lambda index: source[index, own, :],
                store,
                count,
                apart,
                matrix,
                phase_of,
                8,
            )


def middle_levels(x, matrices, src_tables, tgt_tables, levels):
    rows = tgt_tables[0].shape[1]
    return pl.pallas_call(
        functools.partial(middle_kernel, levels, rows),
        out_shape=jax.ShapeDtypeStruct(x.shape, x.dtype),
        in_specs=[VMEM] * 6,
        out_specs=VMEM,
        compiler_params=PARAMS,
    )(x, matrices, *src_tables, *tgt_tables)


def target_kernel(m_ref, c_ref, s_ref, x_ref, o_hbm, state_ref, o_ref, o_sems):
    cols, rows, _ = x_ref.shape
    levels = m_ref.shape[0]

    for level in range(levels):
        source = x_ref if level == 0 else state_ref
        matrix = m_ref[level]
        for start in range(0, rows, 16):
            own = slice(start, start + 16)
            cosine, sine = halved((c_ref[own, :], s_ref[own, :]))

            def store(index, value):
                state_ref[index, own, :] = value

            butterfly(
                lambda index: source[index, own, :],
                store,
                cols,
                1 << (levels - 1 - level),
                matrix,
                lambda index: (cosine, sine),
                16,
            )

    shuffle = shuffle_matrix()
    copies = []
    half = cols // 2
    for piece in range(rows // 16):
        for side in range(2):
            own = (pl.ds(piece * 16, 16), pl.ds(side * half, half))
            copies.append(
                pltpu.make_async_copy(o_ref.at[own], o_hbm.at[own], o_sems.at[len(copies)])
            )

            def store_block(first, second, block):
                o_ref[block_at(piece, side * half // 16 + second)] = block

            swap_axes(
                lambda first, second: state_ref[block_at(side * half // 16 + first, piece)],
                store_block,
                half // 16,
                1,
                shuffle,
            )
            copies[-1].start()
    for copy in copies:
        copy.wait()


def target_levels(x, matrices, angles):
    cols, rows, _ = x.shape
    shape = (rows, cols, WIDE)
    return pl.pallas_call(
        target_kernel,
        out_shape=jax.ShapeDtypeStruct(shape, x.dtype),
        in_specs=[VMEM] * 4,
        out_specs=FAR,
        scratch_shapes=[
            pltpu.VMEM(x.shape, x.dtype),
            pltpu.VMEM(shape, x.dtype),
            pltpu.SemaphoreType.DMA((rows // 8,)),
        ],
        compiler_params=PARAMS,
    )(matrices, *angles, x)


def gathered(values, axis):
    count = lax.axis_size(axis)
    place = lax.axis_index(axis)
    values = values[None]
    apart = 1
    while apart < count:
        other = lax.ppermute(values, axis, [(i, i ^ apart) for i in range(count)])
        mine_first = (place & apart) == 0
        values = jnp.concatenate(
            [jnp.where(mine_first, values, other), jnp.where(mine_first, other, values)]
        )
        apart *= 2
    return values


def local(box_weights, slowness, dip_field):
    rows, cols, _ = box_weights.shape
    src_count = lax.axis_size("src")
    tgt_count = lax.axis_size("tgt")
    devices = src_count * tgt_count
    row_bits, col_bits = rows.bit_length() - 1, cols.bit_length() - 1
    src_bits, tgt_bits = src_count.bit_length() - 1, tgt_count.bit_length() - 1
    first_target = row_bits + src_bits
    total = first_target + tgt_bits + col_bits
    matrices = [level_matrix(number) for number in range(total)]

    run = cols // devices
    place = lax.axis_index("src") * tgt_count + lax.axis_index("tgt")

    def traded(state):
        return lax.all_to_all(state, ("src", "tgt"), 0, 0, tiled=True)

    state = source_levels(box_weights, jnp.asarray(np.stack(matrices[:row_bits])), slowness)

    state, slowness, dip_field = lax.optimization_barrier((state, slowness, dip_field))
    all_dip = gathered(dip_field, "src")
    all_slowness = gathered(slowness, "tgt")
    run_slowness = lax.dynamic_slice_in_dim(all_slowness, place * run, run, 1)

    state = state.reshape(devices, run * rows, WIDE)
    state = traded(state)
    levels = [(tgt_count << bit, True) for bit in range(src_bits)]
    levels += [(1 << bit, False) for bit in reversed(range(tgt_bits))]
    state = middle_levels(
        state,
        whole_matrices(matrices[row_bits : first_target + tgt_bits]),
        tables(run_slowness.reshape(-1)),
        tables(all_dip),
        levels,
    )
    state = traded(state)

    return target_levels(
        state.reshape(cols, rows, WIDE),
        whole_matrices(matrices[first_target + tgt_bits :]),
        tables(dip_field),
    )


def solution(mesh):
    in_specs = (P("src", "tgt", None), P("tgt"), P("src"))
    out_specs = P("src", "tgt", None)
    return jax.shard_map(local, mesh=mesh, in_specs=in_specs, out_specs=out_specs, check_vma=False)
```
